128 devices in a mesh: dp: 8 (over y, z_hi), tensor: 16 (over x, z_lo, core).
Axes of the slice: x: 4, y: 4, z: 4 (z_hi: 2, z_lo: 2; z = z_hi * 2 + z_lo), core: 2. Of those that a mesh axis runs over, the one named last changes fastest.
Arguments:
- layer_input: bfloat16 [3072, 4096], P(('dp', 'tensor')), may hold values from -6 to 6
- gain_vector: float32 [4096], replicated, may hold values from 0.1 to 1.9
- w_gate: bfloat16 [4096, 14784], P(None, 'tensor'), may hold values from -0.09375 to 0.09375
- w_up: bfloat16 [4096, 14784], P(None, 'tensor'), may hold values from -0.09375 to 0.09375
- w_down: bfloat16 [14784, 4096], P('tensor'), may hold values from -0.046875 to 0.046875
- grad_out: bfloat16 [3072, 4096], P(('dp', 'tensor')), may hold values from -12 to 12
Outputs:
- input_gradient: bfloat16 [3072, 4096], P(('dp', 'tensor'))
- gain_gradient: float32 [4096], replicated
- grad_w_gate: bfloat16 [4096, 14784], P('dp', 'tensor')
- grad_w_up: bfloat16 [4096, 14784], P('dp', 'tensor')
- grad_w_down: bfloat16 [14784, 4096], P('tensor', 'dp')
The draws below stay inside these ranges and needn't reach their ends.
All inputs are finite; a program needn't handle non-finite values.
Results may differ from the reference program's by a relative error of at most 0.024.
Values may be sent and summed in bfloat16 or wider, within the bound.
A program may use at most 192 MiB of HBM per device.

```python
import jax
import jax.numpy as jnp
from jax import lax

D = 4096
FF = 14784
SEQ = 384
TOKENS = 3072
N_DP = 8


def draw_grad_out(key, part):
    key = jax.random.fold_in(key, 7)
    first = jax.random.fold_in(key, 0)
    positions = jnp.arange(TOKENS, dtype=jnp.float32)
    ramp = jnp.exp(jnp.log(3.0) * positions / (TOKENS - 1))
    base = jnp.clip(jax.random.normal(first, (TOKENS, D), jnp.float32), -4.0, 4.0)
    return (base * ramp[:, None]).astype(jnp.bfloat16)


def block_levels(stream_key, extent, cuts, smallest, high):
    def one(dim, blocks):
        draws = jax.random.uniform(jax.random.fold_in(jax.random.fold_in(stream_key, 6), dim), (blocks,), jnp.float32, smallest / len(cuts), high / len(cuts))
        return jnp.repeat(jnp.exp(draws), extent[dim] // blocks).reshape((-1,) + (1,) * (len(extent) - dim - 1))

    level = one(*cuts[0])
    for cut in cuts[1:]:
        level = level * one(*cut)
    return level


def gaussian(rng, extent, width, most, pieces=(), kind=jnp.bfloat16):
    factor_of = block_levels(rng, extent, pieces, -0.22, 0.18) if pieces else 1.0
    entries = jax.random.normal(rng, extent, jnp.float32) * width * factor_of
    return jnp.minimum(jnp.maximum(entries, -most), most).astype(kind)


def setup_inputs(seed: int = 0) -> dict:
    splits = jax.random.split(jax.random.key(seed), 7)
    return {
        "layer_input": gaussian(splits[0], (TOKENS, D), 1.0, 6.0, ((0, 128),)),
        "gain_vector": jnp.clip(1.0 + 0.18 * jax.random.normal(splits[1], (D,), jnp.float32), 0.1, 1.9),
        "w_gate": gaussian(splits[2], (D, FF), D ** -0.5, 0.09375, ((1, 16),)),
        "w_up": gaussian(splits[3], (D, FF), D ** -0.5, 0.09375, ((1, 16),)),
        "w_down": gaussian(splits[4], (FF, D), FF ** -0.5, 0.046875, ((0, 16),)),
        "grad_out": draw_grad_out(jax.random.fold_in(splits[6], 71), 0),
    }


def keep_rounded(value):
    return lax.optimization_barrier(value.astype(jnp.bfloat16)).astype(jnp.float32)

def reference(layer_input, gain_vector, w_gate, w_up, w_down, grad_out):
    gradient_rows = []
    gain_reduced = jnp.zeros((D,), jnp.float32)
    gate_total = jnp.zeros((D, FF), jnp.float32)
    up_total = jnp.zeros((D, FF), jnp.float32)
    down_total = jnp.zeros((FF, D), jnp.float32)
    for group in range(N_DP):
        input_rows = layer_input[group * SEQ:(group + 1) * SEQ].astype(jnp.float32)
        upstream = grad_out[group * SEQ:(group + 1) * SEQ]
        root_mean_square = jnp.sqrt(lax.optimization_barrier(jnp.mean(input_rows * input_rows, axis=1, keepdims=True)) + 1e-06)
        unit_input = input_rows / root_mean_square
        normed_rows = (unit_input * gain_vector).astype(jnp.bfloat16)
        gate = jnp.dot(normed_rows, w_gate, preferred_element_type=jnp.float32)
        up = jnp.dot(normed_rows, w_up, preferred_element_type=jnp.float32)
        sigma = jax.nn.sigmoid(gate)
        silu = gate * sigma
        hidden = (silu * up).astype(jnp.bfloat16)
        d_hidden = lax.dot_general(upstream, w_down, (((1,), (1,)), ((), ())), preferred_element_type=jnp.float32)
        d_gate = (d_hidden * up * sigma * (1.0 + gate * (1.0 - sigma))).astype(jnp.bfloat16)
        d_up = (d_hidden * silu).astype(jnp.bfloat16)
        normalized_gradient = lax.dot_general(d_gate, w_gate, (((1,), (1,)), ((), ())), preferred_element_type=jnp.float32)
        normalized_gradient = normalized_gradient + lax.dot_general(d_up, w_up, (((1,), (1,)), ((), ())), preferred_element_type=jnp.float32)
        scaled_rows = gain_vector * normalized_gradient
        inner_product = lax.optimization_barrier(jnp.mean(scaled_rows * unit_input, axis=1, keepdims=True))
        gradient_rows.append(((scaled_rows - unit_input * inner_product) / root_mean_square).astype(jnp.bfloat16))
        gain_reduced = gain_reduced + lax.optimization_barrier(jnp.sum(normalized_gradient * unit_input, axis=0))
        gate_total = gate_total + keep_rounded(lax.dot_general(normed_rows, d_gate, (((0,), (0,)), ((), ())), preferred_element_type=jnp.float32))
        up_total = up_total + keep_rounded(lax.dot_general(normed_rows, d_up, (((0,), (0,)), ((), ())), preferred_element_type=jnp.float32))
        down_total = down_total + keep_rounded(lax.dot_general(hidden, upstream, (((0,), (0,)), ((), ())), preferred_element_type=jnp.float32))
    input_gradient = jnp.concatenate(gradient_rows, axis=0)
    return (input_gradient, gain_reduced, gate_total.astype(jnp.bfloat16), up_total.astype(jnp.bfloat16), down_total.astype(jnp.bfloat16))
```

```python
import functools

import jax
import jax.numpy as jnp
from jax import lax
from jax.experimental import pallas as pl
from jax.experimental.pallas import tpu as pltpu
from jax.sharding import PartitionSpec as P

MESH = pl.DeviceIdType.MESH
BF = jnp.bfloat16
F32 = jnp.float32
D = 4096
HALF = 2048
QUART = 1024
ROWS = 48
PLANE = 768
GROUP = 384
BLK = 512
CORE_FF = 924
MAIN = 896
REM = CORE_FF - MAIN
NW = 2 * MAIN + 128
HW = 928
XW = NW + MAIN


def coords():
    dp = lax.axis_index("dp")
    t = lax.axis_index("tensor")
    y = dp // 2
    z = (dp % 2) * 2 + (t // 2) % 2
    return t // 4, y, z, t % 2


def device(x, y, z, c):
    x, y, z, c = (x + 4) % 4, (y + 4) % 4, (z + 4) % 4, (c + 2) % 2
    return (y * 2 + z // 2, x * 4 + (z % 2) * 2 + c)


def remote(src, dst, ss, rs, to):
    return pltpu.make_async_remote_copy(
        src_ref=src, dst_ref=dst, send_sem=ss, recv_sem=rs, device_id=to, device_id_type=MESH
    )


def greet(peers):
    barrier = pltpu.get_barrier_semaphore()
    for to in peers:
        pl.semaphore_signal(barrier, inc=1, device_id=to, device_id_type=MESH)
    pl.semaphore_wait(barrier, len(peers))


OFFS = (0, -1, 1, 2)


def slot(i, j):
    return (i % 4) * 4 + (j % 4)


def gather_kernel(
    li_ref, go_ref, gain_ref, n_ref, g_ref, other, ex_s, ex_r, s_sem, r_sem, c_s, c_r
):
    x, y, z, c = coords()
    core = device(x, y, z, 1 - c)
    step = {
        "x": (device(x + 1, y, z, c), device(x - 1, y, z, c)),
        "z": (device(x, y, z + 1, c), device(x, y, z - 1, c)),
    }
    greet([core, *step["x"], *step["z"]])
    swaps = []
    for a, ref in enumerate((li_ref, go_ref)):
        cp = remote(ref, other.at[a], ex_s.at[a], ex_r.at[a], core)
        cp.start()
        swaps.append(cp)

    base = pl.multiple_of((z * 4 + x) * ROWS, 16)
    first = c == 0
    outs = (n_ref, g_ref)

    swaps[0].wait_recv()
    scale = []
    for ref in (li_ref, other.at[0]):
        rows = ref[...].astype(F32)
        scale.append(jnp.sqrt(jnp.mean(rows * rows, axis=1, keepdims=True) + 1e-06))
    swaps[1].wait_recv()
    for k in range(8):
        cols = pl.ds(k * 512, 512)
        mine = (li_ref[:, cols].astype(F32) / scale[0]) * gain_ref[:, cols]
        theirs = (other[0, :, cols].astype(F32) / scale[1]) * gain_ref[:, cols]
        both = jnp.concatenate(
            [jnp.where(first, mine, theirs), jnp.where(first, theirs, mine)], axis=0
        )
        n_ref[pl.ds(base, ROWS), cols] = both.astype(BF)
        mine = go_ref[:, cols].astype(F32)
        theirs = other[1, :, cols].astype(F32)
        both = jnp.concatenate(
            [jnp.where(first, mine, theirs), jnp.where(first, theirs, mine)], axis=0
        )
        g_ref[pl.ds(base, ROWS), cols] = both.astype(BF)

    lo = pl.multiple_of(c * HALF, 128)
    wide = (pl.ds(lo, HALF), pl.ds(lo, QUART), pl.ds(pl.multiple_of(lo + QUART, 128), QUART))

    def block(a, i, j, part=0):
        if a == 0:
            zz, xx = (z + j + 4) % 4, (x + i + 4) % 4
        else:
            zz, xx = (z + i + 4) % 4, (x + j + 4) % 4
        return outs[a].at[pl.ds(pl.multiple_of((zz * 4 + xx) * ROWS, 16), ROWS), wide[part]]

    sent = []
    count = [0, 0]

    def push(a, leg, way, i, j, part=0):
        axis = ("x", "z")[(a + leg) % 2]
        to = step[axis][0 if way > 0 else 1]
        ri, rj = (i - way, j) if leg == 0 else (i, j - way)
        ref = block(a, i, j, part)
        k = 1 if part == 2 else 0
        cp = remote(ref, ref, s_sem.at[a, count[a]], r_sem.at[a, slot(ri, rj), k], to)
        count[a] += 1
        cp.start()
        sent.append(cp)

    def arrived(a, i, j):
        if i == 2 and j == 0 or j == 2:
            parts = (1, 2)
        else:
            parts = (0,)
        for part in parts:
            ref = block(a, i, j, part)
            k = 1 if part == 2 else 0
            remote(ref, ref, s_sem.at[a, 0], r_sem.at[a, slot(i, j), k], core).wait_recv()

    def share(a, i, j):
        ref = block(a, i, j)
        k = slot(i, j)
        cp = remote(ref, ref, c_s.at[a, k], c_r.at[a, k], core)
        cp.start()
        sent.append(cp)

    for a in (0, 1):
        for way in (1, -1):
            push(a, 0, way, 0, 0)
    for a in (0, 1):
        for way in (1, -1):
            push(a, 1, way, 0, 0)
    for a in (0, 1):
        for way in (1, -1):
            arrived(a, -way, 0)
            push(a, 0, way, -way, 0, 1 if way > 0 else 2)
            push(a, 1, 1, -way, 0)
            push(a, 1, -1, -way, 0)
            share(a, -way, 0)
    for i in OFFS:
        for a in (0, 1):
            if i == 2:
                arrived(a, 2, 0)
                push(a, 1, 1, 2, 0)
                push(a, 1, -1, 2, 0)
                share(a, 2, 0)
        for a in (0, 1):
            for way in (1, -1):
                arrived(a, i, -way)
                push(a, 1, way, i, -way, 1 if way > 0 else 2)
                share(a, i, -way)
    for i in OFFS:
        for a in (0, 1):
            arrived(a, i, 2)
            share(a, i, 2)

    theirs = pl.ds(pl.multiple_of((1 - c) * HALF, 128), HALF)
    for a in (0, 1):
        for i in OFFS:
            for j in OFFS:
                if (i, j) != (0, 0):
                    if a == 0:
                        zz, xx = (z + j + 4) % 4, (x + i + 4) % 4
                    else:
                        zz, xx = (z + i + 4) % 4, (x + j + 4) % 4
                    ref = outs[a].at[
                        pl.ds(pl.multiple_of((zz * 4 + xx) * ROWS, 16), ROWS), theirs
                    ]
                    k = slot(i, j)
                    remote(ref, ref, c_s.at[a, k], c_r.at[a, k], core).wait_recv()
    for cp in swaps + sent:
        cp.wait_send()


def gather(layer_input, grad_out, gain):
    vmem = pl.BlockSpec(memory_space=pltpu.VMEM)
    dma = pltpu.SemaphoreType.DMA
    return pl.pallas_call(
        gather_kernel,
        out_shape=[jax.ShapeDtypeStruct((PLANE, D), BF)] * 2,
        in_specs=[vmem] * 3,
        out_specs=[vmem] * 2,
        scratch_shapes=[
            pltpu.VMEM((2, 24, D), BF),
            dma((2,)),
            dma((2,)),
            dma((2, 20)),
            dma((2, 16, 2)),
            dma((2, 16)),
            dma((2, 16)),
        ],
        compiler_params=pltpu.CompilerParams(
            collective_id=0, has_side_effects=True, vmem_limit_bytes=48 << 20
        ),
    )(layer_input, grad_out, gain)


PART_A = (("n", 0, 512), ("n", 512, 512), ("h", 0, 400))
PART_B = (("n", 1024, 512), ("n", 1536, 384), ("h", 400, 528))
NC = len(PART_A)


def reduce_kernel(
    n_hbm, g_hbm, x_ref, p_ref, li_ref, gain_ref,
    tn_out, th_out, ig_out, gain_out,
    nb, gb, nt, ht, far_n, far_h, mid_n, mid_h, to_n, to_h, in_n, in_h, own_n, own_h,
    pc, q, xo, xi, xs, xr, zs, zr, dn, gs, gr,
    load, far_s, far_r, near_s, near_r, p_s, p_r, g_sem, g_rec,
):
    x, y, z, c = coords()
    zl, zh = z % 2, z // 2
    core = device(x, y, z, 1 - c)
    xs_dev = [device(x + k, y, z, c) for k in (1, -1, 2)]
    ys_dev = [device(x, y + k, z, c) for k in (1, -1, 2)]
    zs_dev = [device(x, y, z + k, c) for k in (1, -1, 2)]
    zpair = device(x, y, zh * 2 + 1 - zl, c)

    loads = {}
    for r in (2, 1, -1, 0):
        k = r % 4
        cols = pl.ds(pl.multiple_of((((y + r + 4) % 4) * 2 + zh) * BLK, 128), BLK)
        loads[r] = [
            pltpu.make_async_copy(n_hbm.at[:, cols], nb.at[k], load.at[0, k]),
            pltpu.make_async_copy(g_hbm.at[:, cols], gb.at[k], load.at[1, k]),
        ]
        for cp in loads[r]:
            cp.start()
    greet([core, *xs_dev, *ys_dev, *zs_dev])
    sent = []

    def send(src, dst, ss, rs, to):
        cp = remote(src, dst, ss, rs, to)
        cp.start()
        sent.append(cp)
        return cp

    mine = pl.ds(pl.multiple_of(c * HALF, 128), HALF)
    theirs = pl.ds(pl.multiple_of((1 - c) * HALF, 128), HALF)
    swap = send(p_ref.at[:, theirs], pc, p_s.at[0], p_r.at[0], core)

    ht[0:MAIN, :] = x_ref[:, NW:XW].T
    ht[MAIN:, :] = x_ref[:, NW - 128:NW].T

    def ready(r):
        for cp in loads[r]:
            cp.wait()
        nt[r % 4] = nb[r % 4].T

    def term(r, chunk):
        kind, s, w = chunk
        if kind == "n":
            return jnp.dot(nt[r % 4], x_ref[:, s:s + w], preferred_element_type=F32)
        return jnp.dot(ht[s:s + w, :], gb[r % 4], preferred_element_type=F32)

    def view(n, h, chunk):
        kind, s, w = chunk
        return n.at[:, pl.ds(s, w)] if kind == "n" else h.at[pl.ds(s, w), :]

    ready(2)
    for k in range(NC):
        for part, chunk in enumerate((PART_A[k], PART_B[k])):
            ref = view(far_n, far_h, chunk)
            ref[...] = term(2, chunk).astype(BF)
            send(
                ref, view(mid_n, mid_h, chunk), far_s.at[part, k], far_r.at[part, k],
                ys_dev[part],
            )

    def near(part, chunk, k, which, extra):
        r = 1 if part == 0 else -1
        value = term(r, chunk)
        if extra:
            value = value + view(mid_n, mid_h, chunk)[...].astype(F32)
        ref = view(to_n.at[part], to_h.at[part], chunk)
        ref[...] = value.astype(BF)
        send(
            ref, view(in_n.at[part], in_h.at[part], chunk),
            near_s.at[part, which, k], near_r.at[part, which, k], ys_dev[part],
        )

    ready(1)
    ready(-1)
    for k in range(NC):
        near(0, PART_B[k], k, 1, False)
        near(1, PART_A[k], k, 0, False)
    ready(0)
    for k in range(NC):
        for chunk in (PART_A[k], PART_B[k]):
            view(own_n, own_h, chunk)[...] = term(0, chunk)

    swap.wait_recv()
    q[...] = p_ref[:, mine].astype(F32) + pc[...].astype(F32)

    def rows_of(zz, xx):
        return pl.ds(pl.multiple_of((zz * 4 + (xx + 4) % 4) * ROWS, 16), ROWS)

    for zz in (0, 1):
        xo[zz * ROWS:(zz + 1) * ROWS, :] = q[rows_of(zz, x + 2), :].astype(BF)
    far = [
        send(
            xo.at[:, pl.ds(k * QUART, QUART)], xi.at[:, pl.ds(k * QUART, QUART)],
            p_s.at[1 + k], p_r.at[1 + k], xs_dev[k],
        )
        for k in (0, 1)
    ]
    step = []
    for k in (0, 1):
        far[k].wait_recv()
        for zz in (0, 1):
            rows = pl.ds(zz * ROWS, ROWS)
            src = rows_of(zz, x + (1 if k == 0 else -1))
            for half in (0, 1):
                cols = pl.ds(half * QUART, QUART)
                value = q[src, cols]
                if half == k:
                    value = value + xi[rows, cols].astype(F32)
                xs[k, rows, cols] = value.astype(BF)
        step.append(send(xs.at[k], xr.at[k], p_s.at[3 + k], p_r.at[3 + k], xs_dev[k]))
    for k in (0, 1):
        step[k].wait_recv()

    def summed(zz):
        rows = pl.ds(pl.multiple_of(zz * ROWS, 16), ROWS)
        return q[rows_of(zz, x), :] + xr[0, rows, :].astype(F32) + xr[1, rows, :].astype(F32)

    zs[...] = summed(1 - zl).astype(BF)
    hop = send(zs, zr, p_s.at[5], p_r.at[5], zpair)
    hop.wait_recv()
    q[0:ROWS, :] = summed(zl) + zr[...].astype(F32)
    dn[:, mine] = q[pl.ds(pl.multiple_of(c * 24, 8), 24), :]
    last = send(
        q.at[pl.ds(pl.multiple_of((1 - c) * 24, 8), 24), :], dn.at[:, mine],
        p_s.at[6], p_r.at[6], core,
    )
    last.wait_recv()

    inputs = li_ref[...].astype(F32)
    rms = jnp.sqrt(jnp.mean(inputs * inputs, axis=1, keepdims=True) + 1e-06)
    unit = inputs / rms
    scaled = gain_ref[...] * dn[...]
    inner = jnp.mean(scaled * unit, axis=1, keepdims=True)
    ig_out[...] = ((scaled - unit * inner) / rms).astype(BF)
    total = jnp.sum(dn[...] * unit, axis=0, keepdims=True)
    for s, peers in enumerate(([core], xs_dev, zs_dev, ys_dev)):
        gs[s] = total
        cps = []
        for k, to in enumerate(peers):
            cps.append(send(gs.at[s], gr.at[s, k], g_sem.at[s, k], g_rec.at[s, k], to))
        for k, cp in enumerate(cps):
            cp.wait_recv()
            total = total + gr[s, k]
    gain_out[...] = total

    for k in range(NC):
        for part, chunk in enumerate((PART_A[k], PART_B[k])):
            ref = view(mid_n, mid_h, chunk)
            remote(ref, ref, far_s.at[part, k], far_r.at[part, k], core).wait_recv()
            near(part, chunk, k, part, True)

    for which, parts in ((0, PART_A), (1, PART_B)):
        for k in range(NC):
            chunk = parts[k]
            value = view(own_n, own_h, chunk)[...]
            for part in (0, 1):
                ref = view(in_n.at[part], in_h.at[part], chunk)
                remote(
                    ref, ref, near_s.at[part, which, k], near_r.at[part, which, k], core
                ).wait_recv()
                value = value + ref[...].astype(F32)
            view(tn_out, th_out, chunk)[...] = value.astype(BF)
    for cp in sent:
        cp.wait_send()


def reduce(n, g, xp, p, layer_input, gain):
    vmem = pl.BlockSpec(memory_space=pltpu.VMEM)
    hbm = pl.BlockSpec(memory_space=pl.ANY)
    dma = pltpu.SemaphoreType.DMA
    v = pltpu.VMEM
    return pl.pallas_call(
        reduce_kernel,
        out_shape=[
            jax.ShapeDtypeStruct((BLK, NW), BF),
            jax.ShapeDtypeStruct((HW, BLK), BF),
            jax.ShapeDtypeStruct((24, D), BF),
            jax.ShapeDtypeStruct((1, D), F32),
        ],
        in_specs=[hbm, hbm, vmem, vmem, vmem, vmem],
        out_specs=[vmem] * 4,
        scratch_shapes=[
            v((4, PLANE, BLK), BF),
            v((4, PLANE, BLK), BF),
            v((4, BLK, PLANE), BF),
            v((MAIN + 128, PLANE), BF),
            v((BLK, NW), BF),
            v((HW, BLK), BF),
            v((BLK, NW), BF),
            v((HW, BLK), BF),
            v((2, BLK, NW), BF),
            v((2, HW, BLK), BF),
            v((2, BLK, NW), BF),
            v((2, HW, BLK), BF),
            v((BLK, NW), F32),
            v((HW, BLK), F32),
            v((GROUP, HALF), BF),
            v((GROUP, HALF), F32),
            v((2 * ROWS, HALF), BF),
            v((2 * ROWS, HALF), BF),
            v((2, 2 * ROWS, HALF), BF),
            v((2, 2 * ROWS, HALF), BF),
            v((ROWS, HALF), BF),
            v((ROWS, HALF), BF),
            v((24, D), F32),
            v((4, 1, D), F32),
            v((4, 3, 1, D), F32),
            dma((2, 4)),
            dma((2, NC)),
            dma((2, NC)),
            dma((2, 2, NC)),
            dma((2, 2, NC)),
            dma((7,)),
            dma((7,)),
            dma((4, 3)),
            dma((4, 3)),
        ],
        compiler_params=pltpu.CompilerParams(
            collective_id=1, has_side_effects=True, vmem_limit_bytes=60 << 20
        ),
    )(n, g, xp, p, layer_input, gain)


def contract_cols(left, right):
    return lax.dot_general(left, right, (((1,), (1,)), ((), ())), preferred_element_type=F32)


def body(layer_input, gain_vector, w_gate, w_up, w_down, grad_out):
    gain = gain_vector[None, :]
    normed, upstream = gather(layer_input, grad_out, gain)
    gate = jnp.dot(normed, w_gate, preferred_element_type=F32)
    up = jnp.dot(normed, w_up, preferred_element_type=F32)
    sigma = jax.nn.sigmoid(gate)
    silu = gate * sigma
    hidden = (silu * up).astype(BF)
    d_hidden = contract_cols(upstream, w_down)
    d_gate = (d_hidden * up * sigma * (1.0 + gate * (1.0 - sigma))).astype(BF)
    d_up = (d_hidden * silu).astype(BF)
    start = (lax.axis_index("dp") % 2) * GROUP
    own_gate = lax.dynamic_slice_in_dim(d_gate, start, GROUP, 0)
    own_up = lax.dynamic_slice_in_dim(d_up, start, GROUP, 0)
    share = (contract_cols(own_gate, w_gate) + contract_cols(own_up, w_up)).astype(BF)
    packed = jnp.concatenate(
        [
            d_gate[:, :MAIN],
            d_up[:, :MAIN],
            hidden[:, MAIN:],
            d_gate[:, MAIN:],
            d_up[:, MAIN:],
            jnp.zeros((PLANE, 128 - 3 * REM), BF),
            hidden[:, :MAIN],
        ],
        axis=1,
    )
    tn, th, input_gradient, gain_gradient = reduce(
        normed, upstream, packed, share, layer_input, gain
    )
    rest = 2 * MAIN + REM
    return (
        input_gradient,
        gain_gradient[0],
        jnp.concatenate([tn[:, :MAIN], tn[:, rest:rest + REM]], axis=1),
        jnp.concatenate([tn[:, MAIN:2 * MAIN], tn[:, rest + REM:rest + 2 * REM]], axis=1),
        th[:CORE_FF],
    )


def solution(mesh):
    return jax.shard_map(
        body,
        mesh=mesh,
        in_specs=(
            P(("dp", "tensor"), None),
            P(),
            P(None, "tensor"),
            P(None, "tensor"),
            P("tensor", None),
            P(("dp", "tensor"), None),
        ),
        out_specs=(
            P(("dp", "tensor"), None),
            P(),
            P("dp", "tensor"),
            P("dp", "tensor"),
            P("tensor", "dp"),
        ),
        check_vma=False,
    )
```

```python
import functools

import jax
import jax.numpy as jnp
from jax import lax
from jax.experimental import pallas as pl
from jax.experimental.pallas import tpu as pltpu
from jax.sharding import PartitionSpec as P

MESH = pl.DeviceIdType.MESH
BF = jnp.bfloat16
F32 = jnp.float32
D = 4096
HALF = 2048
QUART = 1024
ROWS = 48
PLANE = 768
GROUP = 384
BLK = 512
CORE_FF = 924
MAIN = 896
REM = CORE_FF - MAIN
XW = 3 * MAIN + 128
TR = 3 * MAIN + 96


def coords():
    dp = lax.axis_index("dp")
    t = lax.axis_index("tensor")
    y = dp // 2
    z = (dp % 2) * 2 + (t // 2) % 2
    return t // 4, y, z, t % 2


def device(x, y, z, c):
    x, y, z, c = (x + 4) % 4, (y + 4) % 4, (z + 4) % 4, (c + 2) % 2
    return (y * 2 + z // 2, x * 4 + (z % 2) * 2 + c)


def remote(src, dst, ss, rs, to):
    return pltpu.make_async_remote_copy(
        src_ref=src, dst_ref=dst, send_sem=ss, recv_sem=rs, device_id=to, device_id_type=MESH
    )


def greet(peers):
    barrier = pltpu.get_barrier_semaphore()
    for to in peers:
        pl.semaphore_signal(barrier, inc=1, device_id=to, device_id_type=MESH)
    pl.semaphore_wait(barrier, len(peers))


OFFS = (0, -1, 1, 2)
PIECES = ((0, 256), (256, 256), (512, 256), (768, 156))


def slot(i, j):
    return (i % 4) * 4 + (j % 4)


def contract_cols(left, right):
    return lax.dot_general(left, right, (((1,), (1,)), ((), ())), preferred_element_type=F32)


def gather_kernel(
    li_ref, go_ref, gain_ref, wg_hbm, wu_hbm, wd_hbm, n_hbm, g_hbm, x_hbm, p_hbm,
    n_ref, g_ref, x_ref, dg_ref, du_ref, p_ref, wg, wu, wd, other,
    w_sem, out_sem, ex_s, ex_r, s_sem, r_sem, c_s, c_r,
):
    x, y, z, c = coords()
    s = 1 - 2 * (z % 2)
    core = device(x, y, z, 1 - c)
    step = {
        "x": (device(x + 1, y, z, c), device(x - 1, y, z, c)),
        "z": (device(x, y, z + s, c), device(x, y, z - s, c)),
    }
    weights = [
        pltpu.make_async_copy(src, dst, w_sem.at[k])
        for k, (src, dst) in enumerate(((wg_hbm, wg), (wu_hbm, wu), (wd_hbm, wd)))
    ]
    greet([core, *step["x"], *step["z"]])
    swaps = []
    for a, ref in enumerate((li_ref, go_ref)):
        cp = remote(ref, other.at[a], ex_s.at[a], ex_r.at[a], core)
        cp.start()
        swaps.append(cp)
    for cp in weights:
        cp.start()

    base = pl.multiple_of((z * 4 + x) * ROWS, 16)
    first = c == 0
    outs = (n_ref, g_ref)

    swaps[0].wait_recv()
    scale = []
    for ref in (li_ref, other.at[0]):
        rows = ref[...].astype(F32)
        scale.append(jnp.sqrt(jnp.mean(rows * rows, axis=1, keepdims=True) + 1e-06))
    swaps[1].wait_recv()
    for k in range(8):
        cols = pl.ds(k * 512, 512)
        mine = (li_ref[:, cols].astype(F32) / scale[0]) * gain_ref[:, cols]
        theirs = (other[0, :, cols].astype(F32) / scale[1]) * gain_ref[:, cols]
        both = jnp.concatenate(
            [jnp.where(first, mine, theirs), jnp.where(first, theirs, mine)], axis=0
        )
        n_ref[pl.ds(base, ROWS), cols] = both.astype(BF)
        mine = go_ref[:, cols].astype(F32)
        theirs = other[1, :, cols].astype(F32)
        both = jnp.concatenate(
            [jnp.where(first, mine, theirs), jnp.where(first, theirs, mine)], axis=0
        )
        g_ref[pl.ds(base, ROWS), cols] = both.astype(BF)

    lo = pl.multiple_of(c * HALF, 128)
    wide = (pl.ds(lo, HALF), pl.ds(lo, QUART), pl.ds(pl.multiple_of(lo + QUART, 128), QUART))
    theirs = pl.ds(pl.multiple_of((1 - c) * HALF, 128), HALF)

    def place(a, i, j):
        dz, dx = (j, i) if a == 0 else (i, j)
        zz, xx = (z + s * dz + 4) % 4, (x + dx + 4) % 4
        return pl.ds(pl.multiple_of((zz * 4 + xx) * ROWS, 16), ROWS)

    def block(a, i, j, part=0):
        return outs[a].at[place(a, i, j), wide[part]]

    sent = []
    count = [0, 0]

    def push(a, leg, way, i, j, part=0):
        axis = ("x", "z")[(a + leg) % 2]
        to = step[axis][0 if way > 0 else 1]
        at = (i, j)[leg]
        at = at - way if axis == "x" else way - at
        ri, rj = (at, j) if leg == 0 else (i, at)
        ref = block(a, i, j, part)
        k = 1 if part == 2 else 0
        cp = remote(ref, ref, s_sem.at[a, count[a]], r_sem.at[a, slot(ri, rj), k], to)
        count[a] += 1
        cp.start()
        sent.append(cp)

    def arrive(a, i, j):
        for part in (1, 2) if (i, j) == (2, 0) or j == 2 else (0,):
            ref = block(a, i, j, part)
            k = 1 if part == 2 else 0
            remote(ref, ref, s_sem.at[a, 0], r_sem.at[a, slot(i, j), k], core).wait_recv()
        if j == 0:
            if i in (1, -1):
                push(a, 0, -i, i, 0, 1 if i < 0 else 2)
            push(a, 1, 1, i, 0)
            push(a, 1, -1, i, 0)
        elif j in (1, -1):
            push(a, 1, -j, i, j, 1 if j < 0 else 2)
        ref = block(a, i, j)
        k = slot(i, j)
        cp = remote(ref, ref, c_s.at[a, k], c_r.at[a, k], core)
        cp.start()
        sent.append(cp)

    for a in (0, 1):
        for way in (1, -1):
            push(a, 0, way, 0, 0)
            push(a, 1, way, 0, 0)

    stored = []
    tally = [0]

    def store(src, dst):
        cp = pltpu.make_async_copy(src, dst, out_sem.at[tally[0]])
        tally[0] += 1
        cp.start()
        stored.append(cp)

    def chunk_rows(k):
        return pl.ds(pl.multiple_of(((z // 2 + k) % 2) * GROUP, 16), GROUP)

    def chunk_ready(k):
        for dz in ((0, 1), (-1, 2))[k]:
            for a in (0, 1):
                for dx in OFFS:
                    i, j = (dx, dz) if a == 0 else (dz, dx)
                    if (i, j) != (0, 0):
                        ref = outs[a].at[place(a, i, j), theirs]
                        at = slot(i, j)
                        remote(ref, ref, c_s.at[a, at], c_r.at[a, at], core).wait_recv()
        rows = chunk_rows(k)
        store(n_ref.at[rows, :], n_hbm.at[rows, :])
        store(g_ref.at[rows, :], g_hbm.at[rows, :])

    def piece(k, f, w):
        rows = chunk_rows(k)
        normed = n_ref[rows, :]
        gate = contract_cols(normed, wg[f:f + w, :])
        up = contract_cols(normed, wu[f:f + w, :])
        d_hidden = contract_cols(g_ref[rows, :], wd[f:f + w, :])
        sigma = jax.nn.sigmoid(gate)
        silu = gate * sigma
        hidden = (silu * up).astype(BF)
        d_gate = (d_hidden * up * sigma * (1.0 + gate * (1.0 - sigma))).astype(BF)
        d_up = (d_hidden * silu).astype(BF)
        if k == 0:
            dg_ref[:, f:f + w] = d_gate
            du_ref[:, f:f + w] = d_up
        m = min(w, MAIN - f)
        for q, value in enumerate((d_gate, d_up, hidden)):
            x_ref[rows, q * MAIN + f:q * MAIN + f + m] = value[:, :m]
        if m < w:
            gap = jnp.zeros((GROUP, 32 - REM), BF)
            x_ref[rows, 3 * MAIN:] = jnp.concatenate(
                [d_gate[:, m:], gap, d_up[:, m:], gap, hidden[:, m:], gap,
                 jnp.zeros((GROUP, 32), BF)],
                axis=1,
            )
            store(x_ref.at[rows, :], x_hbm.at[rows, :])

    def moves(*items):
        for item in items:
            arrive(*item)

    moves((0, -1, 0), (1, 0, -1), (0, 1, 0), (1, 0, 1))
    moves((1, 1, 0), (0, 0, 1), (0, 2, 0), (1, 0, 2))
    moves((1, -1, 0), (0, 0, -1))
    moves((0, -1, 1), (1, 1, -1), (0, 1, 1), (1, 1, 1))
    moves((0, -1, -1), (1, -1, -1), (0, 1, -1), (1, -1, 1))
    moves((0, 2, 1), (1, 1, 2))
    for cp in weights:
        cp.wait()
    chunk_ready(0)
    piece(0, *PIECES[0])
    moves((1, 2, 0), (0, 0, 2), (1, -1, 2), (0, 2, -1))
    piece(0, *PIECES[1])
    moves((0, -1, 2), (0, 1, 2), (1, 2, -1), (1, 2, 1))
    piece(0, *PIECES[2])
    moves((0, 2, 2), (1, 2, 2))
    piece(0, *PIECES[3])
    chunk_ready(1)
    for f, w in PIECES:
        piece(1, f, w)

    for k in range(8):
        cols = slice(k * 512, (k + 1) * 512)
        value = jnp.dot(dg_ref[...], wg[:, cols], preferred_element_type=F32)
        value = value + jnp.dot(du_ref[...], wu[:, cols], preferred_element_type=F32)
        p_ref[:, cols] = value.astype(BF)
    store(p_ref, p_hbm)
    for cp in swaps + sent:
        cp.wait_send()
    for cp in stored:
        cp.wait()


def gather(layer_input, grad_out, gain, w_gate, w_up, w_down):
    vmem = pl.BlockSpec(memory_space=pltpu.VMEM)
    hbm = pl.BlockSpec(memory_space=pl.ANY)
    dma = pltpu.SemaphoreType.DMA
    v = pltpu.VMEM
    return pl.pallas_call(
        gather_kernel,
        out_shape=[
            jax.ShapeDtypeStruct((PLANE, D), BF),
            jax.ShapeDtypeStruct((PLANE, D), BF),
            jax.ShapeDtypeStruct((PLANE, XW), BF),
            jax.ShapeDtypeStruct((GROUP, D), BF),
        ],
        in_specs=[vmem] * 3 + [hbm] * 3,
        out_specs=[hbm] * 4,
        scratch_shapes=[
            v((PLANE, D), BF),
            v((PLANE, D), BF),
            v((PLANE, XW), BF),
            v((GROUP, CORE_FF), BF),
            v((GROUP, CORE_FF), BF),
            v((GROUP, D), BF),
            v((CORE_FF, D), BF),
            v((CORE_FF, D), BF),
            v((CORE_FF, D), BF),
            v((2, 24, D), BF),
            dma((3,)),
            dma((7,)),
            dma((2,)),
            dma((2,)),
            dma((2, 20)),
            dma((2, 16, 2)),
            dma((2, 16)),
            dma((2, 16)),
        ],
        compiler_params=pltpu.CompilerParams(
            collective_id=0, has_side_effects=True, vmem_limit_bytes=60 << 20
        ),
    )(layer_input, grad_out, gain, w_gate, w_up, w_down)


PART_A = ((0, 512), (512, 512), (1792, 384))
PART_B = ((1024, 384), (1408, 384), (2176, 608))
NC = len(PART_A)


def reduce_kernel(
    n_hbm, g_hbm, x_ref, p_ref, li_ref, gain_ref,
    t_out, ig_out, gain_out,
    nb, gb, xt, far, mid, outgo, into, own,
    pc, q, xo, xi, xs, xr, zs, zr, dn, gs, gr,
    load, far_s, far_r, near_s, near_r, p_s, p_r, g_sem, g_rec,
):
    x, y, z, c = coords()
    zl, zh = z % 2, z // 2
    core = device(x, y, z, 1 - c)
    xs_dev = [device(x + k, y, z, c) for k in (1, -1, 2)]
    ys_dev = [device(x, y + k, z, c) for k in (1, -1, 2)]
    zs_dev = [device(x, y, z + k, c) for k in (1, -1, 2)]
    zpair = device(x, y, zh * 2 + 1 - zl, c)

    loads = {}
    for r in (2, 1, -1, 0):
        k = r % 4
        cols = pl.ds(pl.multiple_of((((y + r + 4) % 4) * 2 + zh) * BLK, 128), BLK)
        loads[r] = [
            pltpu.make_async_copy(n_hbm.at[:, cols], nb.at[k], load.at[0, k]),
            pltpu.make_async_copy(g_hbm.at[:, cols], gb.at[k], load.at[1, k]),
        ]
        for cp in loads[r]:
            cp.start()
    greet([core, *xs_dev, *ys_dev, *zs_dev])
    sent = []

    def send(src, dst, ss, rs, to):
        cp = remote(src, dst, ss, rs, to)
        cp.start()
        sent.append(cp)
        return cp

    mine = pl.ds(pl.multiple_of(c * HALF, 128), HALF)
    theirs = pl.ds(pl.multiple_of((1 - c) * HALF, 128), HALF)
    swap = send(p_ref.at[:, theirs], pc, p_s.at[0], p_r.at[0], core)

    xt[...] = x_ref[...].T

    def ready(r):
        for cp in loads[r]:
            cp.wait()

    def fill(ref, r, chunk, add=None):
        k = r % 4
        start, size = chunk
        stop = start + size
        marks = [m for m in (start, 2 * MAIN, 3 * MAIN, 3 * MAIN + 64, stop) if start <= m <= stop]
        for p, e in zip(marks, marks[1:]):
            if p == e:
                continue
            tokens = gb if 2 * MAIN <= p < 3 * MAIN or p >= 3 * MAIN + 64 else nb
            value = jnp.dot(xt[p:e, :], tokens[k], preferred_element_type=F32)
            if add is not None:
                value = value + add[p:e, :].astype(F32)
            ref[p:e, :] = value.astype(ref.dtype)

    def view(ref, chunk):
        return ref.at[pl.ds(*chunk), :]

    ready(2)
    for k in range(NC):
        for part, chunk in enumerate((PART_A[k], PART_B[k])):
            fill(far, 2, chunk)
            send(
                view(far, chunk), view(mid, chunk), far_s.at[part, k], far_r.at[part, k],
                ys_dev[part],
            )

    def near(part, chunk, k, which, extra):
        fill(outgo.at[part], 1 if part == 0 else -1, chunk, mid if extra else None)
        send(
            view(outgo.at[part], chunk), view(into.at[part], chunk),
            near_s.at[part, which, k], near_r.at[part, which, k], ys_dev[part],
        )

    ready(1)
    ready(-1)
    for k in range(NC):
        near(0, PART_B[k], k, 1, False)
        near(1, PART_A[k], k, 0, False)
    ready(0)
    for k in range(NC):
        for chunk in (PART_A[k], PART_B[k]):
            fill(own, 0, chunk)

    swap.wait_recv()
    q[...] = p_ref[:, mine].astype(F32) + pc[...].astype(F32)

    def rows_of(zz, xx):
        return pl.ds(pl.multiple_of((zz * 4 + (xx + 4) % 4) * ROWS, 16), ROWS)

    for zz in (0, 1):
        xo[zz * ROWS:(zz + 1) * ROWS, :] = q[rows_of(zz, x + 2), :].astype(BF)
    far = [
        send(
            xo.at[:, pl.ds(k * QUART, QUART)], xi.at[:, pl.ds(k * QUART, QUART)],
            p_s.at[1 + k], p_r.at[1 + k], xs_dev[k],
        )
        for k in (0, 1)
    ]
    step = []
    for k in (0, 1):
        far[k].wait_recv()
        for zz in (0, 1):
            rows = pl.ds(zz * ROWS, ROWS)
            src = rows_of(zz, x + (1 if k == 0 else -1))
            for half in (0, 1):
                cols = pl.ds(half * QUART, QUART)
                value = q[src, cols]
                if half == k:
                    value = value + xi[rows, cols].astype(F32)
                xs[k, rows, cols] = value.astype(BF)
        step.append(send(xs.at[k], xr.at[k], p_s.at[3 + k], p_r.at[3 + k], xs_dev[k]))
    for k in (0, 1):
        step[k].wait_recv()

    def summed(zz):
        rows = pl.ds(pl.multiple_of(zz * ROWS, 16), ROWS)
        return q[rows_of(zz, x), :] + xr[0, rows, :].astype(F32) + xr[1, rows, :].astype(F32)

    zs[...] = summed(1 - zl).astype(BF)
    hop = send(zs, zr, p_s.at[5], p_r.at[5], zpair)
    hop.wait_recv()
    q[0:ROWS, :] = summed(zl) + zr[...].astype(F32)
    dn[:, mine] = q[pl.ds(pl.multiple_of(c * 24, 8), 24), :]
    last = send(
        q.at[pl.ds(pl.multiple_of((1 - c) * 24, 8), 24), :], dn.at[:, mine],
        p_s.at[6], p_r.at[6], core,
    )
    last.wait_recv()

    inputs = li_ref[...].astype(F32)
    rms = jnp.sqrt(jnp.mean(inputs * inputs, axis=1, keepdims=True) + 1e-06)
    unit = inputs / rms
    scaled = gain_ref[...] * dn[...]
    inner = jnp.mean(scaled * unit, axis=1, keepdims=True)
    ig_out[...] = ((scaled - unit * inner) / rms).astype(BF)
    total = jnp.sum(dn[...] * unit, axis=0, keepdims=True)
    for s, peers in enumerate(([core], xs_dev, zs_dev, ys_dev)):
        gs[s] = total
        cps = []
        for k, to in enumerate(peers):
            cps.append(send(gs.at[s], gr.at[s, k], g_sem.at[s, k], g_rec.at[s, k], to))
        for k, cp in enumerate(cps):
            cp.wait_recv()
            total = total + gr[s, k]
    gain_out[...] = total

    for k in range(NC):
        for part, chunk in enumerate((PART_A[k], PART_B[k])):
            ref = view(mid, chunk)
            remote(ref, ref, far_s.at[part, k], far_r.at[part, k], core).wait_recv()
            near(part, chunk, k, part, True)

    for which, parts in ((0, PART_A), (1, PART_B)):
        for k in range(NC):
            chunk = parts[k]
            value = view(own, chunk)[...]
            for part in (0, 1):
                ref = view(into.at[part], chunk)
                remote(
                    ref, ref, near_s.at[part, which, k], near_r.at[part, which, k], core
                ).wait_recv()
                value = value + ref[...].astype(F32)
            view(t_out, chunk)[...] = value.astype(BF)
    for cp in sent:
        cp.wait_send()


def reduce(n, g, xp, p, layer_input, gain):
    vmem = pl.BlockSpec(memory_space=pltpu.VMEM)
    hbm = pl.BlockSpec(memory_space=pl.ANY)
    dma = pltpu.SemaphoreType.DMA
    v = pltpu.VMEM
    return pl.pallas_call(
        reduce_kernel,
        out_shape=[
            jax.ShapeDtypeStruct((TR, BLK), BF),
            jax.ShapeDtypeStruct((24, D), BF),
            jax.ShapeDtypeStruct((1, D), F32),
        ],
        in_specs=[hbm, hbm, vmem, vmem, vmem, vmem],
        out_specs=[vmem] * 3,
        scratch_shapes=[
            v((4, PLANE, BLK), BF),
            v((4, PLANE, BLK), BF),
            v((XW, PLANE), BF),
            v((TR, BLK), BF),
            v((TR, BLK), BF),
            v((2, TR, BLK), BF),
            v((2, TR, BLK), BF),
            v((TR, BLK), F32),
            v((GROUP, HALF), BF),
            v((GROUP, HALF), F32),
            v((2 * ROWS, HALF), BF),
            v((2 * ROWS, HALF), BF),
            v((2, 2 * ROWS, HALF), BF),
            v((2, 2 * ROWS, HALF), BF),
            v((ROWS, HALF), BF),
            v((ROWS, HALF), BF),
            v((24, D), F32),
            v((4, 1, D), F32),
            v((4, 3, 1, D), F32),
            dma((2, 4)),
            dma((2, NC)),
            dma((2, NC)),
            dma((2, 2, NC)),
            dma((2, 2, NC)),
            dma((7,)),
            dma((7,)),
            dma((4, 3)),
            dma((4, 3)),
        ],
        compiler_params=pltpu.CompilerParams(
            collective_id=1, has_side_effects=True, vmem_limit_bytes=60 << 20
        ),
    )(n, g, xp, p, layer_input, gain)


def body(layer_input, gain_vector, w_gate, w_up, w_down, grad_out):
    gain = gain_vector[None, :]
    normed, upstream, packed, share = gather(
        layer_input, grad_out, gain, w_gate.T, w_up.T, w_down
    )
    terms, input_gradient, gain_gradient = reduce(
        normed, upstream, packed, share, layer_input, gain
    )

    def unpack(k):
        rest = 3 * MAIN + 32 * k
        return jnp.concatenate([terms[k * MAIN:(k + 1) * MAIN], terms[rest:rest + REM]], axis=0)

    return input_gradient, gain_gradient[0], unpack(0).T, unpack(1).T, unpack(2)


def solution(mesh):
    return jax.shard_map(
        body,
        mesh=mesh,
        in_specs=(
            P(("dp", "tensor"), None),
            P(),
            P(None, "tensor"),
            P(None, "tensor"),
            P("tensor", None),
            P(("dp", "tensor"), None),
        ),
        out_specs=(
            P(("dp", "tensor"), None),
            P(),
            P("dp", "tensor"),
            P("dp", "tensor"),
            P("tensor", "dp"),
        ),
        check_vma=False,
    )
```

```python
import functools

import jax
import jax.numpy as jnp
from jax import lax
from jax.experimental import pallas as pl
from jax.experimental.pallas import tpu as pltpu
from jax.sharding import PartitionSpec as P

MESH = pl.DeviceIdType.MESH
BF = jnp.bfloat16
F32 = jnp.float32
D = 4096
HALF = 2048
QUART = 1024
ROWS = 48
PLANE = 768
GROUP = 384
BLK = 512
CORE_FF = 924
PIECES = ((0, 256, 0), (256, 208, 768), (464, 256, 1392), (720, 204, 2160))
TR = 2784


def padded(units):
    return (units + 15) // 16 * 16


def coords():
    dp = lax.axis_index("dp")
    t = lax.axis_index("tensor")
    y = dp // 2
    z = (dp % 2) * 2 + (t // 2) % 2
    return t // 4, y, z, t % 2


def device(x, y, z, c):
    x, y, z, c = (x + 4) % 4, (y + 4) % 4, (z + 4) % 4, (c + 2) % 2
    return (y * 2 + z // 2, x * 4 + (z % 2) * 2 + c)


def remote(src, dst, ss, rs, to):
    return pltpu.make_async_remote_copy(
        src_ref=src, dst_ref=dst, send_sem=ss, recv_sem=rs, device_id=to, device_id_type=MESH
    )


def greet(peers):
    barrier = pltpu.get_barrier_semaphore()
    for to in peers:
        pl.semaphore_signal(barrier, inc=1, device_id=to, device_id_type=MESH)
    pl.semaphore_wait(barrier, len(peers))


OFFS = (0, -1, 1, 2)


def slot(i, j):
    return (i % 4) * 4 + (j % 4)


def contract_cols(left, right):
    return lax.dot_general(left, right, (((1,), (1,)), ((), ())), preferred_element_type=F32)


def gather_kernel(
    li_ref, go_ref, gain_ref, wg_hbm, wu_hbm, wd_hbm,
    n_hbm, g_hbm, xt_hbm, r_hbm, e_hbm, p_hbm,
    ng, xt, dg_ref, du_ref, p_ref, wg, wu, wd, other, stage,
    w_sem, out_sem, ex_s, ex_r, s_sem, r_sem, c_s, c_r, y_s, y_r, e_s, e_r,
):
    x, y, z, c = coords()
    s = 1 - 2 * (z % 2)
    sy = 1 - 2 * (y % 2)
    zh = z // 2
    core = device(x, y, z, 1 - c)
    step = {
        "x": (device(x + 1, y, z, c), device(x - 1, y, z, c)),
        "z": (device(x, y, z + s, c), device(x, y, z - s, c)),
    }
    far = {"x": device(x + 2, y, z, c), "z": device(x, y, z + 2, c)}
    near_y = (device(x, y + sy, z, c), device(x, y - sy, z, c))
    weights = [
        pltpu.make_async_copy(src, dst, w_sem.at[k])
        for k, (src, dst) in enumerate(((wg_hbm, wg), (wu_hbm, wu), (wd_hbm, wd)))
    ]
    greet([core, *step["x"], *step["z"], far["x"], far["z"], *near_y])
    swaps = []
    for a, ref in enumerate((li_ref, go_ref)):
        cp = remote(ref, other.at[a], ex_s.at[a], ex_r.at[a], core)
        cp.start()
        swaps.append(cp)
    for cp in weights:
        cp.start()

    base = pl.multiple_of((z * 4 + x) * ROWS, 16)
    first = c == 0
    n_ref, g_ref = ng.at[0], ng.at[1]
    outs = (n_ref, g_ref)

    swaps[0].wait_recv()
    scale = []
    for ref in (li_ref, other.at[0]):
        rows = ref[...].astype(F32)
        scale.append(jnp.sqrt(jnp.mean(rows * rows, axis=1, keepdims=True) + 1e-06))
    swaps[1].wait_recv()
    for k in range(8):
        cols = pl.ds(k * 512, 512)
        mine = (li_ref[:, cols].astype(F32) / scale[0]) * gain_ref[:, cols]
        theirs = (other[0, :, cols].astype(F32) / scale[1]) * gain_ref[:, cols]
        both = jnp.concatenate(
            [jnp.where(first, mine, theirs), jnp.where(first, theirs, mine)], axis=0
        )
        n_ref[pl.ds(base, ROWS), cols] = both.astype(BF)
        mine = go_ref[:, cols].astype(F32)
        theirs = other[1, :, cols].astype(F32)
        both = jnp.concatenate(
            [jnp.where(first, mine, theirs), jnp.where(first, theirs, mine)], axis=0
        )
        g_ref[pl.ds(base, ROWS), cols] = both.astype(BF)

    lo = pl.multiple_of(c * HALF, 128)
    wide = (pl.ds(lo, HALF), pl.ds(lo, QUART), pl.ds(pl.multiple_of(lo + QUART, 128), QUART))
    theirs = pl.ds(pl.multiple_of((1 - c) * HALF, 128), HALF)

    def place(a, i, j):
        dz, dx = (j, i) if a == 0 else (i, j)
        zz, xx = (z + s * dz + 4) % 4, (x + dx + 4) % 4
        return pl.ds(pl.multiple_of((zz * 4 + xx) * ROWS, 16), ROWS)

    def block(a, i, j, part=0):
        return outs[a].at[place(a, i, j), wide[part]]

    sent = []
    count = [0, 0]

    def push(a, leg, way, i, j, part=0):
        axis = ("x", "z")[(a + leg) % 2]
        to = step[axis][0 if way > 0 else 1]
        at = (i, j)[leg]
        at = at - way if axis == "x" else way - at
        ri, rj = (at, j) if leg == 0 else (i, at)
        ref = block(a, i, j, part)
        k = 1 if part == 2 else 0
        cp = remote(ref, ref, s_sem.at[a, count[a]], r_sem.at[a, slot(ri, rj), k], to)
        count[a] += 1
        cp.start()
        sent.append(cp)

    def arrive(a, i, j):
        for part in (1, 2) if (i, j) == (2, 0) or j == 2 else (0,):
            ref = block(a, i, j, part)
            k = 1 if part == 2 else 0
            remote(ref, ref, s_sem.at[a, 0], r_sem.at[a, slot(i, j), k], core).wait_recv()
        if j == 0:
            if i in (1, -1):
                push(a, 0, -i, i, 0, 1 if i < 0 else 2)
            push(a, 1, 1, i, 0)
            push(a, 1, -1, i, 0)
        elif j in (1, -1):
            push(a, 1, -j, i, j, 1 if j < 0 else 2)
        ref = block(a, i, j)
        k = slot(i, j)
        cp = remote(ref, ref, c_s.at[a, k], c_r.at[a, k], core)
        cp.start()
        sent.append(cp)

    for a in (0, 1):
        for way in (1, -1):
            push(a, 0, way, 0, 0)
            push(a, 1, way, 0, 0)

    def hop(src, dst, k, to):
        cp = remote(src, dst, e_s.at[k], e_r.at[k], to)
        cp.start()
        sent.append(cp)

    def landed(ref, k):
        remote(ref, ref, e_s.at[k], e_r.at[k], core).wait_recv()

    for q, to in enumerate(near_y):
        for k, yy in enumerate((y + (sy if q == 0 else -sy), y + 2)):
            cols = pl.ds(pl.multiple_of(((yy + 4) % 4) * 2 * BLK, 128), 2 * BLK)
            hop(ng.at[c, pl.ds(base, ROWS), cols], stage.at[2 * q + k], 2 * q + k, to)

    stored = []
    tally = [0]

    def store(src, dst):
        cp = pltpu.make_async_copy(src, dst, out_sem.at[tally[0]])
        tally[0] += 1
        cp.start()
        return cp

    def set_cols(which):
        return pl.ds(pl.multiple_of(which * BLK, 128), BLK)

    def extra_z():
        for k in range(4):
            landed(stage.at[k], k)
        mine = e_hbm.at[c, :, z, x]
        local = store(stage.at[:, :, set_cols(zh)], mine)
        hop(stage.at[:, :, set_cols(zh)], mine, 4, step["z"][0])
        hop(stage.at[:, :, set_cols(1 - zh)], mine, 5, step["z"][1])
        hop(stage.at[:, :, set_cols(1 - zh)], mine, 6, far["z"])
        return local

    def extra_x(local):
        local.wait()
        for k, dz in ((4, 1), (5, -1), (6, 2)):
            landed(e_hbm.at[c, :, (z + s * dz + 4) % 4, x], k)
        mine = e_hbm.at[c, :, :, x]
        hop(mine, mine, 7, step["x"][0])
        hop(mine, mine, 8, step["x"][1])
        hop(mine, mine, 9, far["x"])
        hop(mine, mine, 10, core)

    def extra_share(k, dx):
        ref = e_hbm.at[c, :, :, (x + dx + 4) % 4]
        landed(ref, k)
        hop(ref, ref, k + 4, core)

    def group_of(k):
        return (zh + k) % 2

    def chunk_rows(k):
        return pl.ds(pl.multiple_of(group_of(k) * GROUP, 16), GROUP)

    def chunk_ready(k):
        for dz in ((0, 1), (-1, 2))[k]:
            for a in (0, 1):
                for dx in OFFS:
                    i, j = (dx, dz) if a == 0 else (dz, dx)
                    if (i, j) != (0, 0):
                        ref = outs[a].at[place(a, i, j), theirs]
                        at = slot(i, j)
                        remote(ref, ref, c_s.at[a, at], c_r.at[a, at], core).wait_recv()
        rows = chunk_rows(k)
        stored.append(store(n_ref.at[rows, :], n_hbm.at[rows, :]))
        stored.append(store(g_ref.at[rows, :], g_hbm.at[rows, :]))

    def term_view(ref, k, p):
        _, w, row = PIECES[p]
        lanes = pl.ds(pl.multiple_of(group_of(k) * GROUP, 128), GROUP)
        return ref.at[pl.ds(row, 3 * padded(w)), lanes]

    def piece(k, p):
        f, w, row = PIECES[p]
        rows = chunk_rows(k)
        normed = n_ref[rows, :]
        gate = contract_cols(normed, wg[f:f + w, :])
        up = contract_cols(normed, wu[f:f + w, :])
        d_hidden = contract_cols(g_ref[rows, :], wd[f:f + w, :])
        sigma = jax.nn.sigmoid(gate)
        silu = gate * sigma
        hidden = silu * up
        d_gate = d_hidden * up * sigma * (1.0 + gate * (1.0 - sigma))
        d_up = d_hidden * silu
        if k == 0:
            dg_ref[:, f:f + w] = d_gate.astype(BF)
            du_ref[:, f:f + w] = d_up.astype(BF)
        size = padded(w)
        lanes = pl.ds(pl.multiple_of(group_of(k) * GROUP, 128), GROUP)
        for q, value in enumerate((d_gate, d_up, hidden)):
            if w < 256:
                value = jnp.concatenate([value, jnp.zeros((GROUP, 256 - w), F32)], axis=1)
            xt[row + q * size:row + (q + 1) * size, lanes] = value.T[:size].astype(BF)
        cp = remote(
            term_view(xt, k, p), term_view(r_hbm, k, p),
            y_s.at[k, p], y_r.at[k, p], near_y[p // 2],
        )
        cp.start()
        sent.append(cp)
        stored.append(store(term_view(xt, k, p), term_view(xt_hbm, k, p)))

    def moves(*items):
        for item in items:
            arrive(*item)

    moves((0, -1, 0), (1, 0, -1), (0, 1, 0), (1, 0, 1))
    moves((1, 1, 0), (0, 0, 1), (0, 2, 0), (1, 0, 2))
    moves((1, -1, 0), (0, 0, -1))
    moves((0, -1, 1), (1, 1, -1), (0, 1, 1), (1, 1, 1))
    moves((0, -1, -1), (1, -1, -1), (0, 1, -1), (1, -1, 1))
    moves((0, 2, 1), (1, 1, 2))
    for cp in weights:
        cp.wait()
    chunk_ready(0)
    piece(0, 0)
    moves((1, 2, 0), (0, 0, 2), (1, -1, 2), (0, 2, -1))
    piece(0, 2)
    moves((0, -1, 2), (0, 1, 2), (1, 2, -1), (1, 2, 1))
    piece(0, 1)
    moves((0, 2, 2), (1, 2, 2))
    local = extra_z()
    piece(0, 3)
    chunk_ready(1)
    piece(1, 0)
    extra_x(local)
    piece(1, 2)
    piece(1, 1)
    piece(1, 3)

    def share(k):
        cols = slice(k * 512, (k + 1) * 512)
        value = jnp.dot(dg_ref[...], wg[:, cols], preferred_element_type=F32)
        value = value + jnp.dot(du_ref[...], wu[:, cols], preferred_element_type=F32)
        p_ref[:, cols] = value.astype(BF)

    for k in range(4):
        share(k)
    extra_share(7, -1)
    extra_share(8, 1)
    for k in range(4, 8):
        share(k)
    stored.append(store(p_ref, p_hbm))
    extra_share(9, 2)
    for k, dx in ((10, 0), (11, -1), (12, 1), (13, 2)):
        landed(e_hbm.at[1 - c, :, :, (x + dx + 4) % 4], k)
    for k in (0, 1):
        for p in range(4):
            ref = term_view(r_hbm, k, p)
            remote(ref, ref, y_s.at[k, p], y_r.at[k, p], core).wait_recv()
    for cp in swaps + sent:
        cp.wait_send()
    for cp in stored:
        cp.wait()


def gather(layer_input, grad_out, gain, w_gate, w_up, w_down):
    vmem = pl.BlockSpec(memory_space=pltpu.VMEM)
    hbm = pl.BlockSpec(memory_space=pl.ANY)
    dma = pltpu.SemaphoreType.DMA
    v = pltpu.VMEM
    return pl.pallas_call(
        gather_kernel,
        out_shape=[
            jax.ShapeDtypeStruct((PLANE, D), BF),
            jax.ShapeDtypeStruct((PLANE, D), BF),
            jax.ShapeDtypeStruct((TR, PLANE), BF),
            jax.ShapeDtypeStruct((TR, PLANE), BF),
            jax.ShapeDtypeStruct((2, 4, 4, 4, ROWS, BLK), BF),
            jax.ShapeDtypeStruct((GROUP, D), BF),
        ],
        in_specs=[vmem] * 3 + [hbm] * 3,
        out_specs=[hbm] * 6,
        scratch_shapes=[
            v((2, PLANE, D), BF),
            v((TR, PLANE), BF),
            v((GROUP, CORE_FF), BF),
            v((GROUP, CORE_FF), BF),
            v((GROUP, D), BF),
            v((CORE_FF, D), BF),
            v((CORE_FF, D), BF),
            v((CORE_FF, D), BF),
            v((2, 24, D), BF),
            v((4, ROWS, 2 * BLK), BF),
            dma((3,)),
            dma((14,)),
            dma((2,)),
            dma((2,)),
            dma((2, 20)),
            dma((2, 16, 2)),
            dma((2, 16)),
            dma((2, 16)),
            dma((2, 4)),
            dma((2, 4)),
            dma((14,)),
            dma((14,)),
        ],
        compiler_params=pltpu.CompilerParams(
            collective_id=0, has_side_effects=True, vmem_limit_bytes=60 << 20
        ),
    )(layer_input, grad_out, gain, w_gate, w_up, w_down)


def reduce_kernel(
    n_hbm, g_hbm, e_hbm, xt, rt, p_ref, li_ref, gain_ref,
    t_out, ig_out, gain_out,
    nb, eb, outgo, into, own,
    pc, q, xo, xi, xs, xr, zs, zr, dn, gs, gr,
    load, t_s, t_r, p_s, p_r, g_sem, g_rec,
):
    x, y, z, c = coords()
    zl, zh = z % 2, z // 2
    sy = 1 - 2 * (y % 2)
    core = device(x, y, z, 1 - c)
    xs_dev = [device(x + k, y, z, c) for k in (1, -1, 2)]
    ys_dev = [device(x, y + k, z, c) for k in (1, -1, 2)]
    zs_dev = [device(x, y, z + k, c) for k in (1, -1, 2)]
    zpair = device(x, y, zh * 2 + 1 - zl, c)
    alpha, beta = device(x, y + sy, z, c), device(x, y - sy, z, c)

    loads = {}

    def fetch(b):
        yy = (y + (0, sy, -sy)[b] + 4) % 4
        cols = pl.ds(pl.multiple_of((yy * 2 + zh) * BLK, 128), BLK)
        loads["n", b] = [
            pltpu.make_async_copy(n_hbm.at[:, cols], nb.at[0, b], load.at[0, b]),
            pltpu.make_async_copy(g_hbm.at[:, cols], nb.at[1, b], load.at[1, b]),
        ]
        for cp in loads["n", b]:
            cp.start()

    def fetch_extra(b):
        loads["e", b] = [
            pltpu.make_async_copy(e_hbm.at[a, b], eb.at[a, b], load.at[a, 3 + b]) for a in (0, 1)
        ]
        for cp in loads["e", b]:
            cp.start()

    fetch(2)
    fetch_extra(1)
    fetch(1)
    fetch_extra(3)
    fetch(0)
    fetch_extra(0)
    fetch_extra(2)

    def ready(*keys):
        for key in keys:
            for cp in loads[key]:
                cp.wait()

    greet([core, *xs_dev, *ys_dev, *zs_dev])
    sent = []

    def send(src, dst, ss, rs, to):
        cp = remote(src, dst, ss, rs, to)
        cp.start()
        sent.append(cp)
        return cp

    mine = pl.ds(pl.multiple_of(c * HALF, 128), HALF)
    theirs = pl.ds(pl.multiple_of((1 - c) * HALF, 128), HALF)
    swap = send(p_ref.at[:, theirs], pc, p_s.at[0], p_r.at[0], core)

    def ranges(p):
        _, w, row = PIECES[p]
        w = padded(w)
        return ((row, 2 * w, 0), (row + 2 * w, w, 1))

    def term(rng, b, e):
        row, size, a = rng
        rows = slice(row, row + size)
        value = jnp.dot(xt[rows, :], nb[a, b], preferred_element_type=F32)
        return value + jnp.dot(rt[rows, :], eb[a, e], preferred_element_type=F32)

    for k in (0, 1):
        for half, (b, e, to) in enumerate(((2, 1, beta), (1, 3, alpha))):
            if k == 0:
                ready(("n", b), ("e", e))
            p = 2 * half + k
            for rng in ranges(p):
                row, size, a = rng
                outgo[row:row + size, :] = term(rng, b, e).astype(BF)
                rows = pl.ds(row, size)
                send(outgo.at[rows, :], into.at[rows, :], t_s.at[p, a], t_r.at[p, a], to)
    ready(("n", 0), ("e", 0), ("e", 2))
    for p in range(4):
        for rng in ranges(p):
            row, size, _ = rng
            own[row:row + size, :] = term(rng, 0, 0 if p < 2 else 2)

    swap.wait_recv()
    q[...] = p_ref[:, mine].astype(F32) + pc[...].astype(F32)

    def rows_of(zz, xx):
        return pl.ds(pl.multiple_of((zz * 4 + (xx + 4) % 4) * ROWS, 16), ROWS)

    for zz in (0, 1):
        xo[zz * ROWS:(zz + 1) * ROWS, :] = q[rows_of(zz, x + 2), :].astype(BF)
    far = [
        send(
            xo.at[:, pl.ds(k * QUART, QUART)], xi.at[:, pl.ds(k * QUART, QUART)],
            p_s.at[1 + k], p_r.at[1 + k], xs_dev[k],
        )
        for k in (0, 1)
    ]
    step = []
    for k in (0, 1):
        far[k].wait_recv()
        for zz in (0, 1):
            rows = pl.ds(zz * ROWS, ROWS)
            src = rows_of(zz, x + (1 if k == 0 else -1))
            for half in (0, 1):
                cols = pl.ds(half * QUART, QUART)
                value = q[src, cols]
                if half == k:
                    value = value + xi[rows, cols].astype(F32)
                xs[k, rows, cols] = value.astype(BF)
        step.append(send(xs.at[k], xr.at[k], p_s.at[3 + k], p_r.at[3 + k], xs_dev[k]))
    for k in (0, 1):
        step[k].wait_recv()

    def summed(zz):
        rows = pl.ds(pl.multiple_of(zz * ROWS, 16), ROWS)
        return q[rows_of(zz, x), :] + xr[0, rows, :].astype(F32) + xr[1, rows, :].astype(F32)

    zs[...] = summed(1 - zl).astype(BF)
    hop = send(zs, zr, p_s.at[5], p_r.at[5], zpair)
    hop.wait_recv()
    q[0:ROWS, :] = summed(zl) + zr[...].astype(F32)
    dn[:, mine] = q[pl.ds(pl.multiple_of(c * 24, 8), 24), :]
    last = send(
        q.at[pl.ds(pl.multiple_of((1 - c) * 24, 8), 24), :], dn.at[:, mine],
        p_s.at[6], p_r.at[6], core,
    )
    last.wait_recv()

    inputs = li_ref[...].astype(F32)
    rms = jnp.sqrt(jnp.mean(inputs * inputs, axis=1, keepdims=True) + 1e-06)
    unit = inputs / rms
    scaled = gain_ref[...] * dn[...]
    inner = jnp.mean(scaled * unit, axis=1, keepdims=True)
    ig_out[...] = ((scaled - unit * inner) / rms).astype(BF)
    total = jnp.sum(dn[...] * unit, axis=0, keepdims=True)
    for s, peers in enumerate(([core], xs_dev, zs_dev, ys_dev)):
        gs[s] = total
        cps = []
        for k, to in enumerate(peers):
            cps.append(send(gs.at[s], gr.at[s, k], g_sem.at[s, k], g_rec.at[s, k], to))
        for k, cp in enumerate(cps):
            cp.wait_recv()
            total = total + gr[s, k]
    gain_out[...] = total

    for k in (0, 1):
        for p in (k, k + 2):
            for row, size, a in ranges(p):
                rows = pl.ds(row, size)
                ref = into.at[rows, :]
                remote(ref, ref, t_s.at[p, a], t_r.at[p, a], core).wait_recv()
                t_out[rows, :] = (own[rows, :] + ref[...].astype(F32)).astype(BF)
    for cp in sent:
        cp.wait_send()


def reduce(n, g, e, xt, rt, p, layer_input, gain):
    vmem = pl.BlockSpec(memory_space=pltpu.VMEM)
    hbm = pl.BlockSpec(memory_space=pl.ANY)
    dma = pltpu.SemaphoreType.DMA
    v = pltpu.VMEM
    return pl.pallas_call(
        reduce_kernel,
        out_shape=[
            jax.ShapeDtypeStruct((TR, BLK), BF),
            jax.ShapeDtypeStruct((24, D), BF),
            jax.ShapeDtypeStruct((1, D), F32),
        ],
        in_specs=[hbm] * 3 + [vmem] * 5,
        out_specs=[vmem] * 3,
        scratch_shapes=[
            v((2, 3, PLANE, BLK), BF),
            v((2, 4, PLANE, BLK), BF),
            v((TR, BLK), BF),
            v((TR, BLK), BF),
            v((TR, BLK), F32),
            v((GROUP, HALF), BF),
            v((GROUP, HALF), F32),
            v((2 * ROWS, HALF), BF),
            v((2 * ROWS, HALF), BF),
            v((2, 2 * ROWS, HALF), BF),
            v((2, 2 * ROWS, HALF), BF),
            v((ROWS, HALF), BF),
            v((ROWS, HALF), BF),
            v((24, D), F32),
            v((4, 1, D), F32),
            v((4, 3, 1, D), F32),
            dma((2, 7)),
            dma((4, 2)),
            dma((4, 2)),
            dma((7,)),
            dma((7,)),
            dma((4, 3)),
            dma((4, 3)),
        ],
        compiler_params=pltpu.CompilerParams(
            collective_id=1, has_side_effects=True, vmem_limit_bytes=60 << 20
        ),
    )(n, g, e, xt, rt, p, layer_input, gain)


def body(layer_input, gain_vector, w_gate, w_up, w_down, grad_out):
    gain = gain_vector[None, :]
    normed, upstream, terms_t, near_t, extra, share = gather(
        layer_input, grad_out, gain, w_gate.T, w_up.T, w_down
    )
    terms, input_gradient, gain_gradient = reduce(
        normed, upstream, extra.reshape(2, 4, PLANE, BLK), terms_t, near_t, share,
        layer_input, gain,
    )

    def unpack(k):
        parts = []
        for _, w, row in PIECES:
            first = row + k * padded(w)
            parts.append(terms[first:first + w])
        return jnp.concatenate(parts, axis=0)

    return input_gradient, gain_gradient[0], unpack(0).T, unpack(1).T, unpack(2)


def solution(mesh):
    return jax.shard_map(
        body,
        mesh=mesh,
        in_specs=(
            P(("dp", "tensor"), None),
            P(),
            P(None, "tensor"),
            P(None, "tensor"),
            P("tensor", None),
            P(("dp", "tensor"), None),
        ),
        out_specs=(
            P(("dp", "tensor"), None),
            P(),
            P("dp", "tensor"),
            P("dp", "tensor"),
            P("tensor", "dp"),
        ),
        check_vma=False,
    )
```

```python
import functools

import jax
import jax.numpy as jnp
from jax import lax
from jax.experimental import pallas as pl
from jax.experimental.pallas import tpu as pltpu
from jax.sharding import PartitionSpec as P

MESH = pl.DeviceIdType.MESH
BF = jnp.bfloat16
F32 = jnp.float32
D = 4096
HALF = 2048
QUART = 1024
ROWS = 48
PLANE = 768
GROUP = 384
BLK = 512
CORE_FF = 924
MAIN = 896
REM = CORE_FF - MAIN
PIECES = ((0, 256), (256, 256), (512, 256), (768, 156))
LAYOUT = (
    ((0, 0, 256, 0), (1, 0, 256, 256), (2, 0, 256, 512)),
    ((0, 0, 256, 768), (1, 0, 256, 1024), (2, 0, 128, 1280), (2, 128, 128, 1408)),
    ((0, 0, 256, 1536), (1, 0, 256, 1792), (2, 0, 256, 2048)),
    ((0, 0, 128, 2304), (1, 0, 128, 2432), (2, 0, 128, 2560)),
)
TAIL = 2688
XW = TAIL + 128
HALF_X = XW // 2
SENDS = (((0, 768, 0),), ((768, 640, 0), (1408, 128, 1)), ((1536, 768, 1),), ((2304, 512, 1),))
RANGES = (
    ((0, 512, 0), (512, 256, 1), (768, 512, 0), (1280, 128, 1)),
    ((1408, 128, 1), (1536, 512, 0), (2048, 256, 1), (2304, 256, 0), (2560, 128, 1), (TAIL, 128, 2)),
)


def coords():
    dp = lax.axis_index("dp")
    t = lax.axis_index("tensor")
    y = dp // 2
    z = (dp % 2) * 2 + (t // 2) % 2
    return t // 4, y, z, t % 2


def device(x, y, z, c):
    x, y, z, c = (x + 4) % 4, (y + 4) % 4, (z + 4) % 4, (c + 2) % 2
    return (y * 2 + z // 2, x * 4 + (z % 2) * 2 + c)


def remote(src, dst, ss, rs, to):
    return pltpu.make_async_remote_copy(
        src_ref=src, dst_ref=dst, send_sem=ss, recv_sem=rs, device_id=to, device_id_type=MESH
    )


def greet(peers):
    barrier = pltpu.get_barrier_semaphore()
    for to in peers:
        pl.semaphore_signal(barrier, inc=1, device_id=to, device_id_type=MESH)
    pl.semaphore_wait(barrier, len(peers))


OFFS = (0, -1, 1, 2)


def slot(i, j):
    return (i % 4) * 4 + (j % 4)


def contract_cols(left, right):
    return lax.dot_general(left, right, (((1,), (1,)), ((), ())), preferred_element_type=F32)


def contract_rows(left, right):
    return lax.dot_general(left, right, (((0,), (0,)), ((), ())), preferred_element_type=F32)


def gather_kernel(
    li_ref, go_ref, gain_ref, wg_hbm, wu_hbm, wd_hbm,
    n_hbm, g_hbm, x_hbm, r_hbm, e_hbm, p_hbm, pc_hbm,
    ng, x_ref, dg_ref, du_ref, p_ref, wg, wu, wd, other, stage,
    w_sem, out_sem, ex_s, ex_r, s_sem, r_sem, c_s, c_r, y_s, y_r, e_s, e_r, p_s, p_r,
):
    x, y, z, c = coords()
    s = 1 - 2 * (z % 2)
    sy = 1 - 2 * (y % 2)
    zh = z // 2
    core = device(x, y, z, 1 - c)
    step = {
        "x": (device(x + 1, y, z, c), device(x - 1, y, z, c)),
        "z": (device(x, y, z + s, c), device(x, y, z - s, c)),
    }
    far = {"x": device(x + 2, y, z, c), "z": device(x, y, z + 2, c)}
    near_y = (device(x, y + sy, z, c), device(x, y - sy, z, c))
    weights = [
        pltpu.make_async_copy(src, dst, w_sem.at[k])
        for k, (src, dst) in enumerate(((wg_hbm, wg), (wu_hbm, wu), (wd_hbm, wd)))
    ]
    greet([core, *step["x"], *step["z"], far["x"], far["z"], *near_y])
    swaps = []
    for a, ref in enumerate((li_ref, go_ref)):
        cp = remote(ref, other.at[a], ex_s.at[a], ex_r.at[a], core)
        cp.start()
        swaps.append(cp)
    for cp in weights:
        cp.start()

    base = pl.multiple_of((z * 4 + x) * ROWS, 16)
    first = c == 0
    n_ref, g_ref = ng.at[0], ng.at[1]
    outs = (n_ref, g_ref)

    swaps[0].wait_recv()
    scale = []
    for ref in (li_ref, other.at[0]):
        rows = ref[...].astype(F32)
        scale.append(jnp.sqrt(jnp.mean(rows * rows, axis=1, keepdims=True) + 1e-06))
    swaps[1].wait_recv()
    for k in range(8):
        cols = pl.ds(k * 512, 512)
        mine = (li_ref[:, cols].astype(F32) / scale[0]) * gain_ref[:, cols]
        theirs = (other[0, :, cols].astype(F32) / scale[1]) * gain_ref[:, cols]
        both = jnp.concatenate(
            [jnp.where(first, mine, theirs), jnp.where(first, theirs, mine)], axis=0
        )
        n_ref[pl.ds(base, ROWS), cols] = both.astype(BF)
        mine = go_ref[:, cols].astype(F32)
        theirs = other[1, :, cols].astype(F32)
        both = jnp.concatenate(
            [jnp.where(first, mine, theirs), jnp.where(first, theirs, mine)], axis=0
        )
        g_ref[pl.ds(base, ROWS), cols] = both.astype(BF)

    lo = pl.multiple_of(c * HALF, 128)
    wide = (pl.ds(lo, HALF), pl.ds(lo, QUART), pl.ds(pl.multiple_of(lo + QUART, 128), QUART))
    theirs = pl.ds(pl.multiple_of((1 - c) * HALF, 128), HALF)

    def place(a, i, j):
        dz, dx = (j, i) if a == 0 else (i, j)
        zz, xx = (z + s * dz + 4) % 4, (x + dx + 4) % 4
        return pl.ds(pl.multiple_of((zz * 4 + xx) * ROWS, 16), ROWS)

    def block(a, i, j, part=0):
        return outs[a].at[place(a, i, j), wide[part]]

    sent = []
    count = [0, 0]

    def push(a, leg, way, i, j, part=0):
        axis = ("x", "z")[(a + leg) % 2]
        to = step[axis][0 if way > 0 else 1]
        at = (i, j)[leg]
        at = at - way if axis == "x" else way - at
        ri, rj = (at, j) if leg == 0 else (i, at)
        ref = block(a, i, j, part)
        k = 1 if part == 2 else 0
        cp = remote(ref, ref, s_sem.at[a, count[a]], r_sem.at[a, slot(ri, rj), k], to)
        count[a] += 1
        cp.start()
        sent.append(cp)

    def arrive(a, i, j):
        for part in (1, 2) if (i, j) == (2, 0) or j == 2 else (0,):
            ref = block(a, i, j, part)
            k = 1 if part == 2 else 0
            remote(ref, ref, s_sem.at[a, 0], r_sem.at[a, slot(i, j), k], core).wait_recv()
        if j == 0:
            if i in (1, -1):
                push(a, 0, -i, i, 0, 1 if i < 0 else 2)
            push(a, 1, 1, i, 0)
            push(a, 1, -1, i, 0)
        elif j in (1, -1):
            push(a, 1, -j, i, j, 1 if j < 0 else 2)
        ref = block(a, i, j)
        k = slot(i, j)
        cp = remote(ref, ref, c_s.at[a, k], c_r.at[a, k], core)
        cp.start()
        sent.append(cp)

    for a in (0, 1):
        for way in (1, -1):
            push(a, 0, way, 0, 0)
            push(a, 1, way, 0, 0)

    def hop(src, dst, k, to):
        cp = remote(src, dst, e_s.at[k], e_r.at[k], to)
        cp.start()
        sent.append(cp)

    def landed(ref, k):
        remote(ref, ref, e_s.at[k], e_r.at[k], core).wait_recv()

    for q, to in enumerate(near_y):
        for k, yy in enumerate((y + (sy if q == 0 else -sy), y + 2)):
            cols = pl.ds(pl.multiple_of(((yy + 4) % 4) * 2 * BLK, 128), 2 * BLK)
            hop(ng.at[c, pl.ds(base, ROWS), cols], stage.at[2 * q + k], 2 * q + k, to)

    stored = []
    tally = [0]

    def store(src, dst):
        cp = pltpu.make_async_copy(src, dst, out_sem.at[tally[0]])
        tally[0] += 1
        cp.start()
        return cp

    def set_cols(which):
        return pl.ds(pl.multiple_of(which * BLK, 128), BLK)

    def extra_z():
        for k in range(4):
            landed(stage.at[k], k)
        mine = e_hbm.at[c, :, z, x]
        local = store(stage.at[:, :, set_cols(zh)], mine)
        hop(stage.at[:, :, set_cols(zh)], mine, 4, step["z"][0])
        hop(stage.at[:, :, set_cols(1 - zh)], mine, 5, step["z"][1])
        hop(stage.at[:, :, set_cols(1 - zh)], mine, 6, far["z"])
        return local

    def extra_x(local):
        local.wait()
        for k, dz in ((4, 1), (5, -1), (6, 2)):
            landed(e_hbm.at[c, :, (z + s * dz + 4) % 4, x], k)
        mine = e_hbm.at[c, :, :, x]
        hop(mine, mine, 7, step["x"][0])
        hop(mine, mine, 8, step["x"][1])
        hop(mine, mine, 10, core)

    def extra_share(k, dx):
        xx = (x + dx + 4) % 4
        ref = e_hbm.at[c, :, :, xx]
        landed(ref, k)
        half = e_hbm.at[c, pl.ds(0 if dx < 0 else 2, 2), :, xx]
        hop(half, half, 9 if dx < 0 else 14, step["x"][0 if dx < 0 else 1])
        hop(ref, ref, k + 4, core)

    def extra_last():
        xx = (x + 2) % 4
        landed(e_hbm.at[c, pl.ds(0, 2), :, xx], 9)
        landed(e_hbm.at[c, pl.ds(2, 2), :, xx], 14)
        ref = e_hbm.at[c, :, :, xx]
        hop(ref, ref, 13, core)

    sizes = (192, 192, GROUP)

    def chunk_rows(k):
        first = (z * 192, (z + s) * 192, (1 - zh) * GROUP)[k]
        return pl.ds(pl.multiple_of(first, 16), sizes[k])

    def chunk_ready(k):
        for dz in ((0,), (1,), (-1, 2))[k]:
            for a in (0, 1):
                for dx in OFFS:
                    i, j = (dx, dz) if a == 0 else (dz, dx)
                    if (i, j) != (0, 0):
                        ref = outs[a].at[place(a, i, j), theirs]
                        at = slot(i, j)
                        remote(ref, ref, c_s.at[a, at], c_r.at[a, at], core).wait_recv()
        rows = chunk_rows(k)
        stored.append(store(n_ref.at[rows, :], n_hbm.at[rows, :]))
        stored.append(store(g_ref.at[rows, :], g_hbm.at[rows, :]))

    def piece(k, p):
        f, w = PIECES[p]
        rows = chunk_rows(k)
        normed = n_ref[rows, :]
        gate = contract_cols(normed, wg[f:f + w, :])
        up = contract_cols(normed, wu[f:f + w, :])
        d_hidden = contract_cols(g_ref[rows, :], wd[f:f + w, :])
        sigma = jax.nn.sigmoid(gate)
        silu = gate * sigma
        hidden = (silu * up).astype(BF)
        d_gate = (d_hidden * up * sigma * (1.0 + gate * (1.0 - sigma))).astype(BF)
        d_up = (d_hidden * silu).astype(BF)
        if k < 2:
            own = pl.ds(pl.multiple_of((z % 2 if k == 0 else 1 - z % 2) * 192, 16), 192)
            dg_ref[own, f:f + w] = d_gate
            du_ref[own, f:f + w] = d_up
        values = (d_gate, d_up, hidden)
        for q, first, count, col in LAYOUT[p]:
            x_ref[rows, col:col + count] = values[q][:, first:first + count]
        if w < 256:
            gap = jnp.zeros((sizes[k], 32 - REM), BF)
            rest = []
            for value in values:
                rest += [value[:, w - REM:], gap]
            rest.append(jnp.zeros((sizes[k], 32), BF))
            x_ref[rows, TAIL:] = jnp.concatenate(rest, axis=1)
        for n, (col, count, to) in enumerate(SENDS[p]):
            view = (rows, pl.ds(col, count))
            at = p + 3 * n
            cp = remote(x_ref.at[view], r_hbm.at[view], y_s.at[k, at], y_r.at[k, at], near_y[to])
            cp.start()
            sent.append(cp)
        if p == 3:
            stored.append(store(x_ref.at[rows, :], x_hbm.at[rows, :]))

    def moves(*items):
        for item in items:
            arrive(*item)

    moves((0, -1, 0), (1, 0, -1), (0, 1, 0), (1, 0, 1))
    moves((1, 1, 0), (0, 0, 1), (1, -1, 0), (0, 0, -1))
    moves((0, 2, 0), (1, 0, 2))
    for cp in weights:
        cp.wait()
    chunk_ready(0)
    piece(0, 0)
    moves((0, -1, 1), (1, 1, -1), (0, 1, 1), (1, 1, 1))
    piece(0, 2)
    moves((0, -1, -1), (1, -1, -1), (0, 1, -1), (1, -1, 1))
    piece(0, 1)
    moves((0, 2, 1), (1, 1, 2))
    local = extra_z()
    piece(0, 3)
    moves((1, 2, 0), (0, 0, 2), (1, -1, 2), (0, 2, -1))
    chunk_ready(1)
    piece(1, 0)
    moves((0, -1, 2), (0, 1, 2), (1, 2, -1), (1, 2, 1))
    extra_x(local)
    piece(1, 2)
    piece(1, 1)
    moves((0, 2, 2), (1, 2, 2))
    piece(1, 3)
    chunk_ready(2)
    piece(2, 0)
    piece(2, 2)
    extra_share(7, -1)
    extra_share(8, 1)
    piece(2, 1)
    piece(2, 3)

    swap = None
    for which in (1, 0):
        for k in range(4):
            lo = (c if which == 0 else 1 - c) * HALF + k * BLK
            cols = pl.ds(pl.multiple_of(lo, 128), BLK)
            value = jnp.dot(dg_ref[...], wg[:, cols], preferred_element_type=F32)
            value = value + jnp.dot(du_ref[...], wu[:, cols], preferred_element_type=F32)
            p_ref[which, :, k * BLK:(k + 1) * BLK] = value.astype(BF)
        if which:
            swap = remote(p_ref.at[1], pc_hbm, p_s.at[0], p_r.at[0], core)
            swap.start()
            extra_last()
    stored.append(store(p_ref.at[0], p_hbm))
    for k, dx in ((10, 0), (11, -1), (12, 1), (13, 2)):
        landed(e_hbm.at[1 - c, :, :, (x + dx + 4) % 4], k)
    swap.wait()
    for k in range(3):
        rows = chunk_rows(k)
        for p in range(4):
            for n, (col, count, _) in enumerate(SENDS[p]):
                ref = r_hbm.at[rows, pl.ds(col, count)]
                at = p + 3 * n
                remote(ref, ref, y_s.at[k, at], y_r.at[k, at], core).wait_recv()
    for cp in swaps + sent:
        cp.wait_send()
    for cp in stored:
        cp.wait()


def gather(layer_input, grad_out, gain, w_gate, w_up, w_down):
    vmem = pl.BlockSpec(memory_space=pltpu.VMEM)
    hbm = pl.BlockSpec(memory_space=pl.ANY)
    dma = pltpu.SemaphoreType.DMA
    v = pltpu.VMEM
    return pl.pallas_call(
        gather_kernel,
        out_shape=[
            jax.ShapeDtypeStruct((PLANE, D), BF),
            jax.ShapeDtypeStruct((PLANE, D), BF),
            jax.ShapeDtypeStruct((PLANE, XW), BF),
            jax.ShapeDtypeStruct((PLANE, XW), BF),
            jax.ShapeDtypeStruct((2, 4, 4, 4, ROWS, BLK), BF),
            jax.ShapeDtypeStruct((GROUP, HALF), BF),
            jax.ShapeDtypeStruct((GROUP, HALF), BF),
        ],
        in_specs=[vmem] * 3 + [hbm] * 3,
        out_specs=[hbm] * 7,
        scratch_shapes=[
            v((2, PLANE, D), BF),
            v((PLANE, XW), BF),
            v((GROUP, CORE_FF), BF),
            v((GROUP, CORE_FF), BF),
            v((2, GROUP, HALF), BF),
            v((CORE_FF, D), BF),
            v((CORE_FF, D), BF),
            v((CORE_FF, D), BF),
            v((2, 24, D), BF),
            v((4, ROWS, 2 * BLK), BF),
            dma((3,)),
            dma((14,)),
            dma((2,)),
            dma((2,)),
            dma((2, 20)),
            dma((2, 16, 2)),
            dma((2, 16)),
            dma((2, 16)),
            dma((3, 5)),
            dma((3, 5)),
            dma((15,)),
            dma((15,)),
            dma((1,)),
            dma((1,)),
        ],
        compiler_params=pltpu.CompilerParams(
            collective_id=0, has_side_effects=True, vmem_limit_bytes=60 << 20
        ),
    )(layer_input, grad_out, gain, w_gate, w_up, w_down)


def reduce_kernel(
    n_hbm, g_hbm, e_hbm, own_x, near_x, p_ref, pc_ref, li_ref, gain_ref,
    gate_out, up_out, down_out, ig_out, gain_out,
    nb, eb, outgo, into, own,
    q, xo, xi, xs, xr, zs, zr, dn, gs, gr,
    load, t_s, t_r, p_s, p_r, g_sem, g_rec,
):
    x, y, z, c = coords()
    zl, zh = z % 2, z // 2
    sy = 1 - 2 * (y % 2)
    core = device(x, y, z, 1 - c)
    xs_dev = [device(x + k, y, z, c) for k in (1, -1, 2)]
    ys_dev = [device(x, y + k, z, c) for k in (1, -1, 2)]
    zs_dev = [device(x, y, z + k, c) for k in (1, -1, 2)]
    zpair = device(x, y, zh * 2 + 1 - zl, c)
    alpha, beta = device(x, y + sy, z, c), device(x, y - sy, z, c)

    loads = {}

    def fetch(b):
        yy = (y + (0, sy, -sy)[b] + 4) % 4
        cols = pl.ds(pl.multiple_of((yy * 2 + zh) * BLK, 128), BLK)
        loads["n", b] = [
            pltpu.make_async_copy(n_hbm.at[:, cols], nb.at[0, b], load.at[0, b]),
            pltpu.make_async_copy(g_hbm.at[:, cols], nb.at[1, b], load.at[1, b]),
        ]
        for cp in loads["n", b]:
            cp.start()

    def fetch_extra(b):
        loads["e", b] = [
            pltpu.make_async_copy(e_hbm.at[a, b], eb.at[a, b], load.at[a, 3 + b]) for a in (0, 1)
        ]
        for cp in loads["e", b]:
            cp.start()

    fetch(2)
    fetch_extra(1)
    fetch(1)
    fetch_extra(3)
    fetch(0)
    fetch_extra(0)
    fetch_extra(2)

    def ready(*keys):
        for key in keys:
            for cp in loads[key]:
                cp.wait()

    greet([core, *xs_dev, *ys_dev, *zs_dev])
    sent = []

    def send(src, dst, ss, rs, to):
        cp = remote(src, dst, ss, rs, to)
        cp.start()
        sent.append(cp)
        return cp

    mine = pl.ds(pl.multiple_of(c * HALF, 128), HALF)
    q[...] = p_ref[...].astype(F32) + pc_ref[...].astype(F32)

    def rows_of(zz, xx):
        return pl.ds(pl.multiple_of((zz * 4 + (xx + 4) % 4) * ROWS, 16), ROWS)

    for zz in (0, 1):
        xo[zz * ROWS:(zz + 1) * ROWS, :] = q[rows_of(zz, x + 2), :].astype(BF)
    far = [
        send(
            xo.at[:, pl.ds(k * QUART, QUART)], xi.at[:, pl.ds(k * QUART, QUART)],
            p_s.at[1 + k], p_r.at[1 + k], xs_dev[k],
        )
        for k in (0, 1)
    ]

    def term(rng, b, e):
        row, size, a = rng

        def product(a):
            cols = slice(row, row + size)
            value = contract_rows(own_x[:, cols], nb[a, b])
            return value + contract_rows(near_x[:, cols], eb[a, e])

        if a < 2:
            return product(a)
        return jnp.concatenate([product(0)[:64], product(1)[64:]], axis=0)

    ready(("n", 2), ("e", 1))
    ready(("n", 1), ("e", 3))
    for k in range(6):
        for half, (b, e, to) in enumerate(((2, 1, beta), (1, 3, alpha))):
            if k < len(RANGES[half]):
                row, size, _ = RANGES[half][k]
                rows = pl.ds(row, size)
                outgo[rows, :] = term(RANGES[half][k], b, e).astype(BF)
                send(outgo.at[rows, :], into.at[rows, :], t_s.at[half, k], t_r.at[half, k], to)

    def own_terms(half):
        for rng in RANGES[half]:
            own[rng[0]:rng[0] + rng[1], :] = term(rng, 0, 2 * half)

    step = []
    for k in (0, 1):
        far[k].wait_recv()
        for zz in (0, 1):
            rows = pl.ds(zz * ROWS, ROWS)
            src = rows_of(zz, x + (1 if k == 0 else -1))
            for half in (0, 1):
                cols = pl.ds(half * QUART, QUART)
                value = q[src, cols]
                if half == k:
                    value = value + xi[rows, cols].astype(F32)
                xs[k, rows, cols] = value.astype(BF)
        step.append(send(xs.at[k], xr.at[k], p_s.at[3 + k], p_r.at[3 + k], xs_dev[k]))
    ready(("n", 0), ("e", 0), ("e", 2))
    own_terms(0)
    for k in (0, 1):
        step[k].wait_recv()

    def summed(zz):
        rows = pl.ds(pl.multiple_of(zz * ROWS, 16), ROWS)
        return q[rows_of(zz, x), :] + xr[0, rows, :].astype(F32) + xr[1, rows, :].astype(F32)

    zs[...] = summed(1 - zl).astype(BF)
    hop = send(zs, zr, p_s.at[5], p_r.at[5], zpair)
    own_terms(1)
    hop.wait_recv()
    q[0:ROWS, :] = summed(zl) + zr[...].astype(F32)
    dn[:, mine] = q[pl.ds(pl.multiple_of(c * 24, 8), 24), :]
    last = send(
        q.at[pl.ds(pl.multiple_of((1 - c) * 24, 8), 24), :], dn.at[:, mine],
        p_s.at[6], p_r.at[6], core,
    )
    last.wait_recv()

    inputs = li_ref[...].astype(F32)
    rms = jnp.sqrt(jnp.mean(inputs * inputs, axis=1, keepdims=True) + 1e-06)
    unit = inputs / rms
    scaled = gain_ref[...] * dn[...]
    inner = jnp.mean(scaled * unit, axis=1, keepdims=True)
    ig_out[...] = ((scaled - unit * inner) / rms).astype(BF)
    total = jnp.sum(dn[...] * unit, axis=0, keepdims=True)
    for s, peers in enumerate(([core], xs_dev, zs_dev, ys_dev)):
        gs[s] = total
        cps = []
        for k, to in enumerate(peers):
            cps.append(send(gs.at[s], gr.at[s, k], g_sem.at[s, k], g_rec.at[s, k], to))
        for k, cp in enumerate(cps):
            cp.wait_recv()
            total = total + gr[s, k]
    gain_out[...] = total

    outs = (gate_out, up_out, down_out)
    for k in range(6):
        for half in (0, 1):
            if k >= len(RANGES[half]):
                continue
            row, size, _ = RANGES[half][k]
            rows = pl.ds(row, size)
            ref = into.at[rows, :]
            remote(ref, ref, t_s.at[half, k], t_r.at[half, k], core).wait_recv()
            value = own[rows, :] + ref[...].astype(F32)
            if row == TAIL:
                for which in range(3):
                    rest = value[32 * which:32 * which + REM]
                    outs[which][MAIN:, :] = rest.astype(BF)
                continue
            for (unit, _), items in zip(PIECES, LAYOUT):
                for which, first, count, col in items:
                    if row <= col < row + size:
                        at = unit + first
                        outs[which][at:at + count, :] = value[col - row:col - row + count].astype(BF)
    for cp in sent:
        cp.wait_send()


def reduce(n, g, e, own_x, near_x, p, pc, layer_input, gain):
    vmem = pl.BlockSpec(memory_space=pltpu.VMEM)
    hbm = pl.BlockSpec(memory_space=pl.ANY)
    dma = pltpu.SemaphoreType.DMA
    v = pltpu.VMEM
    return pl.pallas_call(
        reduce_kernel,
        out_shape=[
            jax.ShapeDtypeStruct((CORE_FF, BLK), BF),
            jax.ShapeDtypeStruct((CORE_FF, BLK), BF),
            jax.ShapeDtypeStruct((CORE_FF, BLK), BF),
            jax.ShapeDtypeStruct((24, D), BF),
            jax.ShapeDtypeStruct((1, D), F32),
        ],
        in_specs=[hbm] * 3 + [vmem] * 6,
        out_specs=[vmem] * 5,
        scratch_shapes=[
            v((2, 3, PLANE, BLK), BF),
            v((2, 4, PLANE, BLK), BF),
            v((XW, BLK), BF),
            v((XW, BLK), BF),
            v((XW, BLK), F32),
            v((GROUP, HALF), F32),
            v((2 * ROWS, HALF), BF),
            v((2 * ROWS, HALF), BF),
            v((2, 2 * ROWS, HALF), BF),
            v((2, 2 * ROWS, HALF), BF),
            v((ROWS, HALF), BF),
            v((ROWS, HALF), BF),
            v((24, D), F32),
            v((4, 1, D), F32),
            v((4, 3, 1, D), F32),
            dma((2, 7)),
            dma((2, 6)),
            dma((2, 6)),
            dma((7,)),
            dma((7,)),
            dma((4, 3)),
            dma((4, 3)),
        ],
        compiler_params=pltpu.CompilerParams(
            collective_id=1, has_side_effects=True, vmem_limit_bytes=60 << 20
        ),
    )(n, g, e, own_x, near_x, p, pc, layer_input, gain)


def body(layer_input, gain_vector, w_gate, w_up, w_down, grad_out):
    gain = gain_vector[None, :]
    normed, upstream, own_x, near_x, extra, share, core_share = gather(
        layer_input, grad_out, gain, w_gate.T, w_up.T, w_down
    )
    gate, up, down, input_gradient, gain_gradient = reduce(
        normed, upstream, extra.reshape(2, 4, PLANE, BLK), own_x, near_x, share, core_share,
        layer_input, gain,
    )
    return input_gradient, gain_gradient[0], gate.T, up.T, down


def solution(mesh):
    return jax.shard_map(
        body,
        mesh=mesh,
        in_specs=(
            P(("dp", "tensor"), None),
            P(),
            P(None, "tensor"),
            P(None, "tensor"),
            P("tensor", None),
            P(("dp", "tensor"), None),
        ),
        out_specs=(
            P(("dp", "tensor"), None),
            P(),
            P("dp", "tensor"),
            P("dp", "tensor"),
            P("tensor", "dp"),
        ),
        check_vma=False,
    )
```

```python
import functools

import jax
import jax.numpy as jnp
from jax import lax
from jax.experimental import pallas as pl
from jax.experimental.pallas import tpu as pltpu
from jax.sharding import PartitionSpec as P

MESH = pl.DeviceIdType.MESH
BF = jnp.bfloat16
F32 = jnp.float32
D = 4096
HALF = 2048
QUART = 1024
ROWS = 48
PLANE = 768
GROUP = 384
BLK = 512
CORE_FF = 924
MAIN = 896
REM = CORE_FF - MAIN
PIECES = ((0, 256), (256, 256), (512, 256), (768, 156))
LAYOUT = (
    ((0, 0, 256, 0), (1, 0, 256, 256), (2, 0, 256, 512)),
    ((0, 0, 256, 768), (1, 0, 256, 1024), (2, 0, 128, 1280), (2, 128, 128, 1408)),
    ((0, 0, 256, 1536), (1, 0, 256, 1792), (2, 0, 256, 2048)),
    ((0, 0, 128, 2304), (1, 0, 128, 2432), (2, 0, 128, 2560)),
)
TAIL = 2688
XW = TAIL + 128
HALF_X = XW // 2
SENDS = (((0, 768, 0),), ((768, 640, 0), (1408, 128, 1)), ((1536, 768, 1),), ((2304, 512, 1),))
ROOM = (
    ((0, 0), (512, 0), (0, 1), (512, 1)),
    ((640, 1), (0, 2), (512, 2), (0, 3), (256, 3), (384, 3)),
)
RANGES = (
    ((0, 512, 0), (512, 256, 1), (768, 512, 0), (1280, 128, 1)),
    ((1408, 128, 1), (1536, 512, 0), (2048, 256, 1), (2304, 256, 0), (2560, 128, 1), (TAIL, 128, 2)),
)


def coords():
    dp = lax.axis_index("dp")
    t = lax.axis_index("tensor")
    y = dp // 2
    z = (dp % 2) * 2 + (t // 2) % 2
    return t // 4, y, z, t % 2


def device(x, y, z, c):
    x, y, z, c = (x + 4) % 4, (y + 4) % 4, (z + 4) % 4, (c + 2) % 2
    return (y * 2 + z // 2, x * 4 + (z % 2) * 2 + c)


def remote(src, dst, ss, rs, to):
    return pltpu.make_async_remote_copy(
        src_ref=src, dst_ref=dst, send_sem=ss, recv_sem=rs, device_id=to, device_id_type=MESH
    )


def greet(peers):
    barrier = pltpu.get_barrier_semaphore()
    for to in peers:
        pl.semaphore_signal(barrier, inc=1, device_id=to, device_id_type=MESH)
    pl.semaphore_wait(barrier, len(peers))


OFFS = (0, -1, 1, 2)


def slot(i, j):
    return (i % 4) * 4 + (j % 4)


def contract_cols(left, right):
    return lax.dot_general(left, right, (((1,), (1,)), ((), ())), preferred_element_type=F32)


def contract_rows(left, right):
    return lax.dot_general(left, right, (((0,), (0,)), ((), ())), preferred_element_type=F32)


def kernel(
    li_ref, go_ref, gain_ref, wg_hbm, wu_hbm, wd_hbm,
    gate_out, up_out, down_out, ig_out, gain_out, e_hbm,
    ng, x_ref, r_ref, dg_ref, du_ref, wg, wu, wd, other, stage,
    into, pc, xi, xr, zr, fin, dn, gs, gr,
    w_sem, out_sem, ex_s, ex_r, s_sem, r_sem, c_s, c_r, y_s, y_r, e_s, e_r,
    load, t_s, t_r, p_s, p_r, g_sem, g_rec,
):
    x, y, z, c = coords()
    s = 1 - 2 * (z % 2)
    sy = 1 - 2 * (y % 2)
    zl, zh = z % 2, z // 2
    core = device(x, y, z, 1 - c)
    xs_dev = [device(x + k, y, z, c) for k in (1, -1, 2)]
    ys_dev = [device(x, y + sy * k, z, c) for k in (1, -1, 2)]
    zs_dev = [device(x, y, z + s * k, c) for k in (1, -1, 2)]
    step = {"x": xs_dev[:2], "z": zs_dev[:2]}
    near_y = ys_dev[:2]
    zpair = zs_dev[0]
    weights = [
        pltpu.make_async_copy(src, dst, w_sem.at[k])
        for k, (src, dst) in enumerate(((wg_hbm, wg), (wu_hbm, wu), (wd_hbm, wd)))
    ]
    greet([core, *xs_dev, *ys_dev, *zs_dev])
    swaps = []
    for a, ref in enumerate((li_ref, go_ref)):
        cp = remote(ref, other.at[a], ex_s.at[a], ex_r.at[a], core)
        cp.start()
        swaps.append(cp)
    for cp in weights:
        cp.start()

    base = pl.multiple_of((z * 4 + x) * ROWS, 16)
    first = c == 0
    n_ref, g_ref = ng.at[0], ng.at[1]
    outs = (n_ref, g_ref)

    swaps[0].wait_recv()
    scale = []
    for ref in (li_ref, other.at[0]):
        rows = ref[...].astype(F32)
        scale.append(jnp.sqrt(jnp.mean(rows * rows, axis=1, keepdims=True) + 1e-06))
    swaps[1].wait_recv()
    for k in range(8):
        cols = pl.ds(k * 512, 512)
        mine = (li_ref[:, cols].astype(F32) / scale[0]) * gain_ref[:, cols]
        theirs = (other[0, :, cols].astype(F32) / scale[1]) * gain_ref[:, cols]
        both = jnp.concatenate(
            [jnp.where(first, mine, theirs), jnp.where(first, theirs, mine)], axis=0
        )
        n_ref[pl.ds(base, ROWS), cols] = both.astype(BF)
        mine = go_ref[:, cols].astype(F32)
        theirs = other[1, :, cols].astype(F32)
        both = jnp.concatenate(
            [jnp.where(first, mine, theirs), jnp.where(first, theirs, mine)], axis=0
        )
        g_ref[pl.ds(base, ROWS), cols] = both.astype(BF)

    lo = pl.multiple_of(c * HALF, 128)
    wide = (pl.ds(lo, HALF), pl.ds(lo, QUART), pl.ds(pl.multiple_of(lo + QUART, 128), QUART))
    theirs = pl.ds(pl.multiple_of((1 - c) * HALF, 128), HALF)

    def place(a, i, j):
        dz, dx = (j, i) if a == 0 else (i, j)
        zz, xx = (z + s * dz + 4) % 4, (x + dx + 4) % 4
        return pl.ds(pl.multiple_of((zz * 4 + xx) * ROWS, 16), ROWS)

    def block(a, i, j, part=0):
        return outs[a].at[place(a, i, j), wide[part]]

    sent, sent_ng = [], []
    count = [0, 0]

    def push(a, leg, way, i, j, part=0):
        axis = ("x", "z")[(a + leg) % 2]
        to = step[axis][0 if way > 0 else 1]
        at = (i, j)[leg]
        at = at - way if axis == "x" else way - at
        ri, rj = (at, j) if leg == 0 else (i, at)
        ref = block(a, i, j, part)
        k = 1 if part == 2 else 0
        cp = remote(ref, ref, s_sem.at[a, count[a]], r_sem.at[a, slot(ri, rj), k], to)
        count[a] += 1
        cp.start()
        sent_ng.append(cp)

    def arrive(a, i, j):
        for part in (1, 2) if (i, j) == (2, 0) or j == 2 else (0,):
            ref = block(a, i, j, part)
            k = 1 if part == 2 else 0
            remote(ref, ref, s_sem.at[a, 0], r_sem.at[a, slot(i, j), k], core).wait_recv()
        if j == 0:
            if i in (1, -1):
                push(a, 0, -i, i, 0, 1 if i < 0 else 2)
            push(a, 1, 1, i, 0)
            push(a, 1, -1, i, 0)
        elif j in (1, -1):
            push(a, 1, -j, i, j, 1 if j < 0 else 2)
        ref = block(a, i, j)
        k = slot(i, j)
        cp = remote(ref, ref, c_s.at[a, k], c_r.at[a, k], core)
        cp.start()
        sent_ng.append(cp)

    for a in (0, 1):
        for way in (1, -1):
            push(a, 0, way, 0, 0)
            push(a, 1, way, 0, 0)

    def hop(src, dst, k, to, kept=sent):
        cp = remote(src, dst, e_s.at[k], e_r.at[k], to)
        cp.start()
        kept.append(cp)

    def landed(ref, k):
        remote(ref, ref, e_s.at[k], e_r.at[k], core).wait_recv()

    for q, to in enumerate(near_y):
        for k, yy in enumerate((y + (sy if q == 0 else -sy), y + 2)):
            cols = pl.ds(pl.multiple_of(((yy + 4) % 4) * 2 * BLK, 128), 2 * BLK)
            hop(ng.at[c, pl.ds(base, ROWS), cols], stage.at[2 * q + k], 2 * q + k, to, sent_ng)

    tally = [0]

    def store(src, dst):
        cp = pltpu.make_async_copy(src, dst, out_sem.at[tally[0]])
        tally[0] += 1
        cp.start()
        return cp

    def set_cols(which):
        return pl.ds(pl.multiple_of(which * BLK, 128), BLK)

    def place_e(zz, xx):
        return pl.ds(pl.multiple_of((((zz + 4) % 4) * 4 + (xx + 4) % 4) * ROWS, 16), ROWS)

    def extra_z():
        for k in range(4):
            landed(stage.at[k], k)
        mine = e_hbm.at[c, :, place_e(z, x), :]
        local = store(stage.at[:, :, set_cols(zh)], mine)
        hop(stage.at[:, :, set_cols(zh)], mine, 4, zs_dev[0])
        hop(stage.at[:, :, set_cols(1 - zh)], mine, 5, zs_dev[1])
        hop(stage.at[:, :, set_cols(1 - zh)], mine, 6, zs_dev[2])
        return local

    def extra_x(local):
        local.wait()
        for k, dz in ((4, 1), (5, -1), (6, 2)):
            landed(e_hbm.at[c, :, place_e(z + s * dz, x), :], k)
        for zz in range(4):
            mine = e_hbm.at[c, :, place_e(zz, x), :]
            hop(mine, mine, 8 + zz, xs_dev[0])
            hop(mine, mine, 12 + zz, xs_dev[1])
            hop(mine, mine, 16 + zz, core)

    def extra_share(k, dx):
        for zz in range(4):
            rows = place_e(zz, x + dx)
            ref = e_hbm.at[c, :, rows, :]
            landed(ref, k + zz)
            half = e_hbm.at[c, pl.ds(0 if dx < 0 else 2, 2), rows, :]
            hop(half, half, (20 if dx < 0 else 24) + zz, xs_dev[0 if dx < 0 else 1])
            hop(ref, ref, (28 if dx < 0 else 32) + zz, core)

    def extra_last():
        for zz in range(4):
            rows = place_e(zz, x + 2)
            landed(e_hbm.at[c, pl.ds(0, 2), rows, :], 20 + zz)
            landed(e_hbm.at[c, pl.ds(2, 2), rows, :], 24 + zz)
            ref = e_hbm.at[c, :, rows, :]
            hop(ref, ref, 36 + zz, core)

    def extra_done():
        for k, dx in ((16, 0), (28, -1), (32, 1), (36, 2)):
            for zz in range(4):
                landed(e_hbm.at[1 - c, :, place_e(zz, x + dx), :], k + zz)

    sizes = (192, 192, GROUP)

    def chunk_rows(k):
        first = (z * 192, (z + s) * 192, (1 - zh) * GROUP)[k]
        return pl.ds(pl.multiple_of(first, 16), sizes[k])

    def chunk_ready(k):
        for dz in ((0,), (1,), (-1, 2))[k]:
            for a in (0, 1):
                for dx in OFFS:
                    i, j = (dx, dz) if a == 0 else (dz, dx)
                    if (i, j) != (0, 0):
                        ref = outs[a].at[place(a, i, j), theirs]
                        at = slot(i, j)
                        remote(ref, ref, c_s.at[a, at], c_r.at[a, at], core).wait_recv()

    def piece(k, p):
        f, w = PIECES[p]
        rows = chunk_rows(k)
        normed = n_ref[rows, :]
        gate = contract_cols(normed, wg[f:f + w, :])
        up = contract_cols(normed, wu[f:f + w, :])
        d_hidden = contract_cols(g_ref[rows, :], wd[f:f + w, :])
        sigma = jax.nn.sigmoid(gate)
        silu = gate * sigma
        hidden = (silu * up).astype(BF)
        d_gate = (d_hidden * up * sigma * (1.0 + gate * (1.0 - sigma))).astype(BF)
        d_up = (d_hidden * silu).astype(BF)
        if k < 2:
            own = pl.ds(pl.multiple_of((z % 2 if k == 0 else 1 - z % 2) * 192, 16), 192)
            dg_ref[own, f:f + w] = d_gate
            du_ref[own, f:f + w] = d_up
        values = (d_gate, d_up, hidden)
        for q, first, count, col in LAYOUT[p]:
            x_ref[rows, col:col + count] = values[q][:, first:first + count]
        if w < 256:
            gap = jnp.zeros((sizes[k], 32 - REM), BF)
            rest = []
            for value in values:
                rest += [value[:, w - REM:], gap]
            rest.append(jnp.zeros((sizes[k], 32), BF))
            x_ref[rows, TAIL:] = jnp.concatenate(rest, axis=1)
        for n, (col, count, to) in enumerate(SENDS[p]):
            view = (rows, pl.ds(col, count))
            at = p + 3 * n
            cp = remote(x_ref.at[view], r_ref.at[view], y_s.at[k, at], y_r.at[k, at], near_y[to])
            cp.start()
            sent.append(cp)

    def moves(*items):
        for item in items:
            arrive(*item)

    moves((0, -1, 0), (1, 0, -1), (0, 1, 0), (1, 0, 1))
    moves((1, 1, 0), (0, 0, 1), (1, -1, 0), (0, 0, -1))
    moves((0, 2, 0), (1, 0, 2))
    for cp in weights:
        cp.wait()
    chunk_ready(0)
    local = extra_z()
    piece(0, 0)
    moves((0, -1, 1), (1, 1, -1), (0, 1, 1), (1, 1, 1))
    piece(0, 2)
    moves((0, -1, -1), (1, -1, -1), (0, 1, -1), (1, -1, 1))
    piece(0, 1)
    moves((0, 2, 1), (1, 1, 2))
    piece(0, 3)
    moves((1, 2, 0), (0, 0, 2), (1, -1, 2), (0, 2, -1))
    chunk_ready(1)
    extra_x(local)
    piece(1, 0)
    moves((0, -1, 2), (0, 1, 2), (1, 2, -1), (1, 2, 1))
    piece(1, 2)
    piece(1, 1)
    moves((0, 2, 2), (1, 2, 2))
    piece(1, 3)
    chunk_ready(2)
    for p in (0, 2, 1, 3):
        piece(2, p)

    def share_cols(k):
        return pl.ds(pl.multiple_of((2 * k + 1 - zh) * BLK, 128), BLK)

    def share(which):
        for k in range(4):
            lo = (c if which == 0 else 1 - c) * HALF + k * BLK
            cols = pl.ds(pl.multiple_of(lo, 128), BLK)
            value = jnp.dot(dg_ref[...], wg[:, cols], preferred_element_type=F32)
            value = value + jnp.dot(du_ref[...], wu[:, cols], preferred_element_type=F32)
            ng[which, 0:GROUP, share_cols(k)] = value.astype(BF)

    def send(src, dst, ss, rs, to):
        cp = remote(src, dst, ss, rs, to)
        cp.start()
        sent.append(cp)
        return cp

    for cp in sent_ng:
        cp.wait_send()
    share(1)
    swap = [
        send(
            ng.at[1, pl.ds(0, GROUP), share_cols(k)], pc.at[:, pl.ds(k * BLK, BLK)],
            p_s.at[7 + k], p_r.at[7 + k], core,
        )
        for k in range(4)
    ]
    extra_share(8, -1)
    extra_share(12, 1)
    share(0)
    extra_last()

    mine = pl.ds(pl.multiple_of(c * HALF, 128), HALF)
    for k in range(4):
        swap[k].wait_recv()
        value = ng[0, 0:GROUP, share_cols(k)].astype(F32)
        value = value + pc[:, k * BLK:(k + 1) * BLK].astype(F32)
        ng[0, 0:GROUP, share_cols(k)] = value.astype(BF)

    def rows_of(zz, xx):
        return pl.ds(pl.multiple_of((zz * 4 + (xx + 4) % 4) * ROWS, 16), ROWS)

    def room(row, rows, col=HALF, cols=HALF):
        return wg.at[pl.ds(row, rows), pl.ds(col, cols)]

    for zz in (0, 1):
        for k in range(4):
            value = ng[0, rows_of(zz, x + 2), share_cols(k)]
            room(zz * ROWS, ROWS, HALF + k * BLK, BLK)[...] = value
    far = [
        send(
            room(0, 2 * ROWS, HALF + k * QUART, QUART), xi.at[:, pl.ds(k * QUART, QUART)],
            p_s.at[1 + k], p_r.at[1 + k], xs_dev[k],
        )
        for k in (0, 1)
    ]

    extra_done()
    loads = {}
    for b in (1, 3, 0, 2):
        loads[b] = []
        for a in (0, 1):
            dst = wd.at[pl.ds(0, PLANE), pl.ds((4 * a + b) * BLK, BLK)]
            cp = pltpu.make_async_copy(e_hbm.at[a, b], dst, load.at[a, b])
            cp.start()
            loads[b].append(cp)

    def block_cols(b):
        yy = (y + (0, sy, -sy)[b] + 4) % 4
        return pl.ds(pl.multiple_of((yy * 2 + zh) * BLK, 128), BLK)

    def term(rng, b, e):
        row, size, a = rng

        def product(a):
            cols = slice(row, row + size)
            value = contract_rows(x_ref[:, cols], ng[a, :, block_cols(b)])
            extra = wd[0:PLANE, (4 * a + e) * BLK:(4 * a + e + 1) * BLK]
            return value + contract_rows(r_ref[:, cols], extra)

        if a < 2:
            return product(a)
        return jnp.concatenate([product(0)[:64], product(1)[64:]], axis=0)

    def unit(p, n):
        col, count, half = SENDS[p][n]
        for k in range(3):
            ref = r_ref.at[chunk_rows(k), pl.ds(col, count)]
            at = p + 3 * n
            remote(ref, ref, y_s.at[k, at], y_r.at[k, at], core).wait_recv()
        b, e = ((2, 1), (1, 3))[half]
        for k, rng in enumerate(RANGES[half]):
            row, size, _ = rng
            if col <= row < col + count:
                at, lane = ROOM[half][k]
                src = room(at, size, lane * BLK, BLK)
                for piece_row in range(0, size, 256):
                    rows = min(256, size - piece_row)
                    part = (row + piece_row, rows, rng[2])
                    room(at + piece_row, rows, lane * BLK, BLK)[...] = term(part, b, e).astype(BF)
                dst = into.at[pl.ds(row, size), :]
                send(src, dst, t_s.at[half, k], t_r.at[half, k], near_y[1 - half])

    outs = (gate_out, up_out, down_out)

    def emit(rng, value, add):
        row, size, _ = rng
        items = []
        if row == TAIL:
            items = [(which, 32 * which, REM, MAIN) for which in range(3)]
        else:
            for (first, _), parts in zip(PIECES, LAYOUT):
                for which, at, count, col in parts:
                    if row <= col < row + size:
                        items.append((which, col - row, count, first + at))
        for which, at, count, to in items:
            rest = value[at:at + count]
            if add:
                rest = rest + outs[which][to:to + count, :].astype(F32)
            outs[which][to:to + count, :] = rest.astype(BF)

    def own_terms(half, first, last):
        for row, size, a in RANGES[half][first:last]:
            for piece_row in range(0, size, 256):
                part = (row + piece_row, min(256, size - piece_row), a)
                emit(part, term(part, 0, 2 * half), False)

    for b in (1, 3):
        for cp in loads[b]:
            cp.wait()
    unit(0, 0)
    step = []
    for k in (0, 1):
        far[k].wait_recv()
        first = 2 * ROWS * (1 + k)
        for zz in (0, 1):
            rows = pl.ds(zz * ROWS, ROWS)
            src = rows_of(zz, x + (1 if k == 0 else -1))
            for n in range(4):
                cols = pl.ds(n * BLK, BLK)
                value = ng[0, src, share_cols(n)]
                if n // 2 == k:
                    value = (value.astype(F32) + xi[rows, cols].astype(F32)).astype(BF)
                room(first + zz * ROWS, ROWS, HALF + n * BLK, BLK)[...] = value
        step.append(
            send(room(first, 2 * ROWS), xr.at[k], p_s.at[3 + k], p_r.at[3 + k], xs_dev[k])
        )
    unit(2, 0)
    unit(1, 1)
    unit(1, 0)
    for k in (0, 1):
        step[k].wait_recv()

    def summed(zz, n):
        rows = pl.ds(pl.multiple_of(zz * ROWS, 16), ROWS)
        cols = pl.ds(n * BLK, BLK)
        value = ng[0, rows_of(zz, x), share_cols(n)].astype(F32)
        return value + xr[0, rows, cols].astype(F32) + xr[1, rows, cols].astype(F32)

    for n in range(4):
        room(6 * ROWS, ROWS, HALF + n * BLK, BLK)[...] = summed(1 - zl, n).astype(BF)
    over = send(room(6 * ROWS, ROWS), zr, p_s.at[5], p_r.at[5], zpair)
    unit(3, 0)
    over.wait_recv()
    for n in range(4):
        cols = pl.ds(n * BLK, BLK)
        fin[:, cols] = summed(zl, n) + zr[:, cols].astype(F32)
    dn[:, mine] = fin[pl.ds(pl.multiple_of(c * 24, 8), 24), :]
    last = send(
        fin.at[pl.ds(pl.multiple_of((1 - c) * 24, 8), 24), :], dn.at[:, mine],
        p_s.at[6], p_r.at[6], core,
    )
    for b in (0, 2):
        for cp in loads[b]:
            cp.wait()
    own_terms(0, 0, 2)
    last.wait_recv()

    inputs = li_ref[...].astype(F32)
    rms = jnp.sqrt(jnp.mean(inputs * inputs, axis=1, keepdims=True) + 1e-06)
    unit_rows = inputs / rms
    scaled = gain_ref[...] * dn[...]
    inner = jnp.mean(scaled * unit_rows, axis=1, keepdims=True)
    ig_out[...] = ((scaled - unit_rows * inner) / rms).astype(BF)
    total = jnp.sum(dn[...] * unit_rows, axis=0, keepdims=True)
    between = ((0, 2, 3), (0, 3, 4), (1, 0, 2), (1, 2, 4))
    for n, peers in enumerate(([core], xs_dev, zs_dev, ys_dev)):
        gs[n] = total
        cps = [send(gs.at[n], gr.at[n, k], g_sem.at[n, k], g_rec.at[n, k], to) for k, to in enumerate(peers)]
        own_terms(*between[n])
        for k, cp in enumerate(cps):
            cp.wait_recv()
            total = total + gr[n, k]
    gain_out[...] = total
    own_terms(1, 4, 6)

    for half, k in ((0, 0), (0, 1), (1, 1), (1, 2), (1, 0), (0, 2), (0, 3), (1, 3), (1, 4), (1, 5)):
        row, size, a = RANGES[half][k]
        ref = into.at[pl.ds(row, size), :]
        remote(ref, ref, t_s.at[half, k], t_r.at[half, k], core).wait_recv()
        for piece_row in range(row, row + size, 256):
            part = (piece_row, min(256, row + size - piece_row), a)
            emit(part, into[piece_row:piece_row + part[1], :].astype(F32), True)
    for cp in swaps + sent:
        cp.wait_send()


def move_kernel(*refs):
    n = len(refs) // 2
    cps = [
        pltpu.make_async_copy(refs[k], refs[n + k], refs[-1].at[k]) for k in range(n)
    ]
    for cp in cps:
        cp.start()
    for cp in cps:
        cp.wait()


def move_out(*arrays):
    hbm = pl.BlockSpec(memory_space=pltpu.HBM)
    return pl.pallas_call(
        move_kernel,
        out_shape=[jax.ShapeDtypeStruct(a.shape, a.dtype) for a in arrays],
        in_specs=[hbm] * len(arrays),
        out_specs=[hbm] * len(arrays),
        scratch_shapes=[pltpu.SemaphoreType.DMA((len(arrays),))],
    )(*arrays)


def backward(layer_input, grad_out, gain, w_gate, w_up, w_down):
    vmem = pl.BlockSpec(memory_space=pltpu.VMEM)
    hbm = pl.BlockSpec(memory_space=pl.ANY)
    dma = pltpu.SemaphoreType.DMA
    v = pltpu.VMEM
    return pl.pallas_call(
        kernel,
        out_shape=[
            jax.ShapeDtypeStruct((CORE_FF, BLK), BF),
            jax.ShapeDtypeStruct((CORE_FF, BLK), BF),
            jax.ShapeDtypeStruct((CORE_FF, BLK), BF),
            jax.ShapeDtypeStruct((24, D), BF),
            jax.ShapeDtypeStruct((1, D), F32),
            jax.ShapeDtypeStruct((2, 4, PLANE, BLK), BF),
        ],
        in_specs=[vmem] * 3 + [hbm] * 3,
        out_specs=[vmem] * 5 + [hbm],
        scratch_shapes=[
            v((2, PLANE, D), BF),
            v((PLANE, XW), BF),
            v((PLANE, XW), BF),
            v((GROUP, CORE_FF), BF),
            v((GROUP, CORE_FF), BF),
            v((CORE_FF, D), BF),
            v((CORE_FF, D), BF),
            v((CORE_FF, D), BF),
            v((2, 24, D), BF),
            v((4, ROWS, 2 * BLK), BF),
            v((XW, BLK), BF),
            v((GROUP, HALF), BF),
            v((2 * ROWS, HALF), BF),
            v((2, 2 * ROWS, HALF), BF),
            v((ROWS, HALF), BF),
            v((ROWS, HALF), F32),
            v((24, D), F32),
            v((4, 1, D), F32),
            v((4, 3, 1, D), F32),
            dma((3,)),
            dma((1,)),
            dma((2,)),
            dma((2,)),
            dma((2, 20)),
            dma((2, 16, 2)),
            dma((2, 16)),
            dma((2, 16)),
            dma((3, 5)),
            dma((3, 5)),
            dma((40,)),
            dma((40,)),
            dma((2, 4)),
            dma((2, 6)),
            dma((2, 6)),
            dma((11,)),
            dma((11,)),
            dma((4, 3)),
            dma((4, 3)),
        ],
        compiler_params=pltpu.CompilerParams(
            collective_id=0, has_side_effects=True, vmem_limit_bytes=62 << 20
        ),
    )(layer_input, grad_out, gain, w_gate, w_up, w_down)


def body(layer_input, gain_vector, w_gate, w_up, w_down, grad_out):
    gain = gain_vector[None, :]
    results = backward(layer_input, grad_out, gain, w_gate.T, w_up.T, w_down)
    gate, up, down, input_gradient, gain_gradient = move_out(*results[:5])
    return input_gradient, gain_gradient[0], gate.T, up.T, down


def solution(mesh):
    return jax.shard_map(
        body,
        mesh=mesh,
        in_specs=(
            P(("dp", "tensor"), None),
            P(),
            P(None, "tensor"),
            P(None, "tensor"),
            P("tensor", None),
            P(("dp", "tensor"), None),
        ),
        out_specs=(
            P(("dp", "tensor"), None),
            P(),
            P("dp", "tensor"),
            P("dp", "tensor"),
            P("tensor", "dp"),
        ),
        check_vma=False,
    )
```

```python
import functools

import jax
import jax.numpy as jnp
from jax import lax
from jax.experimental import pallas as pl
from jax.experimental.pallas import tpu as pltpu
from jax.sharding import PartitionSpec as P

MESH = pl.DeviceIdType.MESH
BF = jnp.bfloat16
F32 = jnp.float32
D = 4096
HALF = 2048
QUART = 1024
ROWS = 48
PLANE = 768
GROUP = 384
BLK = 512
CORE_FF = 924
MAIN = 896
REM = CORE_FF - MAIN
PIECES = ((0, 256), (256, 256), (512, 256), (768, 156))
LAYOUT = (
    ((0, 0, 256, 0), (1, 0, 256, 256), (2, 0, 256, 512)),
    ((0, 0, 256, 768), (1, 0, 256, 1024), (2, 0, 128, 1280), (2, 128, 128, 1408)),
    ((0, 0, 256, 1536), (1, 0, 256, 1792), (2, 0, 256, 2048)),
    ((0, 0, 128, 2304), (1, 0, 128, 2432), (2, 0, 128, 2560)),
)
TAIL = 2688
XW = TAIL + 128
HALF_X = XW // 2
SENDS = (((0, 768, 0),), ((768, 640, 0), (1408, 128, 1)), ((1536, 768, 1),), ((2304, 512, 1),))
ROOM = (
    ((0, 0), (512, 0), (0, 1), (512, 1)),
    ((640, 1), (0, 2), (512, 2), (0, 3), (256, 3), (384, 3)),
)
RANGES = (
    ((0, 512, 0), (512, 256, 1), (768, 512, 0), (1280, 128, 1)),
    ((1408, 128, 1), (1536, 512, 0), (2048, 256, 1), (2304, 256, 0), (2560, 128, 1), (TAIL, 128, 2)),
)


def coords():
    dp = lax.axis_index("dp")
    t = lax.axis_index("tensor")
    y = dp // 2
    z = (dp % 2) * 2 + (t // 2) % 2
    return t // 4, y, z, t % 2


def device(x, y, z, c):
    x, y, z, c = (x + 4) % 4, (y + 4) % 4, (z + 4) % 4, (c + 2) % 2
    return (y * 2 + z // 2, x * 4 + (z % 2) * 2 + c)


def remote(src, dst, ss, rs, to):
    return pltpu.make_async_remote_copy(
        src_ref=src, dst_ref=dst, send_sem=ss, recv_sem=rs, device_id=to, device_id_type=MESH
    )


def greet(peers):
    barrier = pltpu.get_barrier_semaphore()
    for to in peers:
        pl.semaphore_signal(barrier, inc=1, device_id=to, device_id_type=MESH)
    pl.semaphore_wait(barrier, len(peers))


OFFS = (0, -1, 1, 2)


def slot(i, j):
    return (i % 4) * 4 + (j % 4)


def contract_cols(left, right):
    return lax.dot_general(left, right, (((1,), (1,)), ((), ())), preferred_element_type=F32)


def contract_rows(left, right):
    return lax.dot_general(left, right, (((0,), (0,)), ((), ())), preferred_element_type=F32)


def kernel(
    li_ref, go_ref, gain_ref, wg_hbm, wu_hbm, wd_hbm,
    gate_out, up_out, down_out, ig_out, gain_out, r_hbm,
    ng, x_ref, e_ref, dg_ref, du_ref, wg, wu, wd, other, stage,
    into, pc, xi, xr, zr, fin, dn, gs, gr,
    w_sem, out_sem, ex_s, ex_r, s_sem, r_sem, c_s, c_r, y_s, y_r, e_s, e_r,
    load, t_s, t_r, p_s, p_r, g_sem, g_rec,
):
    x, y, z, c = coords()
    s = 1 - 2 * (z % 2)
    sy = 1 - 2 * (y % 2)
    zl, zh = z % 2, z // 2
    core = device(x, y, z, 1 - c)
    xs_dev = [device(x + k, y, z, c) for k in (1, -1, 2)]
    ys_dev = [device(x, y + sy * k, z, c) for k in (1, -1, 2)]
    zs_dev = [device(x, y, z + s * k, c) for k in (1, -1, 2)]
    step = {"x": xs_dev[:2], "z": zs_dev[:2]}
    near_y = ys_dev[:2]
    zpair = zs_dev[0]
    weights = [
        pltpu.make_async_copy(src, dst, w_sem.at[k])
        for k, (src, dst) in enumerate(((wg_hbm, wg), (wu_hbm, wu), (wd_hbm, wd)))
    ]
    greet([core, *xs_dev, *ys_dev, *zs_dev])
    swaps = []
    for a, ref in enumerate((li_ref, go_ref)):
        cp = remote(ref, other.at[a], ex_s.at[a], ex_r.at[a], core)
        cp.start()
        swaps.append(cp)
    for cp in weights:
        cp.start()

    base = pl.multiple_of((z * 4 + x) * ROWS, 16)
    first = c == 0
    n_ref, g_ref = ng.at[0], ng.at[1]
    outs = (n_ref, g_ref)

    swaps[0].wait_recv()
    scale = []
    for ref in (li_ref, other.at[0]):
        rows = ref[...].astype(F32)
        scale.append(jnp.sqrt(jnp.mean(rows * rows, axis=1, keepdims=True) + 1e-06))
    swaps[1].wait_recv()
    for k in range(8):
        cols = pl.ds(k * 512, 512)
        mine = (li_ref[:, cols].astype(F32) / scale[0]) * gain_ref[:, cols]
        theirs = (other[0, :, cols].astype(F32) / scale[1]) * gain_ref[:, cols]
        both = jnp.concatenate(
            [jnp.where(first, mine, theirs), jnp.where(first, theirs, mine)], axis=0
        )
        n_ref[pl.ds(base, ROWS), cols] = both.astype(BF)
        mine = go_ref[:, cols].astype(F32)
        theirs = other[1, :, cols].astype(F32)
        both = jnp.concatenate(
            [jnp.where(first, mine, theirs), jnp.where(first, theirs, mine)], axis=0
        )
        g_ref[pl.ds(base, ROWS), cols] = both.astype(BF)

    lo = pl.multiple_of(c * HALF, 128)
    wide = (pl.ds(lo, HALF), pl.ds(lo, QUART), pl.ds(pl.multiple_of(lo + QUART, 128), QUART))
    theirs = pl.ds(pl.multiple_of((1 - c) * HALF, 128), HALF)

    def place(a, i, j):
        dz, dx = (j, i) if a == 0 else (i, j)
        zz, xx = (z + s * dz + 4) % 4, (x + dx + 4) % 4
        return pl.ds(pl.multiple_of((zz * 4 + xx) * ROWS, 16), ROWS)

    def block(a, i, j, part=0):
        return outs[a].at[place(a, i, j), wide[part]]

    sent, sent_ng = [], []
    count = [0, 0]

    def push(a, leg, way, i, j, part=0):
        axis = ("x", "z")[(a + leg) % 2]
        to = step[axis][0 if way > 0 else 1]
        at = (i, j)[leg]
        at = at - way if axis == "x" else way - at
        ri, rj = (at, j) if leg == 0 else (i, at)
        ref = block(a, i, j, part)
        k = 1 if part == 2 else 0
        cp = remote(ref, ref, s_sem.at[a, count[a]], r_sem.at[a, slot(ri, rj), k], to)
        count[a] += 1
        cp.start()
        sent_ng.append(cp)

    def arrive(a, i, j):
        for part in (1, 2) if (i, j) == (2, 0) or j == 2 else (0,):
            ref = block(a, i, j, part)
            k = 1 if part == 2 else 0
            remote(ref, ref, s_sem.at[a, 0], r_sem.at[a, slot(i, j), k], core).wait_recv()
        if j == 0:
            if i in (1, -1):
                push(a, 0, -i, i, 0, 1 if i < 0 else 2)
            push(a, 1, 1, i, 0)
            push(a, 1, -1, i, 0)
        elif j in (1, -1):
            push(a, 1, -j, i, j, 1 if j < 0 else 2)
        ref = block(a, i, j)
        k = slot(i, j)
        cp = remote(ref, ref, c_s.at[a, k], c_r.at[a, k], core)
        cp.start()
        sent_ng.append(cp)

    for a in (0, 1):
        for way in (1, -1):
            push(a, 0, way, 0, 0)
            push(a, 1, way, 0, 0)

    def hop(src, dst, k, to, kept=sent):
        cp = remote(src, dst, e_s.at[k], e_r.at[k], to)
        cp.start()
        kept.append(cp)

    def landed(ref, k):
        remote(ref, ref, e_s.at[k], e_r.at[k], core).wait_recv()

    for q, to in enumerate(near_y):
        for k, yy in enumerate((y + (sy if q == 0 else -sy), y + 2)):
            cols = pl.ds(pl.multiple_of(((yy + 4) % 4) * 2 * BLK, 128), 2 * BLK)
            hop(ng.at[c, pl.ds(base, ROWS), cols], stage.at[2 * q + k], 2 * q + k, to, sent_ng)

    tally = [0]

    def store(src, dst):
        cp = pltpu.make_async_copy(src, dst, out_sem.at[tally[0]])
        tally[0] += 1
        cp.start()
        return cp

    def set_cols(which):
        return pl.ds(pl.multiple_of(which * BLK, 128), BLK)

    def place_e(zz, xx):
        return pl.ds(pl.multiple_of((((zz + 4) % 4) * 4 + (xx + 4) % 4) * ROWS, 16), ROWS)

    def extra_z():
        for k in range(4):
            landed(stage.at[k], k)
        mine = e_ref.at[c, :, place_e(z, x), :]
        local = store(stage.at[:, :, set_cols(zh)], mine)
        hop(stage.at[:, :, set_cols(zh)], mine, 4, zs_dev[0])
        hop(stage.at[:, :, set_cols(1 - zh)], mine, 5, zs_dev[1])
        hop(stage.at[:, :, set_cols(1 - zh)], mine, 6, zs_dev[2])
        return local

    def extra_x(local):
        local.wait()
        for k, dz in ((4, 1), (5, -1), (6, 2)):
            landed(e_ref.at[c, :, place_e(z + s * dz, x), :], k)
        for zz in range(4):
            mine = e_ref.at[c, :, place_e(zz, x), :]
            hop(mine, mine, 8 + zz, xs_dev[0])
            hop(mine, mine, 12 + zz, xs_dev[1])
            hop(mine, mine, 16 + zz, core)

    def extra_share(k, dx):
        for zz in range(4):
            rows = place_e(zz, x + dx)
            ref = e_ref.at[c, :, rows, :]
            landed(ref, k + zz)
            half = e_ref.at[c, pl.ds(0 if dx < 0 else 2, 2), rows, :]
            hop(half, half, (20 if dx < 0 else 24) + zz, xs_dev[0 if dx < 0 else 1])
            hop(ref, ref, (28 if dx < 0 else 32) + zz, core)

    def extra_last():
        for zz in range(4):
            rows = place_e(zz, x + 2)
            landed(e_ref.at[c, pl.ds(0, 2), rows, :], 20 + zz)
            landed(e_ref.at[c, pl.ds(2, 2), rows, :], 24 + zz)
            ref = e_ref.at[c, :, rows, :]
            hop(ref, ref, 36 + zz, core)

    def extra_done():
        for k, dx in ((16, 0), (28, -1), (32, 1), (36, 2)):
            for zz in range(4):
                landed(e_ref.at[1 - c, :, place_e(zz, x + dx), :], k + zz)

    sizes = (192, 192, GROUP)

    def chunk_rows(k):
        first = (z * 192, (z + s) * 192, (1 - zh) * GROUP)[k]
        return pl.ds(pl.multiple_of(first, 16), sizes[k])

    def chunk_ready(k):
        for dz in ((0,), (1,), (-1, 2))[k]:
            for a in (0, 1):
                for dx in OFFS:
                    i, j = (dx, dz) if a == 0 else (dz, dx)
                    if (i, j) != (0, 0):
                        ref = outs[a].at[place(a, i, j), theirs]
                        at = slot(i, j)
                        remote(ref, ref, c_s.at[a, at], c_r.at[a, at], core).wait_recv()

    def piece(k, p):
        f, w = PIECES[p]
        rows = chunk_rows(k)
        normed = n_ref[rows, :]
        gate = contract_cols(normed, wg[f:f + w, :])
        up = contract_cols(normed, wu[f:f + w, :])
        d_hidden = contract_cols(g_ref[rows, :], wd[f:f + w, :])
        sigma = jax.nn.sigmoid(gate)
        silu = gate * sigma
        hidden = (silu * up).astype(BF)
        d_gate = (d_hidden * up * sigma * (1.0 + gate * (1.0 - sigma))).astype(BF)
        d_up = (d_hidden * silu).astype(BF)
        if k < 2:
            own = pl.ds(pl.multiple_of((z % 2 if k == 0 else 1 - z % 2) * 192, 16), 192)
            dg_ref[own, f:f + w] = d_gate
            du_ref[own, f:f + w] = d_up
        values = (d_gate, d_up, hidden)
        for q, first, count, col in LAYOUT[p]:
            x_ref[rows, col:col + count] = values[q][:, first:first + count]
        if w < 256:
            gap = jnp.zeros((sizes[k], 32 - REM), BF)
            rest = []
            for value in values:
                rest += [value[:, w - REM:], gap]
            rest.append(jnp.zeros((sizes[k], 32), BF))
            x_ref[rows, TAIL:] = jnp.concatenate(rest, axis=1)
        for n, (col, count, to) in enumerate(SENDS[p]):
            view = (rows, pl.ds(col, count))
            at = p + 3 * n
            cp = remote(x_ref.at[view], r_hbm.at[view], y_s.at[k, at], y_r.at[k, at], near_y[to])
            cp.start()
            sent.append(cp)

    def moves(*items):
        for item in items:
            arrive(*item)

    moves((0, -1, 0), (1, 0, -1), (0, 1, 0), (1, 0, 1))
    moves((1, 1, 0), (0, 0, 1), (1, -1, 0), (0, 0, -1))
    moves((0, 2, 0), (1, 0, 2))
    for cp in weights:
        cp.wait()
    chunk_ready(0)
    local = extra_z()
    piece(0, 0)
    moves((0, -1, 1), (1, 1, -1), (0, 1, 1), (1, 1, 1))
    piece(0, 2)
    moves((0, -1, -1), (1, -1, -1), (0, 1, -1), (1, -1, 1))
    piece(0, 1)
    moves((0, 2, 1), (1, 1, 2))
    piece(0, 3)
    moves((1, 2, 0), (0, 0, 2), (1, -1, 2), (0, 2, -1))
    chunk_ready(1)
    extra_x(local)
    piece(1, 0)
    moves((0, -1, 2), (0, 1, 2), (1, 2, -1), (1, 2, 1))
    piece(1, 2)
    piece(1, 1)
    moves((0, 2, 2), (1, 2, 2))
    piece(1, 3)
    chunk_ready(2)
    for p in (0, 2, 1, 3):
        piece(2, p)

    def share_cols(k):
        return pl.ds(pl.multiple_of((2 * k + 1 - zh) * BLK, 128), BLK)

    def share(which):
        for k in range(4):
            lo = (c if which == 0 else 1 - c) * HALF + k * BLK
            cols = pl.ds(pl.multiple_of(lo, 128), BLK)
            value = jnp.dot(dg_ref[...], wg[:, cols], preferred_element_type=F32)
            value = value + jnp.dot(du_ref[...], wu[:, cols], preferred_element_type=F32)
            ng[which, 0:GROUP, share_cols(k)] = value.astype(BF)

    def send(src, dst, ss, rs, to):
        cp = remote(src, dst, ss, rs, to)
        cp.start()
        sent.append(cp)
        return cp

    for cp in sent_ng:
        cp.wait_send()
    fetched = {}

    def fetch(p, n, k):
        col, count, _ = SENDS[p][n]
        rows, cols, at = chunk_rows(k), pl.ds(col, count), p + 3 * n
        ref = r_hbm.at[rows, cols]
        remote(ref, ref, y_s.at[k, at], y_r.at[k, at], core).wait_recv()
        cp = pltpu.make_async_copy(ref, wd.at[rows, cols], load.at[at, k])
        cp.start()
        fetched[p, n, k] = cp

    share(1)
    swap = [
        send(
            ng.at[1, pl.ds(0, GROUP), share_cols(k)], pc.at[:, pl.ds(k * BLK, BLK)],
            p_s.at[7 + k], p_r.at[7 + k], core,
        )
        for k in range(4)
    ]
    extra_share(8, -1)
    extra_share(12, 1)
    for p, n in ((0, 0), (2, 0), (1, 0), (1, 1), (3, 0)):
        fetch(p, n, 0)
        fetch(p, n, 1)
    share(0)
    extra_last()

    mine = pl.ds(pl.multiple_of(c * HALF, 128), HALF)
    for k in range(4):
        swap[k].wait_recv()
        value = ng[0, 0:GROUP, share_cols(k)].astype(F32)
        value = value + pc[:, k * BLK:(k + 1) * BLK].astype(F32)
        ng[0, 0:GROUP, share_cols(k)] = value.astype(BF)

    def rows_of(zz, xx):
        return pl.ds(pl.multiple_of((zz * 4 + (xx + 4) % 4) * ROWS, 16), ROWS)

    def room(row, rows, col=HALF, cols=HALF):
        return wg.at[pl.ds(row, rows), pl.ds(col, cols)]

    for zz in (0, 1):
        for k in range(4):
            value = ng[0, rows_of(zz, x + 2), share_cols(k)]
            room(zz * ROWS, ROWS, HALF + k * BLK, BLK)[...] = value
    far = [
        send(
            room(0, 2 * ROWS, HALF + k * QUART, QUART), xi.at[:, pl.ds(k * QUART, QUART)],
            p_s.at[1 + k], p_r.at[1 + k], xs_dev[k],
        )
        for k in (0, 1)
    ]

    extra_done()

    def block_cols(b):
        yy = (y + (0, sy, -sy)[b] + 4) % 4
        return pl.ds(pl.multiple_of((yy * 2 + zh) * BLK, 128), BLK)

    def term(rng, b, e):
        row, size, a = rng

        def product(a):
            cols = slice(row, row + size)
            value = contract_rows(x_ref[:, cols], ng[a, :, block_cols(b)])
            return value + contract_rows(wd[0:PLANE, cols], e_ref[a, e])

        if a < 2:
            return product(a)
        return jnp.concatenate([product(0)[:64], product(1)[64:]], axis=0)

    def unit(p, n):
        col, count, half = SENDS[p][n]
        fetch(p, n, 2)
        for k in range(3):
            fetched[p, n, k].wait()
        b, e = ((2, 1), (1, 3))[half]
        for k, rng in enumerate(RANGES[half]):
            row, size, _ = rng
            if col <= row < col + count:
                at, lane = ROOM[half][k]
                src = room(at, size, lane * BLK, BLK)
                for piece_row in range(0, size, 256):
                    rows = min(256, size - piece_row)
                    part = (row + piece_row, rows, rng[2])
                    room(at + piece_row, rows, lane * BLK, BLK)[...] = term(part, b, e).astype(BF)
                dst = into.at[pl.ds(row, size), :]
                send(src, dst, t_s.at[half, k], t_r.at[half, k], near_y[1 - half])

    outs = (gate_out, up_out, down_out)

    def emit(rng, value, add):
        row, size, _ = rng
        items = []
        if row == TAIL:
            items = [(which, 32 * which, REM, MAIN) for which in range(3)]
        else:
            for (first, _), parts in zip(PIECES, LAYOUT):
                for which, at, count, col in parts:
                    if row <= col < row + size:
                        items.append((which, col - row, count, first + at))
        for which, at, count, to in items:
            rest = value[at:at + count]
            if add:
                rest = rest + outs[which][to:to + count, :].astype(F32)
            outs[which][to:to + count, :] = rest.astype(BF)

    def own_terms(half, first, last):
        for row, size, a in RANGES[half][first:last]:
            for piece_row in range(0, size, 256):
                part = (row + piece_row, min(256, size - piece_row), a)
                emit(part, term(part, 0, 2 * half), False)

    unit(0, 0)
    step = []
    for k in (0, 1):
        far[k].wait_recv()
        first = 2 * ROWS * (1 + k)
        for zz in (0, 1):
            rows = pl.ds(zz * ROWS, ROWS)
            src = rows_of(zz, x + (1 if k == 0 else -1))
            for n in range(4):
                cols = pl.ds(n * BLK, BLK)
                value = ng[0, src, share_cols(n)]
                if n // 2 == k:
                    value = (value.astype(F32) + xi[rows, cols].astype(F32)).astype(BF)
                room(first + zz * ROWS, ROWS, HALF + n * BLK, BLK)[...] = value
        step.append(
            send(room(first, 2 * ROWS), xr.at[k], p_s.at[3 + k], p_r.at[3 + k], xs_dev[k])
        )
    unit(2, 0)
    unit(1, 1)
    unit(1, 0)
    for k in (0, 1):
        step[k].wait_recv()

    def summed(zz, n):
        rows = pl.ds(pl.multiple_of(zz * ROWS, 16), ROWS)
        cols = pl.ds(n * BLK, BLK)
        value = ng[0, rows_of(zz, x), share_cols(n)].astype(F32)
        return value + xr[0, rows, cols].astype(F32) + xr[1, rows, cols].astype(F32)

    for n in range(4):
        room(6 * ROWS, ROWS, HALF + n * BLK, BLK)[...] = summed(1 - zl, n).astype(BF)
    over = send(room(6 * ROWS, ROWS), zr, p_s.at[5], p_r.at[5], zpair)
    unit(3, 0)
    over.wait_recv()
    for n in range(4):
        cols = pl.ds(n * BLK, BLK)
        fin[:, cols] = summed(zl, n) + zr[:, cols].astype(F32)
    dn[:, mine] = fin[pl.ds(pl.multiple_of(c * 24, 8), 24), :]
    last = send(
        fin.at[pl.ds(pl.multiple_of((1 - c) * 24, 8), 24), :], dn.at[:, mine],
        p_s.at[6], p_r.at[6], core,
    )
    own_terms(0, 0, 2)
    last.wait_recv()

    inputs = li_ref[...].astype(F32)
    rms = jnp.sqrt(jnp.mean(inputs * inputs, axis=1, keepdims=True) + 1e-06)
    unit_rows = inputs / rms
    scaled = gain_ref[...] * dn[...]
    inner = jnp.mean(scaled * unit_rows, axis=1, keepdims=True)
    ig_out[...] = ((scaled - unit_rows * inner) / rms).astype(BF)
    total = jnp.sum(dn[...] * unit_rows, axis=0, keepdims=True)
    between = ((0, 2, 3), (0, 3, 4), (1, 0, 2), (1, 2, 4))
    for n, peers in enumerate(([core], xs_dev, zs_dev, ys_dev)):
        gs[n] = total
        cps = [send(gs.at[n], gr.at[n, k], g_sem.at[n, k], g_rec.at[n, k], to) for k, to in enumerate(peers)]
        own_terms(*between[n])
        for k, cp in enumerate(cps):
            cp.wait_recv()
            total = total + gr[n, k]
    gain_out[...] = total
    own_terms(1, 4, 6)

    for half, k in ((0, 0), (0, 1), (1, 1), (1, 2), (1, 0), (0, 2), (0, 3), (1, 3), (1, 4), (1, 5)):
        row, size, a = RANGES[half][k]
        ref = into.at[pl.ds(row, size), :]
        remote(ref, ref, t_s.at[half, k], t_r.at[half, k], core).wait_recv()
        for piece_row in range(row, row + size, 256):
            part = (piece_row, min(256, row + size - piece_row), a)
            emit(part, into[piece_row:piece_row + part[1], :].astype(F32), True)
    for cp in swaps + sent:
        cp.wait_send()


def move_kernel(*refs):
    n = len(refs) // 2
    cps = [
        pltpu.make_async_copy(refs[k], refs[n + k], refs[-1].at[k]) for k in range(n)
    ]
    for cp in cps:
        cp.start()
    for cp in cps:
        cp.wait()


def move_out(*arrays):
    hbm = pl.BlockSpec(memory_space=pl.ANY)
    return pl.pallas_call(
        move_kernel,
        out_shape=[jax.ShapeDtypeStruct(a.shape, a.dtype) for a in arrays],
        in_specs=[pl.BlockSpec(memory_space=pltpu.VMEM)] * len(arrays),
        out_specs=[hbm] * len(arrays),
        scratch_shapes=[pltpu.SemaphoreType.DMA((len(arrays),))],
    )(*arrays)


def backward(layer_input, grad_out, gain, w_gate, w_up, w_down):
    vmem = pl.BlockSpec(memory_space=pltpu.VMEM)
    hbm = pl.BlockSpec(memory_space=pl.ANY)
    dma = pltpu.SemaphoreType.DMA
    v = pltpu.VMEM
    return pl.pallas_call(
        kernel,
        out_shape=[
            jax.ShapeDtypeStruct((CORE_FF, BLK), BF),
            jax.ShapeDtypeStruct((CORE_FF, BLK), BF),
            jax.ShapeDtypeStruct((CORE_FF, BLK), BF),
            jax.ShapeDtypeStruct((24, D), BF),
            jax.ShapeDtypeStruct((1, D), F32),
            jax.ShapeDtypeStruct((PLANE, XW), BF),
        ],
        in_specs=[vmem] * 3 + [hbm] * 3,
        out_specs=[vmem] * 5 + [hbm],
        scratch_shapes=[
            v((2, PLANE, D), BF),
            v((PLANE, XW), BF),
            v((2, 4, PLANE, BLK), BF),
            v((GROUP, CORE_FF), BF),
            v((GROUP, CORE_FF), BF),
            v((CORE_FF, D), BF),
            v((CORE_FF, D), BF),
            v((CORE_FF, D), BF),
            v((2, 24, D), BF),
            v((4, ROWS, 2 * BLK), BF),
            v((XW, BLK), BF),
            v((GROUP, HALF), BF),
            v((2 * ROWS, HALF), BF),
            v((2, 2 * ROWS, HALF), BF),
            v((ROWS, HALF), BF),
            v((ROWS, HALF), F32),
            v((24, D), F32),
            v((4, 1, D), F32),
            v((4, 3, 1, D), F32),
            dma((3,)),
            dma((1,)),
            dma((2,)),
            dma((2,)),
            dma((2, 20)),
            dma((2, 16, 2)),
            dma((2, 16)),
            dma((2, 16)),
            dma((3, 5)),
            dma((3, 5)),
            dma((40,)),
            dma((40,)),
            dma((5, 3)),
            dma((2, 6)),
            dma((2, 6)),
            dma((11,)),
            dma((11,)),
            dma((4, 3)),
            dma((4, 3)),
        ],
        compiler_params=pltpu.CompilerParams(
            collective_id=0, has_side_effects=True, vmem_limit_bytes=63 << 20
        ),
    )(layer_input, grad_out, gain, w_gate, w_up, w_down)


def body(layer_input, gain_vector, w_gate, w_up, w_down, grad_out):
    gain = gain_vector[None, :]
    results = backward(layer_input, grad_out, gain, w_gate.T, w_up.T, w_down)
    gate, up, down, input_gradient, gain_gradient = move_out(*results[:5])
    return input_gradient, gain_gradient[0], gate.T, up.T, down


def solution(mesh):
    return jax.shard_map(
        body,
        mesh=mesh,
        in_specs=(
            P(("dp", "tensor"), None),
            P(),
            P(None, "tensor"),
            P(None, "tensor"),
            P("tensor", None),
            P(("dp", "tensor"), None),
        ),
        out_specs=(
            P(("dp", "tensor"), None),
            P(),
            P("dp", "tensor"),
            P("dp", "tensor"),
            P("tensor", "dp"),
        ),
        check_vma=False,
    )
```

```python
import functools

import jax
import jax.numpy as jnp
from jax import lax
from jax.experimental import pallas as pl
from jax.experimental.pallas import tpu as pltpu
from jax.sharding import PartitionSpec as P

MESH = pl.DeviceIdType.MESH
BF = jnp.bfloat16
F32 = jnp.float32
D = 4096
HALF = 2048
QUART = 1024
ROWS = 48
PLANE = 768
GROUP = 384
BLK = 512
CORE_FF = 924
MAIN = 896
REM = CORE_FF - MAIN
PIECES = ((0, 256), (256, 256), (512, 256), (768, 156))
LAYOUT = (
    ((0, 0, 256, 0), (1, 0, 256, 256), (2, 0, 256, 512)),
    ((0, 0, 256, 768), (1, 0, 256, 1024), (2, 0, 128, 1280), (2, 128, 128, 1408)),
    ((0, 0, 256, 1536), (1, 0, 256, 1792), (2, 0, 256, 2048)),
    ((0, 0, 128, 2304), (1, 0, 128, 2432), (2, 0, 128, 2560)),
)
TAIL = 2688
XW = TAIL + 128
HALF_X = XW // 2
SENDS = (((0, 768, 0),), ((768, 640, 0), (1408, 128, 1)), ((1536, 768, 1),), ((2304, 512, 1),))
RANGES = (
    ((0, 512, 0), (512, 256, 1), (768, 512, 0), (1280, 128, 1)),
    ((1408, 128, 1), (1536, 512, 0), (2048, 256, 1), (2304, 256, 0), (2560, 128, 1), (TAIL, 128, 2)),
)


def coords():
    dp = lax.axis_index("dp")
    t = lax.axis_index("tensor")
    y = dp // 2
    z = (dp % 2) * 2 + (t // 2) % 2
    return t // 4, y, z, t % 2


def device(x, y, z, c):
    x, y, z, c = (x + 4) % 4, (y + 4) % 4, (z + 4) % 4, (c + 2) % 2
    return (y * 2 + z // 2, x * 4 + (z % 2) * 2 + c)


def remote(src, dst, ss, rs, to):
    return pltpu.make_async_remote_copy(
        src_ref=src, dst_ref=dst, send_sem=ss, recv_sem=rs, device_id=to, device_id_type=MESH
    )


def greet(peers):
    barrier = pltpu.get_barrier_semaphore()
    for to in peers:
        pl.semaphore_signal(barrier, inc=1, device_id=to, device_id_type=MESH)
    pl.semaphore_wait(barrier, len(peers))


OFFS = (0, -1, 1, 2)


def slot(i, j):
    return (i % 4) * 4 + (j % 4)


def contract_cols(left, right):
    return lax.dot_general(left, right, (((1,), (1,)), ((), ())), preferred_element_type=F32)


def contract_rows(left, right):
    return lax.dot_general(left, right, (((0,), (0,)), ((), ())), preferred_element_type=F32)


def gather_kernel(
    li_ref, go_ref, gain_ref, wg_hbm, wu_hbm, wd_hbm,
    n_hbm, g_hbm, x_hbm, r_hbm, e_hbm, p_hbm, pc_hbm,
    ng, x_ref, dg_ref, du_ref, p_ref, wg, wu, wd, other, stage,
    w_sem, out_sem, ex_s, ex_r, s_sem, r_sem, c_s, c_r, y_s, y_r, e_s, e_r, p_s, p_r,
):
    x, y, z, c = coords()
    s = 1 - 2 * (z % 2)
    sy = 1 - 2 * (y % 2)
    zh = z // 2
    core = device(x, y, z, 1 - c)
    step = {
        "x": (device(x + 1, y, z, c), device(x - 1, y, z, c)),
        "z": (device(x, y, z + s, c), device(x, y, z - s, c)),
    }
    far = {"x": device(x + 2, y, z, c), "z": device(x, y, z + 2, c)}
    near_y = (device(x, y + sy, z, c), device(x, y - sy, z, c))
    weights = [
        pltpu.make_async_copy(src, dst, w_sem.at[k])
        for k, (src, dst) in enumerate(((wg_hbm, wg), (wu_hbm, wu), (wd_hbm, wd)))
    ]
    greet([core, *step["x"], *step["z"], far["x"], far["z"], *near_y])
    swaps = []
    for a, ref in enumerate((li_ref, go_ref)):
        cp = remote(ref, other.at[a], ex_s.at[a], ex_r.at[a], core)
        cp.start()
        swaps.append(cp)
    for cp in weights:
        cp.start()

    base = pl.multiple_of((z * 4 + x) * ROWS, 16)
    first = c == 0
    n_ref, g_ref = ng.at[0], ng.at[1]
    outs = (n_ref, g_ref)

    swaps[0].wait_recv()
    scale = []
    for ref in (li_ref, other.at[0]):
        rows = ref[...].astype(F32)
        scale.append(jnp.sqrt(jnp.mean(rows * rows, axis=1, keepdims=True) + 1e-06))
    swaps[1].wait_recv()
    for k in range(8):
        cols = pl.ds(k * 512, 512)
        mine = (li_ref[:, cols].astype(F32) / scale[0]) * gain_ref[:, cols]
        theirs = (other[0, :, cols].astype(F32) / scale[1]) * gain_ref[:, cols]
        both = jnp.concatenate(
            [jnp.where(first, mine, theirs), jnp.where(first, theirs, mine)], axis=0
        )
        n_ref[pl.ds(base, ROWS), cols] = both.astype(BF)
        mine = go_ref[:, cols].astype(F32)
        theirs = other[1, :, cols].astype(F32)
        both = jnp.concatenate(
            [jnp.where(first, mine, theirs), jnp.where(first, theirs, mine)], axis=0
        )
        g_ref[pl.ds(base, ROWS), cols] = both.astype(BF)

    lo = pl.multiple_of(c * HALF, 128)
    wide = (pl.ds(lo, HALF), pl.ds(lo, QUART), pl.ds(pl.multiple_of(lo + QUART, 128), QUART))
    theirs = pl.ds(pl.multiple_of((1 - c) * HALF, 128), HALF)

    def place(a, i, j):
        dz, dx = (j, i) if a == 0 else (i, j)
        zz, xx = (z + s * dz + 4) % 4, (x + dx + 4) % 4
        return pl.ds(pl.multiple_of((zz * 4 + xx) * ROWS, 16), ROWS)

    def block(a, i, j, part=0):
        return outs[a].at[place(a, i, j), wide[part]]

    sent = []
    count = [0, 0]

    def push(a, leg, way, i, j, part=0):
        axis = ("x", "z")[(a + leg) % 2]
        to = step[axis][0 if way > 0 else 1]
        at = (i, j)[leg]
        at = at - way if axis == "x" else way - at
        ri, rj = (at, j) if leg == 0 else (i, at)
        ref = block(a, i, j, part)
        k = 1 if part == 2 else 0
        cp = remote(ref, ref, s_sem.at[a, count[a]], r_sem.at[a, slot(ri, rj), k], to)
        count[a] += 1
        cp.start()
        sent.append(cp)

    def arrive(a, i, j):
        for part in (1, 2) if (i, j) == (2, 0) or j == 2 else (0,):
            ref = block(a, i, j, part)
            k = 1 if part == 2 else 0
            remote(ref, ref, s_sem.at[a, 0], r_sem.at[a, slot(i, j), k], core).wait_recv()
        if j == 0:
            if i in (1, -1):
                push(a, 0, -i, i, 0, 1 if i < 0 else 2)
            push(a, 1, 1, i, 0)
            push(a, 1, -1, i, 0)
        elif j in (1, -1):
            push(a, 1, -j, i, j, 1 if j < 0 else 2)
        ref = block(a, i, j)
        k = slot(i, j)
        cp = remote(ref, ref, c_s.at[a, k], c_r.at[a, k], core)
        cp.start()
        sent.append(cp)

    for a in (0, 1):
        for way in (1, -1):
            push(a, 0, way, 0, 0)
            push(a, 1, way, 0, 0)

    def hop(src, dst, k, to):
        cp = remote(src, dst, e_s.at[k], e_r.at[k], to)
        cp.start()
        sent.append(cp)

    def landed(ref, k):
        remote(ref, ref, e_s.at[k], e_r.at[k], core).wait_recv()

    for q, to in enumerate(near_y):
        for k, yy in enumerate((y + (sy if q == 0 else -sy), y + 2)):
            cols = pl.ds(pl.multiple_of(((yy + 4) % 4) * 2 * BLK, 128), 2 * BLK)
            hop(ng.at[c, pl.ds(base, ROWS), cols], stage.at[2 * q + k], 2 * q + k, to)

    stored = []
    tally = [0]

    def store(src, dst):
        cp = pltpu.make_async_copy(src, dst, out_sem.at[tally[0]])
        tally[0] += 1
        cp.start()
        return cp

    def set_cols(which):
        return pl.ds(pl.multiple_of(which * BLK, 128), BLK)

    def extra_z():
        for k in range(4):
            landed(stage.at[k], k)
        mine = e_hbm.at[c, :, z, x]
        local = store(stage.at[:, :, set_cols(zh)], mine)
        hop(stage.at[:, :, set_cols(zh)], mine, 4, step["z"][0])
        hop(stage.at[:, :, set_cols(1 - zh)], mine, 5, step["z"][1])
        hop(stage.at[:, :, set_cols(1 - zh)], mine, 6, far["z"])
        return local

    def extra_x(local):
        local.wait()
        for k, dz in ((4, 1), (5, -1), (6, 2)):
            landed(e_hbm.at[c, :, (z + s * dz + 4) % 4, x], k)
        mine = e_hbm.at[c, :, :, x]
        hop(mine, mine, 7, step["x"][0])
        hop(mine, mine, 8, step["x"][1])
        hop(mine, mine, 10, core)

    def extra_share(k, dx):
        xx = (x + dx + 4) % 4
        ref = e_hbm.at[c, :, :, xx]
        landed(ref, k)
        half = e_hbm.at[c, pl.ds(0 if dx < 0 else 2, 2), :, xx]
        hop(half, half, 9 if dx < 0 else 14, step["x"][0 if dx < 0 else 1])
        hop(ref, ref, k + 4, core)

    def extra_last():
        xx = (x + 2) % 4
        landed(e_hbm.at[c, pl.ds(0, 2), :, xx], 9)
        landed(e_hbm.at[c, pl.ds(2, 2), :, xx], 14)
        ref = e_hbm.at[c, :, :, xx]
        hop(ref, ref, 13, core)

    sizes = (192, 192, GROUP)

    def chunk_rows(k):
        first = (z * 192, (z + s) * 192, (1 - zh) * GROUP)[k]
        return pl.ds(pl.multiple_of(first, 16), sizes[k])

    def chunk_ready(k):
        for dz in ((0,), (1,), (-1, 2))[k]:
            for a in (0, 1):
                for dx in OFFS:
                    i, j = (dx, dz) if a == 0 else (dz, dx)
                    if (i, j) != (0, 0):
                        ref = outs[a].at[place(a, i, j), theirs]
                        at = slot(i, j)
                        remote(ref, ref, c_s.at[a, at], c_r.at[a, at], core).wait_recv()
        rows = chunk_rows(k)
        stored.append(store(n_ref.at[rows, :], n_hbm.at[rows, :]))
        stored.append(store(g_ref.at[rows, :], g_hbm.at[rows, :]))

    def piece(k, p):
        f, w = PIECES[p]
        rows = chunk_rows(k)
        normed = n_ref[rows, :]
        gate = contract_cols(normed, wg[f:f + w, :])
        up = contract_cols(normed, wu[f:f + w, :])
        d_hidden = contract_cols(g_ref[rows, :], wd[f:f + w, :])
        sigma = jax.nn.sigmoid(gate)
        silu = gate * sigma
        hidden = (silu * up).astype(BF)
        d_gate = (d_hidden * up * sigma * (1.0 + gate * (1.0 - sigma))).astype(BF)
        d_up = (d_hidden * silu).astype(BF)
        if k < 2:
            own = pl.ds(pl.multiple_of((z % 2 if k == 0 else 1 - z % 2) * 192, 16), 192)
            dg_ref[own, f:f + w] = d_gate
            du_ref[own, f:f + w] = d_up
        values = (d_gate, d_up, hidden)
        for q, first, count, col in LAYOUT[p]:
            x_ref[rows, col:col + count] = values[q][:, first:first + count]
        if w < 256:
            gap = jnp.zeros((sizes[k], 32 - REM), BF)
            rest = []
            for value in values:
                rest += [value[:, w - REM:], gap]
            rest.append(jnp.zeros((sizes[k], 32), BF))
            x_ref[rows, TAIL:] = jnp.concatenate(rest, axis=1)
        for n, (col, count, to) in enumerate(SENDS[p]):
            view = (rows, pl.ds(col, count))
            at = p + 3 * n
            cp = remote(x_ref.at[view], r_hbm.at[view], y_s.at[k, at], y_r.at[k, at], near_y[to])
            cp.start()
            sent.append(cp)
        if p == 3:
            stored.append(store(x_ref.at[rows, :], x_hbm.at[rows, :]))

    def moves(*items):
        for item in items:
            arrive(*item)

    moves((0, -1, 0), (1, 0, -1), (0, 1, 0), (1, 0, 1))
    moves((1, 1, 0), (0, 0, 1), (1, -1, 0), (0, 0, -1))
    moves((0, 2, 0), (1, 0, 2))
    for cp in weights:
        cp.wait()
    chunk_ready(0)
    local = extra_z()
    piece(0, 0)
    moves((0, -1, 1), (1, 1, -1), (0, 1, 1), (1, 1, 1))
    piece(0, 2)
    moves((0, -1, -1), (1, -1, -1), (0, 1, -1), (1, -1, 1))
    piece(0, 1)
    moves((0, 2, 1), (1, 1, 2))
    piece(0, 3)
    moves((1, 2, 0), (0, 0, 2), (1, -1, 2), (0, 2, -1))
    chunk_ready(1)
    extra_x(local)
    piece(1, 0)
    moves((0, -1, 2), (0, 1, 2), (1, 2, -1), (1, 2, 1))
    piece(1, 2)
    piece(1, 1)
    moves((0, 2, 2), (1, 2, 2))
    piece(1, 3)
    chunk_ready(2)
    for p in (0, 2, 1, 3):
        piece(2, p)
    extra_share(7, -1)
    extra_share(8, 1)

    swap = None
    for which in (1, 0):
        for k in range(4):
            lo = (c if which == 0 else 1 - c) * HALF + k * BLK
            cols = pl.ds(pl.multiple_of(lo, 128), BLK)
            value = jnp.dot(dg_ref[...], wg[:, cols], preferred_element_type=F32)
            value = value + jnp.dot(du_ref[...], wu[:, cols], preferred_element_type=F32)
            p_ref[which, :, k * BLK:(k + 1) * BLK] = value.astype(BF)
        if which:
            swap = remote(p_ref.at[1], pc_hbm, p_s.at[0], p_r.at[0], core)
            swap.start()
            extra_last()
    stored.append(store(p_ref.at[0], p_hbm))
    for k, dx in ((10, 0), (11, -1), (12, 1), (13, 2)):
        landed(e_hbm.at[1 - c, :, :, (x + dx + 4) % 4], k)
    swap.wait()
    for k in range(3):
        rows = chunk_rows(k)
        for p in range(4):
            for n, (col, count, _) in enumerate(SENDS[p]):
                ref = r_hbm.at[rows, pl.ds(col, count)]
                at = p + 3 * n
                remote(ref, ref, y_s.at[k, at], y_r.at[k, at], core).wait_recv()
    for cp in swaps + sent:
        cp.wait_send()
    for cp in stored:
        cp.wait()


def gather(layer_input, grad_out, gain, w_gate, w_up, w_down):
    vmem = pl.BlockSpec(memory_space=pltpu.VMEM)
    hbm = pl.BlockSpec(memory_space=pl.ANY)
    dma = pltpu.SemaphoreType.DMA
    v = pltpu.VMEM
    return pl.pallas_call(
        gather_kernel,
        out_shape=[
            jax.ShapeDtypeStruct((PLANE, D), BF),
            jax.ShapeDtypeStruct((PLANE, D), BF),
            jax.ShapeDtypeStruct((PLANE, XW), BF),
            jax.ShapeDtypeStruct((PLANE, XW), BF),
            jax.ShapeDtypeStruct((2, 4, 4, 4, ROWS, BLK), BF),
            jax.ShapeDtypeStruct((GROUP, HALF), BF),
            jax.ShapeDtypeStruct((GROUP, HALF), BF),
        ],
        in_specs=[vmem] * 3 + [hbm] * 3,
        out_specs=[hbm] * 7,
        scratch_shapes=[
            v((2, PLANE, D), BF),
            v((PLANE, XW), BF),
            v((GROUP, CORE_FF), BF),
            v((GROUP, CORE_FF), BF),
            v((2, GROUP, HALF), BF),
            v((CORE_FF, D), BF),
            v((CORE_FF, D), BF),
            v((CORE_FF, D), BF),
            v((2, 24, D), BF),
            v((4, ROWS, 2 * BLK), BF),
            dma((3,)),
            dma((14,)),
            dma((2,)),
            dma((2,)),
            dma((2, 20)),
            dma((2, 16, 2)),
            dma((2, 16)),
            dma((2, 16)),
            dma((3, 5)),
            dma((3, 5)),
            dma((15,)),
            dma((15,)),
            dma((1,)),
            dma((1,)),
        ],
        compiler_params=pltpu.CompilerParams(
            collective_id=0, has_side_effects=True, vmem_limit_bytes=60 << 20
        ),
    )(layer_input, grad_out, gain, w_gate, w_up, w_down)


def reduce_kernel(
    n_hbm, g_hbm, e_hbm, own_hbm, near_hbm, p_ref, pc_ref, li_ref, gain_ref,
    gate_out, up_out, down_out, ig_out, gain_out,
    nb, eb, own_x, near_x, outgo, into, own,
    q, xo, xi, xs, xr, zs, zr, dn, gs, gr,
    load, t_s, t_r, p_s, p_r, g_sem, g_rec,
):
    x, y, z, c = coords()
    zl, zh = z % 2, z // 2
    sy = 1 - 2 * (y % 2)
    core = device(x, y, z, 1 - c)
    xs_dev = [device(x + k, y, z, c) for k in (1, -1, 2)]
    ys_dev = [device(x, y + k, z, c) for k in (1, -1, 2)]
    zs_dev = [device(x, y, z + k, c) for k in (1, -1, 2)]
    zpair = device(x, y, zh * 2 + 1 - zl, c)
    alpha, beta = device(x, y + sy, z, c), device(x, y - sy, z, c)

    loads = {}

    def fetch(b):
        yy = (y + (0, sy, -sy)[b] + 4) % 4
        cols = pl.ds(pl.multiple_of((yy * 2 + zh) * BLK, 128), BLK)
        loads["n", b] = [
            pltpu.make_async_copy(n_hbm.at[:, cols], nb.at[0, b], load.at[0, b]),
            pltpu.make_async_copy(g_hbm.at[:, cols], nb.at[1, b], load.at[1, b]),
        ]
        for cp in loads["n", b]:
            cp.start()

    def fetch_extra(b):
        loads["e", b] = [
            pltpu.make_async_copy(e_hbm.at[a, b], eb.at[a, b], load.at[a, 3 + b]) for a in (0, 1)
        ]
        for cp in loads["e", b]:
            cp.start()

    def fetch_terms(n):
        cols = pl.ds(*((0, 768), (1408, 896), (768, 640), (2304, 512))[n])
        loads["x", n] = [
            pltpu.make_async_copy(own_hbm.at[:, cols], own_x.at[:, cols], load.at[0, 7 + n]),
            pltpu.make_async_copy(near_hbm.at[:, cols], near_x.at[:, cols], load.at[1, 7 + n]),
        ]
        for cp in loads["x", n]:
            cp.start()

    fetch(2)
    fetch_extra(1)
    fetch_terms(0)
    fetch(1)
    fetch_extra(3)
    fetch_terms(1)
    fetch_terms(2)
    fetch_terms(3)
    fetch(0)
    fetch_extra(0)
    fetch_extra(2)

    def ready(*keys):
        for key in keys:
            for cp in loads[key]:
                cp.wait()

    greet([core, *xs_dev, *ys_dev, *zs_dev])
    sent = []

    def send(src, dst, ss, rs, to):
        cp = remote(src, dst, ss, rs, to)
        cp.start()
        sent.append(cp)
        return cp

    mine = pl.ds(pl.multiple_of(c * HALF, 128), HALF)
    q[...] = p_ref[...].astype(F32) + pc_ref[...].astype(F32)

    def rows_of(zz, xx):
        return pl.ds(pl.multiple_of((zz * 4 + (xx + 4) % 4) * ROWS, 16), ROWS)

    for zz in (0, 1):
        xo[zz * ROWS:(zz + 1) * ROWS, :] = q[rows_of(zz, x + 2), :].astype(BF)
    far = [
        send(
            xo.at[:, pl.ds(k * QUART, QUART)], xi.at[:, pl.ds(k * QUART, QUART)],
            p_s.at[1 + k], p_r.at[1 + k], xs_dev[k],
        )
        for k in (0, 1)
    ]

    def term(rng, b, e):
        row, size, a = rng

        def product(a):
            cols = slice(row, row + size)
            value = contract_rows(own_x[:, cols], nb[a, b])
            return value + contract_rows(near_x[:, cols], eb[a, e])

        if a < 2:
            return product(a)
        return jnp.concatenate([product(0)[:64], product(1)[64:]], axis=0)

    needs = {
        (0, 0): (("n", 2), ("e", 1), ("x", 0)),
        (1, 0): (("n", 1), ("e", 3), ("x", 1)),
        (0, 2): (("x", 2),),
        (1, 3): (("x", 3),),
    }
    for k in range(6):
        for half, (b, e, to) in enumerate(((2, 1, beta), (1, 3, alpha))):
            if k < len(RANGES[half]):
                ready(*needs.get((half, k), ()))
                row, size, _ = RANGES[half][k]
                rows = pl.ds(row, size)
                outgo[rows, :] = term(RANGES[half][k], b, e).astype(BF)
                send(outgo.at[rows, :], into.at[rows, :], t_s.at[half, k], t_r.at[half, k], to)

    def own_terms(half):
        for rng in RANGES[half]:
            own[rng[0]:rng[0] + rng[1], :] = term(rng, 0, 2 * half)

    step = []
    for k in (0, 1):
        far[k].wait_recv()
        for zz in (0, 1):
            rows = pl.ds(zz * ROWS, ROWS)
            src = rows_of(zz, x + (1 if k == 0 else -1))
            for half in (0, 1):
                cols = pl.ds(half * QUART, QUART)
                value = q[src, cols]
                if half == k:
                    value = value + xi[rows, cols].astype(F32)
                xs[k, rows, cols] = value.astype(BF)
        step.append(send(xs.at[k], xr.at[k], p_s.at[3 + k], p_r.at[3 + k], xs_dev[k]))
    ready(("n", 0), ("e", 0), ("e", 2))
    own_terms(0)
    for k in (0, 1):
        step[k].wait_recv()

    def summed(zz):
        rows = pl.ds(pl.multiple_of(zz * ROWS, 16), ROWS)
        return q[rows_of(zz, x), :] + xr[0, rows, :].astype(F32) + xr[1, rows, :].astype(F32)

    zs[...] = summed(1 - zl).astype(BF)
    hop = send(zs, zr, p_s.at[5], p_r.at[5], zpair)
    own_terms(1)
    hop.wait_recv()
    q[0:ROWS, :] = summed(zl) + zr[...].astype(F32)
    dn[:, mine] = q[pl.ds(pl.multiple_of(c * 24, 8), 24), :]
    last = send(
        q.at[pl.ds(pl.multiple_of((1 - c) * 24, 8), 24), :], dn.at[:, mine],
        p_s.at[6], p_r.at[6], core,
    )
    last.wait_recv()

    inputs = li_ref[...].astype(F32)
    rms = jnp.sqrt(jnp.mean(inputs * inputs, axis=1, keepdims=True) + 1e-06)
    unit = inputs / rms
    scaled = gain_ref[...] * dn[...]
    inner = jnp.mean(scaled * unit, axis=1, keepdims=True)
    ig_out[...] = ((scaled - unit * inner) / rms).astype(BF)
    total = jnp.sum(dn[...] * unit, axis=0, keepdims=True)
    for s, peers in enumerate(([core], xs_dev, zs_dev, ys_dev)):
        gs[s] = total
        cps = []
        for k, to in enumerate(peers):
            cps.append(send(gs.at[s], gr.at[s, k], g_sem.at[s, k], g_rec.at[s, k], to))
        for k, cp in enumerate(cps):
            cp.wait_recv()
            total = total + gr[s, k]
    gain_out[...] = total

    outs = (gate_out, up_out, down_out)
    for k in range(6):
        for half in (0, 1):
            if k >= len(RANGES[half]):
                continue
            row, size, _ = RANGES[half][k]
            rows = pl.ds(row, size)
            ref = into.at[rows, :]
            remote(ref, ref, t_s.at[half, k], t_r.at[half, k], core).wait_recv()
            value = own[rows, :] + ref[...].astype(F32)
            if row == TAIL:
                for which in range(3):
                    rest = value[32 * which:32 * which + REM]
                    outs[which][MAIN:, :] = rest.astype(BF)
                continue
            for (unit, _), items in zip(PIECES, LAYOUT):
                for which, first, count, col in items:
                    if row <= col < row + size:
                        at = unit + first
                        outs[which][at:at + count, :] = value[col - row:col - row + count].astype(BF)
    for cp in sent:
        cp.wait_send()


def reduce(n, g, e, own_x, near_x, p, pc, layer_input, gain):
    vmem = pl.BlockSpec(memory_space=pltpu.VMEM)
    hbm = pl.BlockSpec(memory_space=pl.ANY)
    dma = pltpu.SemaphoreType.DMA
    v = pltpu.VMEM
    return pl.pallas_call(
        reduce_kernel,
        out_shape=[
            jax.ShapeDtypeStruct((CORE_FF, BLK), BF),
            jax.ShapeDtypeStruct((CORE_FF, BLK), BF),
            jax.ShapeDtypeStruct((CORE_FF, BLK), BF),
            jax.ShapeDtypeStruct((24, D), BF),
            jax.ShapeDtypeStruct((1, D), F32),
        ],
        in_specs=[hbm] * 5 + [vmem] * 4,
        out_specs=[vmem] * 5,
        scratch_shapes=[
            v((2, 3, PLANE, BLK), BF),
            v((2, 4, PLANE, BLK), BF),
            v((PLANE, XW), BF),
            v((PLANE, XW), BF),
            v((XW, BLK), BF),
            v((XW, BLK), BF),
            v((XW, BLK), F32),
            v((GROUP, HALF), F32),
            v((2 * ROWS, HALF), BF),
            v((2 * ROWS, HALF), BF),
            v((2, 2 * ROWS, HALF), BF),
            v((2, 2 * ROWS, HALF), BF),
            v((ROWS, HALF), BF),
            v((ROWS, HALF), BF),
            v((24, D), F32),
            v((4, 1, D), F32),
            v((4, 3, 1, D), F32),
            dma((2, 11)),
            dma((2, 6)),
            dma((2, 6)),
            dma((7,)),
            dma((7,)),
            dma((4, 3)),
            dma((4, 3)),
        ],
        compiler_params=pltpu.CompilerParams(
            collective_id=1, has_side_effects=True, vmem_limit_bytes=60 << 20
        ),
    )(n, g, e, own_x, near_x, p, pc, layer_input, gain)


def move_kernel(*refs):
    n = len(refs) // 2
    cps = [
        pltpu.make_async_copy(refs[k], refs[n + k], refs[-1].at[k]) for k in range(n)
    ]
    for cp in cps:
        cp.start()
    for cp in cps:
        cp.wait()


def move_out(*arrays):
    hbm = pl.BlockSpec(memory_space=pl.ANY)
    return pl.pallas_call(
        move_kernel,
        out_shape=[jax.ShapeDtypeStruct(a.shape, a.dtype) for a in arrays],
        in_specs=[pl.BlockSpec(memory_space=pltpu.VMEM)] * len(arrays),
        out_specs=[hbm] * len(arrays),
        scratch_shapes=[pltpu.SemaphoreType.DMA((len(arrays),))],
    )(*arrays)


def body(layer_input, gain_vector, w_gate, w_up, w_down, grad_out):
    gain = gain_vector[None, :]
    normed, upstream, own_x, near_x, extra, share, core_share = gather(
        layer_input, grad_out, gain, w_gate.T, w_up.T, w_down
    )
    results = reduce(
        normed, upstream, extra.reshape(2, 4, PLANE, BLK), own_x, near_x, share, core_share,
        layer_input, gain,
    )
    gate, up, down, input_gradient, gain_gradient = move_out(*results)
    return input_gradient, gain_gradient[0], gate.T, up.T, down


def solution(mesh):
    return jax.shard_map(
        body,
        mesh=mesh,
        in_specs=(
            P(("dp", "tensor"), None),
            P(),
            P(None, "tensor"),
            P(None, "tensor"),
            P("tensor", None),
            P(("dp", "tensor"), None),
        ),
        out_specs=(
            P(("dp", "tensor"), None),
            P(),
            P("dp", "tensor"),
            P("dp", "tensor"),
            P("tensor", "dp"),
        ),
        check_vma=False,
    )
```

```python
import functools

import jax
import jax.numpy as jnp
from jax import lax
from jax.experimental import pallas as pl
from jax.experimental.pallas import tpu as pltpu
from jax.sharding import PartitionSpec as P

MESH = pl.DeviceIdType.MESH
BF = jnp.bfloat16
F32 = jnp.float32
D = 4096
HALF = 2048
QUART = 1024
ROWS = 48
PLANE = 768
GROUP = 384
BLK = 512
CORE_FF = 924
MAIN = 896
REM = CORE_FF - MAIN
PIECES = ((0, 256), (256, 256), (512, 256), (768, 156))
LAYOUT = (
    ((0, 0, 256, 0), (1, 0, 256, 256), (2, 0, 256, 512)),
    ((0, 0, 256, 768), (1, 0, 256, 1024), (2, 0, 128, 1280), (2, 128, 128, 1408)),
    ((0, 0, 256, 1536), (1, 0, 256, 1792), (2, 0, 256, 2048)),
    ((0, 0, 128, 2304), (1, 0, 128, 2432), (2, 0, 128, 2560)),
)
TAIL = 2688
XW = TAIL + 128
HALF_X = XW // 2
SENDS = (((0, 768, 0),), ((768, 640, 0), (1408, 128, 1)), ((1536, 768, 1),), ((2304, 512, 1),))
ROOM = (
    ((0, 0), (512, 0), (0, 1), (512, 1)),
    ((640, 1), (0, 2), (512, 2), (0, 3), (256, 3), (384, 3)),
)
RANGES = (
    ((0, 512, 0), (512, 256, 1), (768, 512, 0), (1280, 128, 1)),
    ((1408, 128, 1), (1536, 512, 0), (2048, 256, 1), (2304, 256, 0), (2560, 128, 1), (TAIL, 128, 2)),
)


def coords():
    dp = lax.axis_index("dp")
    t = lax.axis_index("tensor")
    y = dp // 2
    z = (dp % 2) * 2 + (t // 2) % 2
    return t // 4, y, z, t % 2


def device(x, y, z, c):
    x, y, z, c = (x + 4) % 4, (y + 4) % 4, (z + 4) % 4, (c + 2) % 2
    return (y * 2 + z // 2, x * 4 + (z % 2) * 2 + c)


def remote(src, dst, ss, rs, to):
    return pltpu.make_async_remote_copy(
        src_ref=src, dst_ref=dst, send_sem=ss, recv_sem=rs, device_id=to, device_id_type=MESH
    )


def greet(peers):
    barrier = pltpu.get_barrier_semaphore()
    for to in peers:
        pl.semaphore_signal(barrier, inc=1, device_id=to, device_id_type=MESH)
    pl.semaphore_wait(barrier, len(peers))


OFFS = (0, -1, 1, 2)


def slot(i, j):
    return (i % 4) * 4 + (j % 4)


def contract_cols(left, right):
    return lax.dot_general(left, right, (((1,), (1,)), ((), ())), preferred_element_type=F32)


def contract_rows(left, right):
    return lax.dot_general(left, right, (((0,), (0,)), ((), ())), preferred_element_type=F32)


def kernel(
    li_ref, go_ref, gain_ref, wg_hbm, wu_hbm, wd_hbm,
    gate_out, up_out, down_out, ig_out, gain_out, r_hbm,
    ng, x_ref, e_ref, dg_ref, du_ref, wg, wu, wd, other, stage,
    into, pc, xi, xr, zr, fin, dn, gs, gr,
    w_sem, out_sem, ex_s, ex_r, s_sem, r_sem, c_s, c_r, y_s, y_r, e_s, e_r,
    load, t_s, t_r, p_s, p_r, g_sem, g_rec,
):
    x, y, z, c = coords()
    s = 1 - 2 * (z % 2)
    sy = 1 - 2 * (y % 2)
    zl, zh = z % 2, z // 2
    core = device(x, y, z, 1 - c)
    xs_dev = [device(x + k, y, z, c) for k in (1, -1, 2)]
    ys_dev = [device(x, y + sy * k, z, c) for k in (1, -1, 2)]
    zs_dev = [device(x, y, z + s * k, c) for k in (1, -1, 2)]
    step = {"x": xs_dev[:2], "z": zs_dev[:2]}
    near_y = ys_dev[:2]
    zpair = zs_dev[0]
    weights = [
        pltpu.make_async_copy(src, dst, w_sem.at[k])
        for k, (src, dst) in enumerate(((wg_hbm, wg), (wu_hbm, wu), (wd_hbm, wd)))
    ]
    greet([core, *xs_dev, *ys_dev, *zs_dev])
    swaps = []
    for a, ref in enumerate((li_ref, go_ref)):
        cp = remote(ref, other.at[a], ex_s.at[a], ex_r.at[a], core)
        cp.start()
        swaps.append(cp)
    for cp in weights:
        cp.start()

    base = pl.multiple_of((z * 4 + x) * ROWS, 16)
    first = c == 0
    n_ref, g_ref = ng.at[0], ng.at[1]
    outs = (n_ref, g_ref)

    swaps[0].wait_recv()
    scale = []
    for ref in (li_ref, other.at[0]):
        rows = ref[...].astype(F32)
        scale.append(jnp.sqrt(jnp.mean(rows * rows, axis=1, keepdims=True) + 1e-06))
    swaps[1].wait_recv()
    for k in range(8):
        cols = pl.ds(k * 512, 512)
        mine = (li_ref[:, cols].astype(F32) / scale[0]) * gain_ref[:, cols]
        theirs = (other[0, :, cols].astype(F32) / scale[1]) * gain_ref[:, cols]
        both = jnp.concatenate(
            [jnp.where(first, mine, theirs), jnp.where(first, theirs, mine)], axis=0
        )
        n_ref[pl.ds(base, ROWS), cols] = both.astype(BF)
        mine = go_ref[:, cols].astype(F32)
        theirs = other[1, :, cols].astype(F32)
        both = jnp.concatenate(
            [jnp.where(first, mine, theirs), jnp.where(first, theirs, mine)], axis=0
        )
        g_ref[pl.ds(base, ROWS), cols] = both.astype(BF)

    lo = pl.multiple_of(c * HALF, 128)
    wide = (pl.ds(lo, HALF), pl.ds(lo, QUART), pl.ds(pl.multiple_of(lo + QUART, 128), QUART))
    theirs = pl.ds(pl.multiple_of((1 - c) * HALF, 128), HALF)

    def place(a, i, j):
        dz, dx = (j, i) if a == 0 else (i, j)
        zz, xx = (z + s * dz + 4) % 4, (x + dx + 4) % 4
        return pl.ds(pl.multiple_of((zz * 4 + xx) * ROWS, 16), ROWS)

    def block(a, i, j, part=0):
        return outs[a].at[place(a, i, j), wide[part]]

    sent, sent_ng = [], []
    count = [0, 0]

    def push(a, leg, way, i, j, part=0):
        axis = ("x", "z")[(a + leg) % 2]
        to = step[axis][0 if way > 0 else 1]
        at = (i, j)[leg]
        at = at - way if axis == "x" else way - at
        ri, rj = (at, j) if leg == 0 else (i, at)
        ref = block(a, i, j, part)
        k = 1 if part == 2 else 0
        cp = remote(ref, ref, s_sem.at[a, count[a]], r_sem.at[a, slot(ri, rj), k], to)
        count[a] += 1
        cp.start()
        sent_ng.append(cp)

    def arrive(a, i, j):
        for part in (1, 2) if (i, j) == (2, 0) or j == 2 else (0,):
            ref = block(a, i, j, part)
            k = 1 if part == 2 else 0
            remote(ref, ref, s_sem.at[a, 0], r_sem.at[a, slot(i, j), k], core).wait_recv()
        if j == 0:
            if i in (1, -1):
                push(a, 0, -i, i, 0, 1 if i < 0 else 2)
            push(a, 1, 1, i, 0)
            push(a, 1, -1, i, 0)
        elif j in (1, -1):
            push(a, 1, -j, i, j, 1 if j < 0 else 2)
        ref = block(a, i, j)
        k = slot(i, j)
        cp = remote(ref, ref, c_s.at[a, k], c_r.at[a, k], core)
        cp.start()
        sent_ng.append(cp)

    for a in (0, 1):
        for way in (1, -1):
            push(a, 0, way, 0, 0)
            push(a, 1, way, 0, 0)

    def hop(src, dst, k, to, kept=sent):
        cp = remote(src, dst, e_s.at[k], e_r.at[k], to)
        cp.start()
        kept.append(cp)

    def landed(ref, k):
        remote(ref, ref, e_s.at[k], e_r.at[k], core).wait_recv()

    for q, to in enumerate(near_y):
        for k, yy in enumerate((y + (sy if q == 0 else -sy), y + 2)):
            cols = pl.ds(pl.multiple_of(((yy + 4) % 4) * 2 * BLK, 128), 2 * BLK)
            hop(ng.at[c, pl.ds(base, ROWS), cols], stage.at[2 * q + k], 2 * q + k, to, sent_ng)

    tally = [0]

    def store(src, dst):
        cp = pltpu.make_async_copy(src, dst, out_sem.at[tally[0]])
        tally[0] += 1
        cp.start()
        return cp

    def set_cols(which):
        return pl.ds(pl.multiple_of(which * BLK, 128), BLK)

    def place_e(zz, xx):
        return pl.ds(pl.multiple_of((((zz + 4) % 4) * 4 + (xx + 4) % 4) * ROWS, 16), ROWS)

    def extra_z():
        for k in range(4):
            landed(stage.at[k], k)
        mine = e_ref.at[c, :, place_e(z, x), :]
        local = store(stage.at[:, :, set_cols(zh)], mine)
        hop(stage.at[:, :, set_cols(zh)], mine, 4, zs_dev[0])
        hop(stage.at[:, :, set_cols(1 - zh)], mine, 5, zs_dev[1])
        hop(stage.at[:, :, set_cols(1 - zh)], mine, 6, zs_dev[2])
        return local

    def extra_x(local):
        local.wait()
        for k, dz in ((4, 1), (5, -1), (6, 2)):
            landed(e_ref.at[c, :, place_e(z + s * dz, x), :], k)
        for zz in range(4):
            mine = e_ref.at[c, :, place_e(zz, x), :]
            hop(mine, mine, 8 + zz, xs_dev[0])
            hop(mine, mine, 12 + zz, xs_dev[1])
            hop(mine, mine, 16 + zz, core)

    def extra_share(k, dx):
        for zz in range(4):
            rows = place_e(zz, x + dx)
            ref = e_ref.at[c, :, rows, :]
            landed(ref, k + zz)
            half = e_ref.at[c, pl.ds(0 if dx < 0 else 2, 2), rows, :]
            hop(half, half, (20 if dx < 0 else 24) + zz, xs_dev[0 if dx < 0 else 1])
            hop(ref, ref, (28 if dx < 0 else 32) + zz, core)

    def extra_last():
        for zz in range(4):
            rows = place_e(zz, x + 2)
            landed(e_ref.at[c, pl.ds(0, 2), rows, :], 20 + zz)
            landed(e_ref.at[c, pl.ds(2, 2), rows, :], 24 + zz)
            ref = e_ref.at[c, :, rows, :]
            hop(ref, ref, 36 + zz, core)

    def extra_done():
        for k, dx in ((16, 0), (28, -1), (32, 1), (36, 2)):
            for zz in range(4):
                landed(e_ref.at[1 - c, :, place_e(zz, x + dx), :], k + zz)

    sizes = (192, 192, GROUP)

    def chunk_rows(k):
        first = (z * 192, (z + s) * 192, (1 - zh) * GROUP)[k]
        return pl.ds(pl.multiple_of(first, 16), sizes[k])

    def chunk_ready(k):
        for dz in ((0,), (1,), (-1, 2))[k]:
            for a in (0, 1):
                for dx in OFFS:
                    i, j = (dx, dz) if a == 0 else (dz, dx)
                    if (i, j) != (0, 0):
                        ref = outs[a].at[place(a, i, j), theirs]
                        at = slot(i, j)
                        remote(ref, ref, c_s.at[a, at], c_r.at[a, at], core).wait_recv()

    def piece(k, p):
        f, w = PIECES[p]
        rows = chunk_rows(k)
        normed = n_ref[rows, :]
        gate = contract_cols(normed, wg[f:f + w, :])
        up = contract_cols(normed, wu[f:f + w, :])
        d_hidden = contract_cols(g_ref[rows, :], wd[f:f + w, :])
        sigma = jax.nn.sigmoid(gate)
        silu = gate * sigma
        hidden = (silu * up).astype(BF)
        d_gate = (d_hidden * up * sigma * (1.0 + gate * (1.0 - sigma))).astype(BF)
        d_up = (d_hidden * silu).astype(BF)
        if k < 2:
            own = pl.ds(pl.multiple_of((z % 2 if k == 0 else 1 - z % 2) * 192, 16), 192)
            dg_ref[own, f:f + w] = d_gate
            du_ref[own, f:f + w] = d_up
        values = (d_gate, d_up, hidden)
        for q, first, count, col in LAYOUT[p]:
            x_ref[rows, col:col + count] = values[q][:, first:first + count]
        if w < 256:
            gap = jnp.zeros((sizes[k], 32 - REM), BF)
            rest = []
            for value in values:
                rest += [value[:, w - REM:], gap]
            rest.append(jnp.zeros((sizes[k], 32), BF))
            x_ref[rows, TAIL:] = jnp.concatenate(rest, axis=1)
        for n, (col, count, to) in enumerate(SENDS[p]):
            view = (rows, pl.ds(col, count))
            at = p + 3 * n
            cp = remote(x_ref.at[view], r_hbm.at[view], y_s.at[k, at], y_r.at[k, at], near_y[to])
            cp.start()
            sent.append(cp)

    def moves(*items):
        for item in items:
            arrive(*item)

    moves((0, -1, 0), (1, 0, -1), (0, 1, 0), (1, 0, 1))
    moves((1, 1, 0), (0, 0, 1), (1, -1, 0), (0, 0, -1))
    moves((0, 2, 0), (1, 0, 2))
    for cp in weights:
        cp.wait()
    chunk_ready(0)
    piece(0, 0)
    moves((0, -1, 1), (1, 1, -1), (0, 1, 1), (1, 1, 1))
    piece(0, 2)
    moves((0, -1, -1), (1, -1, -1), (0, 1, -1), (1, -1, 1))
    piece(0, 1)
    moves((0, 2, 1), (1, 1, 2))
    local = extra_z()
    piece(0, 3)
    moves((1, 2, 0), (0, 0, 2), (1, -1, 2), (0, 2, -1))
    chunk_ready(1)
    piece(1, 0)
    moves((0, -1, 2), (0, 1, 2), (1, 2, -1), (1, 2, 1))
    extra_x(local)
    piece(1, 2)
    piece(1, 1)
    moves((0, 2, 2), (1, 2, 2))
    piece(1, 3)
    chunk_ready(2)
    piece(2, 0)
    piece(2, 2)
    extra_share(8, -1)
    extra_share(12, 1)
    piece(2, 1)
    piece(2, 3)

    def share_cols(k):
        return pl.ds(pl.multiple_of((2 * k + 1 - zh) * BLK, 128), BLK)

    def share(which):
        for k in range(4):
            lo = (c if which == 0 else 1 - c) * HALF + k * BLK
            cols = pl.ds(pl.multiple_of(lo, 128), BLK)
            value = jnp.dot(dg_ref[...], wg[:, cols], preferred_element_type=F32)
            value = value + jnp.dot(du_ref[...], wu[:, cols], preferred_element_type=F32)
            ng[which, 0:GROUP, share_cols(k)] = value.astype(BF)

    def send(src, dst, ss, rs, to):
        cp = remote(src, dst, ss, rs, to)
        cp.start()
        sent.append(cp)
        return cp

    for cp in sent_ng:
        cp.wait_send()
    fetched = {}

    def fetch(p, n, k):
        col, count, _ = SENDS[p][n]
        rows, cols, at = chunk_rows(k), pl.ds(col, count), p + 3 * n
        ref = r_hbm.at[rows, cols]
        remote(ref, ref, y_s.at[k, at], y_r.at[k, at], core).wait_recv()
        cp = pltpu.make_async_copy(ref, wd.at[rows, cols], load.at[at, k])
        cp.start()
        fetched[p, n, k] = cp

    share(1)
    swap = [
        send(
            ng.at[1, pl.ds(0, GROUP), share_cols(k)], pc.at[:, pl.ds(k * BLK, BLK)],
            p_s.at[7 + k], p_r.at[7 + k], core,
        )
        for k in range(4)
    ]
    extra_last()
    share(0)

    mine = pl.ds(pl.multiple_of(c * HALF, 128), HALF)
    for k in range(4):
        swap[k].wait_recv()
        value = ng[0, 0:GROUP, share_cols(k)].astype(F32)
        value = value + pc[:, k * BLK:(k + 1) * BLK].astype(F32)
        ng[0, 0:GROUP, share_cols(k)] = value.astype(BF)

    def rows_of(zz, xx):
        return pl.ds(pl.multiple_of((zz * 4 + (xx + 4) % 4) * ROWS, 16), ROWS)

    def room(row, rows, col=HALF, cols=HALF):
        return wg.at[pl.ds(row, rows), pl.ds(col, cols)]

    for zz in (0, 1):
        for k in range(4):
            value = ng[0, rows_of(zz, x + 2), share_cols(k)]
            room(zz * ROWS, ROWS, HALF + k * BLK, BLK)[...] = value
    far = [
        send(
            room(0, 2 * ROWS, HALF + k * QUART, QUART), xi.at[:, pl.ds(k * QUART, QUART)],
            p_s.at[1 + k], p_r.at[1 + k], xs_dev[k],
        )
        for k in (0, 1)
    ]

    for p, n in ((0, 0), (2, 0), (1, 0), (1, 1), (3, 0)):
        fetch(p, n, 0)
        fetch(p, n, 1)
    extra_done()

    def block_cols(b):
        yy = (y + (0, sy, -sy)[b] + 4) % 4
        return pl.ds(pl.multiple_of((yy * 2 + zh) * BLK, 128), BLK)

    def term(rng, b, e):
        row, size, a = rng

        def product(a):
            cols = slice(row, row + size)
            value = contract_rows(x_ref[:, cols], ng[a, :, block_cols(b)])
            return value + contract_rows(wd[0:PLANE, cols], e_ref[a, e])

        if a < 2:
            return product(a)
        return jnp.concatenate([product(0)[:64], product(1)[64:]], axis=0)

    def unit(p, n):
        col, count, half = SENDS[p][n]
        fetch(p, n, 2)
        for k in range(3):
            fetched[p, n, k].wait()
        b, e = ((2, 1), (1, 3))[half]
        for k, rng in enumerate(RANGES[half]):
            row, size, _ = rng
            if col <= row < col + count:
                at, lane = ROOM[half][k]
                src = room(at, size, lane * BLK, BLK)
                for piece_row in range(0, size, 256):
                    rows = min(256, size - piece_row)
                    part = (row + piece_row, rows, rng[2])
                    room(at + piece_row, rows, lane * BLK, BLK)[...] = term(part, b, e).astype(BF)
                dst = into.at[pl.ds(row, size), :]
                send(src, dst, t_s.at[half, k], t_r.at[half, k], near_y[1 - half])

    outs = (gate_out, up_out, down_out)

    def emit(rng, value, add):
        row, size, _ = rng
        items = []
        if row == TAIL:
            items = [(which, 32 * which, REM, MAIN) for which in range(3)]
        else:
            for (first, _), parts in zip(PIECES, LAYOUT):
                for which, at, count, col in parts:
                    if row <= col < row + size:
                        items.append((which, col - row, count, first + at))
        for which, at, count, to in items:
            rest = value[at:at + count]
            if add:
                rest = rest + outs[which][to:to + count, :].astype(F32)
            outs[which][to:to + count, :] = rest.astype(BF)

    def own_terms(half, first, last):
        for row, size, a in RANGES[half][first:last]:
            for piece_row in range(0, size, 256):
                part = (row + piece_row, min(256, size - piece_row), a)
                emit(part, term(part, 0, 2 * half), False)

    unit(0, 0)
    step = []
    for k in (0, 1):
        far[k].wait_recv()
        first = 2 * ROWS * (1 + k)
        for zz in (0, 1):
            rows = pl.ds(zz * ROWS, ROWS)
            src = rows_of(zz, x + (1 if k == 0 else -1))
            for n in range(4):
                cols = pl.ds(n * BLK, BLK)
                value = ng[0, src, share_cols(n)]
                if n // 2 == k:
                    value = (value.astype(F32) + xi[rows, cols].astype(F32)).astype(BF)
                room(first + zz * ROWS, ROWS, HALF + n * BLK, BLK)[...] = value
        step.append(
            send(room(first, 2 * ROWS), xr.at[k], p_s.at[3 + k], p_r.at[3 + k], xs_dev[k])
        )
    unit(2, 0)
    unit(1, 1)
    unit(1, 0)
    for k in (0, 1):
        step[k].wait_recv()

    def summed(zz, n):
        rows = pl.ds(pl.multiple_of(zz * ROWS, 16), ROWS)
        cols = pl.ds(n * BLK, BLK)
        value = ng[0, rows_of(zz, x), share_cols(n)].astype(F32)
        return value + xr[0, rows, cols].astype(F32) + xr[1, rows, cols].astype(F32)

    for n in range(4):
        room(6 * ROWS, ROWS, HALF + n * BLK, BLK)[...] = summed(1 - zl, n).astype(BF)
    over = send(room(6 * ROWS, ROWS), zr, p_s.at[5], p_r.at[5], zpair)
    unit(3, 0)
    over.wait_recv()
    for n in range(4):
        cols = pl.ds(n * BLK, BLK)
        fin[:, cols] = summed(zl, n) + zr[:, cols].astype(F32)
    dn[:, mine] = fin[pl.ds(pl.multiple_of(c * 24, 8), 24), :]
    last = send(
        fin.at[pl.ds(pl.multiple_of((1 - c) * 24, 8), 24), :], dn.at[:, mine],
        p_s.at[6], p_r.at[6], core,
    )
    own_terms(0, 0, 2)
    last.wait_recv()

    inputs = li_ref[...].astype(F32)
    rms = jnp.sqrt(jnp.mean(inputs * inputs, axis=1, keepdims=True) + 1e-06)
    unit_rows = inputs / rms
    scaled = gain_ref[...] * dn[...]
    inner = jnp.mean(scaled * unit_rows, axis=1, keepdims=True)
    ig_out[...] = ((scaled - unit_rows * inner) / rms).astype(BF)
    total = jnp.sum(dn[...] * unit_rows, axis=0, keepdims=True)
    between = ((0, 2, 3), (0, 3, 4), (1, 0, 2), (1, 2, 4))
    for n, peers in enumerate(([core], xs_dev, zs_dev, ys_dev)):
        gs[n] = total
        cps = [send(gs.at[n], gr.at[n, k], g_sem.at[n, k], g_rec.at[n, k], to) for k, to in enumerate(peers)]
        own_terms(*between[n])
        for k, cp in enumerate(cps):
            cp.wait_recv()
            total = total + gr[n, k]
    gain_out[...] = total
    own_terms(1, 4, 6)

    for half, k in ((0, 0), (0, 1), (1, 1), (1, 2), (1, 0), (0, 2), (0, 3), (1, 3), (1, 4), (1, 5)):
        row, size, a = RANGES[half][k]
        ref = into.at[pl.ds(row, size), :]
        remote(ref, ref, t_s.at[half, k], t_r.at[half, k], core).wait_recv()
        for piece_row in range(row, row + size, 256):
            part = (piece_row, min(256, row + size - piece_row), a)
            emit(part, into[piece_row:piece_row + part[1], :].astype(F32), True)
    for cp in swaps + sent:
        cp.wait_send()


def move_kernel(*refs):
    n = len(refs) // 2
    cps = [
        pltpu.make_async_copy(refs[k], refs[n + k], refs[-1].at[k]) for k in range(n)
    ]
    for cp in cps:
        cp.start()
    for cp in cps:
        cp.wait()


def move_out(*arrays):
    hbm = pl.BlockSpec(memory_space=pl.ANY)
    return pl.pallas_call(
        move_kernel,
        out_shape=[jax.ShapeDtypeStruct(a.shape, a.dtype) for a in arrays],
        in_specs=[pl.BlockSpec(memory_space=pltpu.VMEM)] * len(arrays),
        out_specs=[hbm] * len(arrays),
        scratch_shapes=[pltpu.SemaphoreType.DMA((len(arrays),))],
    )(*arrays)


def backward(layer_input, grad_out, gain, w_gate, w_up, w_down):
    vmem = pl.BlockSpec(memory_space=pltpu.VMEM)
    hbm = pl.BlockSpec(memory_space=pl.ANY)
    dma = pltpu.SemaphoreType.DMA
    v = pltpu.VMEM
    return pl.pallas_call(
        kernel,
        out_shape=[
            jax.ShapeDtypeStruct((CORE_FF, BLK), BF),
            jax.ShapeDtypeStruct((CORE_FF, BLK), BF),
            jax.ShapeDtypeStruct((CORE_FF, BLK), BF),
            jax.ShapeDtypeStruct((24, D), BF),
            jax.ShapeDtypeStruct((1, D), F32),
            jax.ShapeDtypeStruct((PLANE, XW), BF),
        ],
        in_specs=[vmem] * 3 + [hbm] * 3,
        out_specs=[vmem] * 5 + [hbm],
        scratch_shapes=[
            v((2, PLANE, D), BF),
            v((PLANE, XW), BF),
            v((2, 4, PLANE, BLK), BF),
            v((GROUP, CORE_FF), BF),
            v((GROUP, CORE_FF), BF),
            v((CORE_FF, D), BF),
            v((CORE_FF, D), BF),
            v((CORE_FF, D), BF),
            v((2, 24, D), BF),
            v((4, ROWS, 2 * BLK), BF),
            v((XW, BLK), BF),
            v((GROUP, HALF), BF),
            v((2 * ROWS, HALF), BF),
            v((2, 2 * ROWS, HALF), BF),
            v((ROWS, HALF), BF),
            v((ROWS, HALF), F32),
            v((24, D), F32),
            v((4, 1, D), F32),
            v((4, 3, 1, D), F32),
            dma((3,)),
            dma((1,)),
            dma((2,)),
            dma((2,)),
            dma((2, 20)),
            dma((2, 16, 2)),
            dma((2, 16)),
            dma((2, 16)),
            dma((3, 5)),
            dma((3, 5)),
            dma((40,)),
            dma((40,)),
            dma((5, 3)),
            dma((2, 6)),
            dma((2, 6)),
            dma((11,)),
            dma((11,)),
            dma((4, 3)),
            dma((4, 3)),
        ],
        compiler_params=pltpu.CompilerParams(
            collective_id=0, has_side_effects=True, vmem_limit_bytes=63 << 20
        ),
    )(layer_input, grad_out, gain, w_gate, w_up, w_down)


def body(layer_input, gain_vector, w_gate, w_up, w_down, grad_out):
    gain = gain_vector[None, :]
    results = backward(layer_input, grad_out, gain, w_gate.T, w_up.T, w_down)
    gate, up, down, input_gradient, gain_gradient = move_out(*results[:5])
    return input_gradient, gain_gradient[0], gate.T, up.T, down


def solution(mesh):
    return jax.shard_map(
        body,
        mesh=mesh,
        in_specs=(
            P(("dp", "tensor"), None),
            P(),
            P(None, "tensor"),
            P(None, "tensor"),
            P("tensor", None),
            P(("dp", "tensor"), None),
        ),
        out_specs=(
            P(("dp", "tensor"), None),
            P(),
            P("dp", "tensor"),
            P("dp", "tensor"),
            P("tensor", "dp"),
        ),
        check_vma=False,
    )
```

```python
import functools

import jax
import jax.numpy as jnp
from jax import lax
from jax.experimental import pallas as pl
from jax.experimental.pallas import tpu as pltpu
from jax.sharding import PartitionSpec as P

MESH = pl.DeviceIdType.MESH
BF = jnp.bfloat16
F32 = jnp.float32
D = 4096
HALF = 2048
QUART = 1024
ROWS = 48
PLANE = 768
GROUP = 384
BLK = 512
CORE_FF = 924
MAIN = 896
REM = CORE_FF - MAIN
PIECES = ((0, 256), (256, 256), (512, 256), (768, 156))
LAYOUT = (
    ((0, 0, 256, 0), (1, 0, 256, 256), (2, 0, 256, 512)),
    ((0, 0, 256, 768), (1, 0, 256, 1024), (2, 0, 128, 1280), (2, 128, 128, 1408)),
    ((0, 0, 256, 1536), (1, 0, 256, 1792), (2, 0, 256, 2048)),
    ((0, 0, 128, 2304), (1, 0, 128, 2432), (2, 0, 128, 2560)),
)
TAIL = 2688
XW = TAIL + 128
HALF_X = XW // 2
SENDS = (((0, 768, 0),), ((768, 640, 0), (1408, 128, 1)), ((1536, 768, 1),), ((2304, 512, 1),))
ROOM = (
    ((0, 0), (512, 0), (0, 1), (512, 1)),
    ((640, 1), (0, 2), (512, 2), (0, 3), (256, 3), (384, 3)),
)
RANGES = (
    ((0, 512, 0), (512, 256, 1), (768, 512, 0), (1280, 128, 1)),
    ((1408, 128, 1), (1536, 512, 0), (2048, 256, 1), (2304, 256, 0), (2560, 128, 1), (TAIL, 128, 2)),
)


def coords():
    dp = lax.axis_index("dp")
    t = lax.axis_index("tensor")
    y = dp // 2
    z = (dp % 2) * 2 + (t // 2) % 2
    return t // 4, y, z, t % 2


def device(x, y, z, c):
    x, y, z, c = (x + 4) % 4, (y + 4) % 4, (z + 4) % 4, (c + 2) % 2
    return (y * 2 + z // 2, x * 4 + (z % 2) * 2 + c)


def remote(src, dst, ss, rs, to):
    return pltpu.make_async_remote_copy(
        src_ref=src, dst_ref=dst, send_sem=ss, recv_sem=rs, device_id=to, device_id_type=MESH
    )


def greet(peers):
    barrier = pltpu.get_barrier_semaphore()
    for to in peers:
        pl.semaphore_signal(barrier, inc=1, device_id=to, device_id_type=MESH)
    pl.semaphore_wait(barrier, len(peers))


OFFS = (0, -1, 1, 2)


def slot(i, j):
    return (i % 4) * 4 + (j % 4)


def contract_cols(left, right):
    return lax.dot_general(left, right, (((1,), (1,)), ((), ())), preferred_element_type=F32)


def contract_rows(left, right):
    return lax.dot_general(left, right, (((0,), (0,)), ((), ())), preferred_element_type=F32)


def kernel(
    li_ref, go_ref, gain_ref, wg_hbm, wu_hbm, wd_hbm,
    gate_out, up_out, down_out, ig_out, gain_out, r_hbm,
    ng, x_ref, e_ref, dg_ref, du_ref, wg, wu, wd, other, stage,
    into, pc, xi, xr, zr, fin, dn, gs, gr,
    w_sem, out_sem, ex_s, ex_r, s_sem, r_sem, c_s, c_r, y_s, y_r, e_s, e_r,
    load, t_s, t_r, p_s, p_r, g_sem, g_rec,
):
    x, y, z, c = coords()
    s = 1 - 2 * (z % 2)
    sy = 1 - 2 * (y % 2)
    zl, zh = z % 2, z // 2
    core = device(x, y, z, 1 - c)
    xs_dev = [device(x + k, y, z, c) for k in (1, -1, 2)]
    ys_dev = [device(x, y + sy * k, z, c) for k in (1, -1, 2)]
    zs_dev = [device(x, y, z + s * k, c) for k in (1, -1, 2)]
    step = {"x": xs_dev[:2], "z": zs_dev[:2]}
    near_y = ys_dev[:2]
    zpair = zs_dev[0]
    weights = [
        pltpu.make_async_copy(src, dst, w_sem.at[k])
        for k, (src, dst) in enumerate(((wg_hbm, wg), (wu_hbm, wu), (wd_hbm, wd)))
    ]
    greet([core, *xs_dev, *ys_dev, *zs_dev])
    swaps = []
    for a, ref in enumerate((li_ref, go_ref)):
        cp = remote(ref, other.at[a], ex_s.at[a], ex_r.at[a], core)
        cp.start()
        swaps.append(cp)
    for cp in weights:
        cp.start()

    base = pl.multiple_of((z * 4 + x) * ROWS, 16)
    first = c == 0
    n_ref, g_ref = ng.at[0], ng.at[1]
    outs = (n_ref, g_ref)

    swaps[0].wait_recv()
    scale = []
    for ref in (li_ref, other.at[0]):
        rows = ref[...].astype(F32)
        scale.append(jnp.sqrt(jnp.mean(rows * rows, axis=1, keepdims=True) + 1e-06))
    swaps[1].wait_recv()
    for k in range(8):
        cols = pl.ds(k * 512, 512)
        mine = (li_ref[:, cols].astype(F32) / scale[0]) * gain_ref[:, cols]
        theirs = (other[0, :, cols].astype(F32) / scale[1]) * gain_ref[:, cols]
        both = jnp.concatenate(
            [jnp.where(first, mine, theirs), jnp.where(first, theirs, mine)], axis=0
        )
        n_ref[pl.ds(base, ROWS), cols] = both.astype(BF)
        mine = go_ref[:, cols].astype(F32)
        theirs = other[1, :, cols].astype(F32)
        both = jnp.concatenate(
            [jnp.where(first, mine, theirs), jnp.where(first, theirs, mine)], axis=0
        )
        g_ref[pl.ds(base, ROWS), cols] = both.astype(BF)

    lo = pl.multiple_of(c * HALF, 128)
    wide = (pl.ds(lo, HALF), pl.ds(lo, QUART), pl.ds(pl.multiple_of(lo + QUART, 128), QUART))
    theirs = pl.ds(pl.multiple_of((1 - c) * HALF, 128), HALF)

    def place(a, i, j):
        dz, dx = (j, i) if a == 0 else (i, j)
        zz, xx = (z + s * dz + 4) % 4, (x + dx + 4) % 4
        return pl.ds(pl.multiple_of((zz * 4 + xx) * ROWS, 16), ROWS)

    def block(a, i, j, part=0):
        return outs[a].at[place(a, i, j), wide[part]]

    sent, sent_ng = [], []
    count = [0, 0]

    def push(a, leg, way, i, j, part=0):
        axis = ("x", "z")[(a + leg) % 2]
        to = step[axis][0 if way > 0 else 1]
        at = (i, j)[leg]
        at = at - way if axis == "x" else way - at
        ri, rj = (at, j) if leg == 0 else (i, at)
        ref = block(a, i, j, part)
        k = 1 if part == 2 else 0
        cp = remote(ref, ref, s_sem.at[a, count[a]], r_sem.at[a, slot(ri, rj), k], to)
        count[a] += 1
        cp.start()
        sent_ng.append(cp)

    def arrive(a, i, j):
        for part in (1, 2) if (i, j) == (2, 0) or j == 2 else (0,):
            ref = block(a, i, j, part)
            k = 1 if part == 2 else 0
            remote(ref, ref, s_sem.at[a, 0], r_sem.at[a, slot(i, j), k], core).wait_recv()
        if j == 0:
            if i in (1, -1):
                push(a, 0, -i, i, 0, 1 if i < 0 else 2)
            push(a, 1, 1, i, 0)
            push(a, 1, -1, i, 0)
        elif j in (1, -1):
            push(a, 1, -j, i, j, 1 if j < 0 else 2)
        ref = block(a, i, j)
        k = slot(i, j)
        cp = remote(ref, ref, c_s.at[a, k], c_r.at[a, k], core)
        cp.start()
        sent_ng.append(cp)

    for a in (0, 1):
        for way in (1, -1):
            push(a, 0, way, 0, 0)
            push(a, 1, way, 0, 0)

    def hop(src, dst, k, to, kept=sent):
        cp = remote(src, dst, e_s.at[k], e_r.at[k], to)
        cp.start()
        kept.append(cp)

    def landed(ref, k):
        remote(ref, ref, e_s.at[k], e_r.at[k], core).wait_recv()

    for q, to in enumerate(near_y):
        for k, yy in enumerate((y + (sy if q == 0 else -sy), y + 2)):
            cols = pl.ds(pl.multiple_of(((yy + 4) % 4) * 2 * BLK, 128), 2 * BLK)
            at = 2 + q if k == 0 else q
            hop(ng.at[c, pl.ds(base, ROWS), cols], stage.at[at], at, to, sent_ng)

    tally = [0]

    def store(src, dst):
        cp = pltpu.make_async_copy(src, dst, out_sem.at[tally[0]])
        tally[0] += 1
        cp.start()
        return cp

    def set_cols(which):
        return pl.ds(pl.multiple_of(which * BLK, 128), BLK)

    def place_e(zz, xx):
        return pl.ds(pl.multiple_of((((zz + 4) % 4) * 4 + (xx + 4) % 4) * ROWS, 16), ROWS)

    def set_of(n):
        return pl.ds(2 * n, 2)

    def extra_z():
        for k in range(4):
            landed(stage.at[k], k)
        local = store(stage.at[:, :, set_cols(zh)], e_ref.at[c, :, place_e(z, x), :])
        for n in (0, 1):
            mine = e_ref.at[c, set_of(n), place_e(z, x), :]
            hop(stage.at[set_of(n), :, set_cols(zh)], mine, 4 + 40 * n, zs_dev[0])
            hop(stage.at[set_of(n), :, set_cols(1 - zh)], mine, 5 + 40 * n, zs_dev[1])
            hop(stage.at[set_of(n), :, set_cols(1 - zh)], mine, 6 + 40 * n, zs_dev[2])
        return local

    def extra_x(n):
        if n == 0:
            local.wait()
        for k, dz in ((4, 1), (5, -1), (6, 2)):
            landed(e_ref.at[c, set_of(n), place_e(z + s * dz, x), :], k + 40 * n)
        for zz in range(4):
            mine = e_ref.at[c, set_of(n), place_e(zz, x), :]
            hop(mine, mine, 8 + 40 * n + zz, xs_dev[0])
            hop(mine, mine, 12 + 40 * n + zz, xs_dev[1])
            hop(mine, mine, 16 + 40 * n + zz, core)

    def extra_share(n, dx):
        k = (8 if dx < 0 else 12) + 40 * n
        for zz in range(4):
            rows = place_e(zz, x + dx)
            ref = e_ref.at[c, set_of(n), rows, :]
            landed(ref, k + zz)
            half = e_ref.at[c, pl.ds(2 * n + (0 if dx < 0 else 1), 1), rows, :]
            hop(half, half, (20 if dx < 0 else 24) + 40 * n + zz, xs_dev[0 if dx < 0 else 1])
            hop(ref, ref, (28 if dx < 0 else 32) + 40 * n + zz, core)

    def extra_last(n):
        for zz in range(4):
            rows = place_e(zz, x + 2)
            landed(e_ref.at[c, pl.ds(2 * n, 1), rows, :], 20 + 40 * n + zz)
            landed(e_ref.at[c, pl.ds(2 * n + 1, 1), rows, :], 24 + 40 * n + zz)
            ref = e_ref.at[c, set_of(n), rows, :]
            hop(ref, ref, 36 + 40 * n + zz, core)

    def extra_done(n):
        for k, dx in ((16, 0), (28, -1), (32, 1), (36, 2)):
            for zz in range(4):
                rows = place_e(zz, x + dx)
                landed(e_ref.at[1 - c, set_of(n), rows, :], k + 40 * n + zz)

    sizes = (192, 192, GROUP)

    def chunk_rows(k):
        first = (z * 192, (z + s) * 192, (1 - zh) * GROUP)[k]
        return pl.ds(pl.multiple_of(first, 16), sizes[k])

    def chunk_ready(k):
        for dz in ((0,), (1,), (-1, 2))[k]:
            for a in (0, 1):
                for dx in OFFS:
                    i, j = (dx, dz) if a == 0 else (dz, dx)
                    if (i, j) != (0, 0):
                        ref = outs[a].at[place(a, i, j), theirs]
                        at = slot(i, j)
                        remote(ref, ref, c_s.at[a, at], c_r.at[a, at], core).wait_recv()

    def piece(k, p):
        f, w = PIECES[p]
        rows = chunk_rows(k)
        normed = n_ref[rows, :]
        gate = contract_cols(normed, wg[f:f + w, :])
        up = contract_cols(normed, wu[f:f + w, :])
        d_hidden = contract_cols(g_ref[rows, :], wd[f:f + w, :])
        sigma = jax.nn.sigmoid(gate)
        silu = gate * sigma
        hidden = (silu * up).astype(BF)
        d_gate = (d_hidden * up * sigma * (1.0 + gate * (1.0 - sigma))).astype(BF)
        d_up = (d_hidden * silu).astype(BF)
        if k < 2:
            own = pl.ds(pl.multiple_of((z % 2 if k == 0 else 1 - z % 2) * 192, 16), 192)
            dg_ref[own, f:f + w] = d_gate
            du_ref[own, f:f + w] = d_up
        values = (d_gate, d_up, hidden)
        for q, first, count, col in LAYOUT[p]:
            x_ref[rows, col:col + count] = values[q][:, first:first + count]
        if w < 256:
            gap = jnp.zeros((sizes[k], 32 - REM), BF)
            rest = []
            for value in values:
                rest += [value[:, w - REM:], gap]
            rest.append(jnp.zeros((sizes[k], 32), BF))
            x_ref[rows, TAIL:] = jnp.concatenate(rest, axis=1)
        for n, (col, count, to) in enumerate(SENDS[p]):
            view = (rows, pl.ds(col, count))
            at = p + 3 * n
            cp = remote(x_ref.at[view], r_hbm.at[view], y_s.at[k, at], y_r.at[k, at], near_y[to])
            cp.start()
            sent.append(cp)

    def moves(*items):
        for item in items:
            arrive(*item)

    moves((0, -1, 0), (1, 0, -1), (0, 1, 0), (1, 0, 1))
    moves((1, 1, 0), (0, 0, 1), (1, -1, 0), (0, 0, -1))
    moves((0, 2, 0), (1, 0, 2))
    for cp in weights:
        cp.wait()
    chunk_ready(0)
    piece(0, 0)
    moves((0, -1, 1), (1, 1, -1), (0, 1, 1), (1, 1, 1))
    piece(0, 2)
    moves((0, -1, -1), (1, -1, -1), (0, 1, -1), (1, -1, 1))
    piece(0, 1)
    moves((0, 2, 1), (1, 1, 2))
    local = extra_z()
    piece(0, 3)
    moves((1, 2, 0), (0, 0, 2), (1, -1, 2), (0, 2, -1))
    chunk_ready(1)
    piece(1, 0)
    moves((0, -1, 2), (0, 1, 2), (1, 2, -1), (1, 2, 1))
    extra_x(0)
    piece(1, 2)
    piece(1, 1)
    moves((0, 2, 2), (1, 2, 2))
    piece(1, 3)
    chunk_ready(2)
    piece(2, 0)
    piece(2, 2)
    extra_share(0, -1)
    extra_share(0, 1)
    extra_x(1)
    piece(2, 1)
    piece(2, 3)

    def share_cols(k):
        return pl.ds(pl.multiple_of((2 * k + 1 - zh) * BLK, 128), BLK)

    def share(which):
        for k in range(4):
            lo = (c if which == 0 else 1 - c) * HALF + k * BLK
            cols = pl.ds(pl.multiple_of(lo, 128), BLK)
            value = jnp.dot(dg_ref[...], wg[:, cols], preferred_element_type=F32)
            value = value + jnp.dot(du_ref[...], wu[:, cols], preferred_element_type=F32)
            ng[which, 0:GROUP, share_cols(k)] = value.astype(BF)

    def send(src, dst, ss, rs, to):
        cp = remote(src, dst, ss, rs, to)
        cp.start()
        sent.append(cp)
        return cp

    for cp in sent_ng:
        cp.wait_send()
    fetched = {}

    def fetch(p, n, k):
        col, count, _ = SENDS[p][n]
        rows, cols, at = chunk_rows(k), pl.ds(col, count), p + 3 * n
        ref = r_hbm.at[rows, cols]
        remote(ref, ref, y_s.at[k, at], y_r.at[k, at], core).wait_recv()
        cp = pltpu.make_async_copy(ref, wd.at[rows, cols], load.at[at, k])
        cp.start()
        fetched[p, n, k] = cp

    share(1)
    swap = [
        send(
            ng.at[1, pl.ds(0, GROUP), share_cols(k)], pc.at[:, pl.ds(k * BLK, BLK)],
            p_s.at[7 + k], p_r.at[7 + k], core,
        )
        for k in range(4)
    ]
    extra_last(0)
    share(0)
    extra_share(1, -1)
    extra_share(1, 1)

    mine = pl.ds(pl.multiple_of(c * HALF, 128), HALF)
    for k in range(4):
        swap[k].wait_recv()
        value = ng[0, 0:GROUP, share_cols(k)].astype(F32)
        value = value + pc[:, k * BLK:(k + 1) * BLK].astype(F32)
        ng[0, 0:GROUP, share_cols(k)] = value.astype(BF)

    def rows_of(zz, xx):
        return pl.ds(pl.multiple_of((zz * 4 + (xx + 4) % 4) * ROWS, 16), ROWS)

    def room(row, rows, col=HALF, cols=HALF):
        return wg.at[pl.ds(row, rows), pl.ds(col, cols)]

    for zz in (0, 1):
        for k in range(4):
            value = ng[0, rows_of(zz, x + 2), share_cols(k)]
            room(zz * ROWS, ROWS, HALF + k * BLK, BLK)[...] = value
    far = [
        send(
            room(0, 2 * ROWS, HALF + k * QUART, QUART), xi.at[:, pl.ds(k * QUART, QUART)],
            p_s.at[1 + k], p_r.at[1 + k], xs_dev[k],
        )
        for k in (0, 1)
    ]

    for p, n in ((0, 0), (2, 0), (1, 0), (1, 1), (3, 0)):
        fetch(p, n, 0)
        fetch(p, n, 1)
    extra_done(0)

    def block_cols(b):
        yy = (y + (0, sy, -sy)[b] + 4) % 4
        return pl.ds(pl.multiple_of((yy * 2 + zh) * BLK, 128), BLK)

    def term(rng, b, e):
        row, size, a = rng

        def product(a):
            cols = slice(row, row + size)
            value = contract_rows(x_ref[:, cols], ng[a, :, block_cols(b)])
            return value + contract_rows(wd[0:PLANE, cols], e_ref[a, e])

        if a < 2:
            return product(a)
        return jnp.concatenate([product(0)[:64], product(1)[64:]], axis=0)

    def unit(p, n):
        col, count, half = SENDS[p][n]
        fetch(p, n, 2)
        for k in range(3):
            fetched[p, n, k].wait()
        b, e = ((2, 0), (1, 1))[half]
        for k, rng in enumerate(RANGES[half]):
            row, size, _ = rng
            if col <= row < col + count:
                at, lane = ROOM[half][k]
                src = room(at, size, lane * BLK, BLK)
                for piece_row in range(0, size, 256):
                    rows = min(256, size - piece_row)
                    part = (row + piece_row, rows, rng[2])
                    room(at + piece_row, rows, lane * BLK, BLK)[...] = term(part, b, e).astype(BF)
                dst = into.at[pl.ds(row, size), :]
                send(src, dst, t_s.at[half, k], t_r.at[half, k], near_y[1 - half])

    outs = (gate_out, up_out, down_out)

    def emit(rng, value, add):
        row, size, _ = rng
        items = []
        if row == TAIL:
            items = [(which, 32 * which, REM, MAIN) for which in range(3)]
        else:
            for (first, _), parts in zip(PIECES, LAYOUT):
                for which, at, count, col in parts:
                    if row <= col < row + size:
                        items.append((which, col - row, count, first + at))
        for which, at, count, to in items:
            rest = value[at:at + count]
            if add:
                rest = rest + outs[which][to:to + count, :].astype(F32)
            outs[which][to:to + count, :] = rest.astype(BF)

    def own_terms(half, first, last):
        for row, size, a in RANGES[half][first:last]:
            for piece_row in range(0, size, 256):
                part = (row + piece_row, min(256, size - piece_row), a)
                emit(part, term(part, 0, 2 + half), False)

    unit(0, 0)
    step = []
    for k in (0, 1):
        far[k].wait_recv()
        first = 2 * ROWS * (1 + k)
        for zz in (0, 1):
            rows = pl.ds(zz * ROWS, ROWS)
            src = rows_of(zz, x + (1 if k == 0 else -1))
            for n in range(4):
                cols = pl.ds(n * BLK, BLK)
                value = ng[0, src, share_cols(n)]
                if n // 2 == k:
                    value = (value.astype(F32) + xi[rows, cols].astype(F32)).astype(BF)
                room(first + zz * ROWS, ROWS, HALF + n * BLK, BLK)[...] = value
        step.append(
            send(room(first, 2 * ROWS), xr.at[k], p_s.at[3 + k], p_r.at[3 + k], xs_dev[k])
        )
    unit(2, 0)
    unit(1, 1)
    unit(1, 0)
    extra_last(1)
    for k in (0, 1):
        step[k].wait_recv()

    def summed(zz, n):
        rows = pl.ds(pl.multiple_of(zz * ROWS, 16), ROWS)
        cols = pl.ds(n * BLK, BLK)
        value = ng[0, rows_of(zz, x), share_cols(n)].astype(F32)
        return value + xr[0, rows, cols].astype(F32) + xr[1, rows, cols].astype(F32)

    for n in range(4):
        room(6 * ROWS, ROWS, HALF + n * BLK, BLK)[...] = summed(1 - zl, n).astype(BF)
    over = send(room(6 * ROWS, ROWS), zr, p_s.at[5], p_r.at[5], zpair)
    unit(3, 0)
    over.wait_recv()
    for n in range(4):
        cols = pl.ds(n * BLK, BLK)
        fin[:, cols] = summed(zl, n) + zr[:, cols].astype(F32)
    dn[:, mine] = fin[pl.ds(pl.multiple_of(c * 24, 8), 24), :]
    last = send(
        fin.at[pl.ds(pl.multiple_of((1 - c) * 24, 8), 24), :], dn.at[:, mine],
        p_s.at[6], p_r.at[6], core,
    )
    extra_done(1)
    own_terms(0, 0, 2)
    last.wait_recv()

    inputs = li_ref[...].astype(F32)
    rms = jnp.sqrt(jnp.mean(inputs * inputs, axis=1, keepdims=True) + 1e-06)
    unit_rows = inputs / rms
    scaled = gain_ref[...] * dn[...]
    inner = jnp.mean(scaled * unit_rows, axis=1, keepdims=True)
    ig_out[...] = ((scaled - unit_rows * inner) / rms).astype(BF)
    total = jnp.sum(dn[...] * unit_rows, axis=0, keepdims=True)
    between = ((0, 2, 3), (0, 3, 4), (1, 0, 2), (1, 2, 4))
    for n, peers in enumerate(([core], xs_dev, zs_dev, ys_dev)):
        gs[n] = total
        cps = [send(gs.at[n], gr.at[n, k], g_sem.at[n, k], g_rec.at[n, k], to) for k, to in enumerate(peers)]
        own_terms(*between[n])
        for k, cp in enumerate(cps):
            cp.wait_recv()
            total = total + gr[n, k]
    gain_out[...] = total
    own_terms(1, 4, 6)

    for half, k in ((0, 0), (0, 1), (1, 1), (1, 2), (1, 0), (0, 2), (0, 3), (1, 3), (1, 4), (1, 5)):
        row, size, a = RANGES[half][k]
        ref = into.at[pl.ds(row, size), :]
        remote(ref, ref, t_s.at[half, k], t_r.at[half, k], core).wait_recv()
        for piece_row in range(row, row + size, 256):
            part = (piece_row, min(256, row + size - piece_row), a)
            emit(part, into[piece_row:piece_row + part[1], :].astype(F32), True)
    for cp in swaps + sent:
        cp.wait_send()


def move_kernel(*refs):
    n = len(refs) // 2
    cps = [
        pltpu.make_async_copy(refs[k], refs[n + k], refs[-1].at[k]) for k in range(n)
    ]
    for cp in cps:
        cp.start()
    for cp in cps:
        cp.wait()


def move_out(*arrays):
    hbm = pl.BlockSpec(memory_space=pl.ANY)
    return pl.pallas_call(
        move_kernel,
        out_shape=[jax.ShapeDtypeStruct(a.shape, a.dtype) for a in arrays],
        in_specs=[pl.BlockSpec(memory_space=pltpu.VMEM)] * len(arrays),
        out_specs=[hbm] * len(arrays),
        scratch_shapes=[pltpu.SemaphoreType.DMA((len(arrays),))],
    )(*arrays)


def backward(layer_input, grad_out, gain, w_gate, w_up, w_down):
    vmem = pl.BlockSpec(memory_space=pltpu.VMEM)
    hbm = pl.BlockSpec(memory_space=pl.ANY)
    dma = pltpu.SemaphoreType.DMA
    v = pltpu.VMEM
    return pl.pallas_call(
        kernel,
        out_shape=[
            jax.ShapeDtypeStruct((CORE_FF, BLK), BF),
            jax.ShapeDtypeStruct((CORE_FF, BLK), BF),
            jax.ShapeDtypeStruct((CORE_FF, BLK), BF),
            jax.ShapeDtypeStruct((24, D), BF),
            jax.ShapeDtypeStruct((1, D), F32),
            jax.ShapeDtypeStruct((PLANE, XW), BF),
        ],
        in_specs=[vmem] * 3 + [hbm] * 3,
        out_specs=[vmem] * 5 + [hbm],
        scratch_shapes=[
            v((2, PLANE, D), BF),
            v((PLANE, XW), BF),
            v((2, 4, PLANE, BLK), BF),
            v((GROUP, CORE_FF), BF),
            v((GROUP, CORE_FF), BF),
            v((CORE_FF, D), BF),
            v((CORE_FF, D), BF),
            v((CORE_FF, D), BF),
            v((2, 24, D), BF),
            v((4, ROWS, 2 * BLK), BF),
            v((XW, BLK), BF),
            v((GROUP, HALF), BF),
            v((2 * ROWS, HALF), BF),
            v((2, 2 * ROWS, HALF), BF),
            v((ROWS, HALF), BF),
            v((ROWS, HALF), F32),
            v((24, D), F32),
            v((4, 1, D), F32),
            v((4, 3, 1, D), F32),
            dma((3,)),
            dma((1,)),
            dma((2,)),
            dma((2,)),
            dma((2, 20)),
            dma((2, 16, 2)),
            dma((2, 16)),
            dma((2, 16)),
            dma((3, 5)),
            dma((3, 5)),
            dma((80,)),
            dma((80,)),
            dma((5, 3)),
            dma((2, 6)),
            dma((2, 6)),
            dma((11,)),
            dma((11,)),
            dma((4, 3)),
            dma((4, 3)),
        ],
        compiler_params=pltpu.CompilerParams(
            collective_id=0, has_side_effects=True, vmem_limit_bytes=63 << 20
        ),
    )(layer_input, grad_out, gain, w_gate, w_up, w_down)


def body(layer_input, gain_vector, w_gate, w_up, w_down, grad_out):
    gain = gain_vector[None, :]
    results = backward(layer_input, grad_out, gain, w_gate.T, w_up.T, w_down)
    gate, up, down, input_gradient, gain_gradient = move_out(*results[:5])
    return input_gradient, gain_gradient[0], gate.T, up.T, down


def solution(mesh):
    return jax.shard_map(
        body,
        mesh=mesh,
        in_specs=(
            P(("dp", "tensor"), None),
            P(),
            P(None, "tensor"),
            P(None, "tensor"),
            P("tensor", None),
            P(("dp", "tensor"), None),
        ),
        out_specs=(
            P(("dp", "tensor"), None),
            P(),
            P("dp", "tensor"),
            P("dp", "tensor"),
            P("tensor", "dp"),
        ),
        check_vma=False,
    )
```
